32 devices in a mesh: dp: 16 (over z, x, core), tensor: 2 (over y).
Axes of the slice: x: 2, y: 2, z: 4, core: 2. Of those that a mesh axis runs over, the one named last changes fastest.
Arguments:
- images_in: bfloat16 [8352, 768], P('dp')
- small_counts: int32 [16], P('dp'), may hold values from 0 to 1, as said below
- large_counts: int32 [16], P('dp'), may hold values from 0 to 1, as said below
- norm1_gain: float32 [768], replicated, may hold values from 0.25 to 1.75
- norm1_bias: float32 [768], replicated, may hold values from -4 to 4
- qkv_weight: bfloat16 [768, 3, 768], P(None, None, 'tensor'), may hold values from -0.3125 to 0.3125
- qv_bias: float32 [2, 768], P(None, 'tensor'), may hold values from -6 to 6
- out_weight: bfloat16 [768, 768], P('tensor'), may hold values from -0.875 to 0.875
- out_bias: float32 [768], replicated, may hold values from -4 to 4
- norm2_gain: float32 [768], replicated, may hold values from 0.25 to 1.75
- norm2_bias: float32 [768], replicated, may hold values from -4 to 4
- up_weight: bfloat16 [768, 3072], P(None, 'tensor'), may hold values from -0.21875 to 0.21875
- up_bias: float32 [3072], P('tensor'), may hold values from -6 to 6
- down_weight: bfloat16 [3072, 768], P('tensor'), may hold values from -0.15625 to 0.15625
- down_bias: float32 [768], replicated, may hold values from -4 to 4
- out_cotangent: bfloat16 [8352, 768], P('dp'), may hold values from -6 to 6
Outputs:
- block_out: bfloat16 [8352, 768], P('dp')
- input_grad: float32 [8352, 768], P('dp')
- norm1_gain_grad: float32 [768], replicated
- norm1_bias_grad: float32 [768], replicated
- qkv_weight_grad: float32 [768, 3, 768], P('dp', None, 'tensor')
- qv_bias_grad: float32 [2, 768], P(None, 'tensor')
- out_weight_grad: float32 [768, 768], P('tensor', 'dp')
- out_bias_grad: float32 [768], replicated
- norm2_gain_grad: float32 [768], replicated
- norm2_bias_grad: float32 [768], replicated
- up_weight_grad: float32 [768, 3072], P('dp', 'tensor')
- up_bias_grad: float32 [3072], P('tensor')
- down_weight_grad: float32 [3072, 768], P('tensor', 'dp')
- down_bias_grad: float32 [768], replicated
The draws below stay inside these ranges and needn't reach their ends.
Inputs may be any that keep to these rules, and one draw needn't show every extreme that they name: `small_counts`: the first 197 rows of each index's block hold its small images, slots below the count are used, some index uses all 1 and some uses none. `large_counts`: large image slots below the count are used, some index uses all 1 and some uses none.
All inputs are finite; a program needn't handle non-finite values.
Results may differ from the reference program's by a relative error of at most 0.012.
The reference program's roundings to bfloat16 on the way count: a program that leaves them out, or rounds other values in their place, can miss the bound.
Values sent between devices are 32-bit elements; how exact they have to be, the bound alone decides.
No kernel may reach another device: no remote copies, remote signals or barrier semaphores. Data moves between devices by JAX's collectives and lax.ppermute only.
A program may use at most 128 MiB of HBM per device.

```python
import jax
import jax.numpy as jnp
from jax import lax

D = 768
HEADS = 12
HEAD_DIM = 64
FF = 3072
HH = 768
SMALL_LEN = 197
LARGE_LEN = 325
SMALL_SLOTS = 1
LARGE_SLOTS = 1
TOK_DEV = 522
TOKENS = 8352


def draw_images_in(key, part):
    key_base, key_cols, key_rows = jax.random.split(key, 3)
    column_scale = jnp.exp(jax.random.uniform(key_cols, (1, D), jnp.float32, jnp.log(0.3), jnp.log(3.0)))
    row_scale = jnp.exp(jax.random.uniform(key_rows, (TOKENS, 1), jnp.float32, jnp.log(0.3), jnp.log(3.0)))
    values = jax.random.normal(key_base, (TOKENS, D), jnp.float32) * column_scale * row_scale
    return jnp.clip(values, -20.0, 20.0).astype(jnp.bfloat16)


def counts_for(key, least, most):
    groups = TOKENS // TOK_DEV
    key_vals, key_pick = jax.random.split(key)
    drawn = jax.random.randint(key_vals, (groups,), least, most + 1)
    picked = jax.random.randint(key_pick, (), 0, groups)
    places = jnp.arange(groups)
    drawn = jnp.where(places == picked, most, drawn)
    drawn = jnp.where(places == (picked + 1) % groups, least, drawn)
    return drawn.astype(jnp.int32)


def draw_small_counts(key, part):
    return counts_for(jax.random.fold_in(key, 11), 0, SMALL_SLOTS)


def draw_large_counts(key, part):
    return counts_for(jax.random.fold_in(key, 23), 0, LARGE_SLOTS)


def raised(values, own_key, source, target, shards_of, factor):
    owner, partner = [(jnp.arange(values.shape[position]) // (values.shape[position] // shards_of)).reshape([-1 if axis == position else 1 for axis in range(values.ndim)]) for position in (source, target)]
    chosen = jax.random.permutation(own_key, shards_of)[partner]
    strong = (owner == chosen) | (owner == (partner + shards_of // 2) % shards_of)
    return jnp.where(strong, factor * values, values)


def steps_of(rng, extent, cuts, low, largest):
    factor_of, own = 1.0, jax.random.fold_in(rng, 6)
    for axis_at, shards_of in cuts:
        heights = jnp.exp(jax.random.uniform(jax.random.fold_in(own, axis_at), (shards_of,), jnp.float32, low / len(cuts), largest / len(cuts)))
        factor_of = factor_of * jnp.repeat(heights, extent[axis_at] // shards_of).reshape([-1 if axis == axis_at else 1 for axis in range(len(extent))])
    return factor_of


def bell_draw(rng, shape, spread, limit, cuts=(), held_as=jnp.bfloat16):
    level = steps_of(rng, shape, cuts, -0.22, 0.18) if cuts else 1.0
    values = jax.random.normal(rng, shape, jnp.float32) * spread * level
    return jnp.minimum(jnp.maximum(values, -limit), limit).astype(held_as)


def heavy_noise(own_key, extent, width, most, pieces, heavy, dtype=jnp.bfloat16):
    values = width * jax.random.normal(own_key, extent, jnp.float32)
    if pieces:
        values = values * steps_of(own_key, extent, pieces, -0.22, 0.18)
    return jnp.clip(raised(values, jax.random.fold_in(own_key, 3), *heavy), -most, most).astype(dtype)


def setup_inputs(seed: int = 0) -> dict:
    streams_of = jax.random.split(jax.random.key(seed), 17)
    images_in = draw_images_in(jax.random.fold_in(streams_of[16], 71), 0)
    small_counts = draw_small_counts(jax.random.fold_in(streams_of[16], 71), 0)
    large_counts = draw_large_counts(jax.random.fold_in(streams_of[16], 71), 0)
    norm1_gain = jnp.clip(1.0 + 0.15 * jax.random.normal(streams_of[3], (D,), jnp.float32), 0.25, 1.75)
    norm1_bias = bell_draw(streams_of[4], (D,), 0.3, 4.0, (), jnp.float32)
    qkv_weight = bell_draw(streams_of[5], (D, 3, HH), (D // 2) ** -0.5, 0.3125, ((2, 2),))
    qv_bias = bell_draw(streams_of[6], (2, HH), 0.5, 6.0, ((1, 2),), jnp.float32)
    out_weight = bell_draw(streams_of[7], (HH, D), (HH // 16) ** -0.5, 0.875, ((0, 2),))
    out_bias = bell_draw(streams_of[8], (D,), 0.3, 4.0, (), jnp.float32)
    norm2_gain = jnp.clip(1.0 + 0.15 * jax.random.normal(streams_of[9], (D,), jnp.float32), 0.25, 1.75)
    norm2_bias = bell_draw(streams_of[10], (D,), 0.3, 4.0, (), jnp.float32)
    up_weight = bell_draw(streams_of[11], (D, FF), D ** -0.5, 0.21875, ((1, 2),))
    up_bias = bell_draw(streams_of[12], (FF,), 0.5, 6.0, ((0, 2),), jnp.float32)
    down_weight = bell_draw(streams_of[13], (FF, D), (FF // 2) ** -0.5, 0.15625, ((0, 2),))
    down_bias = bell_draw(streams_of[14], (D,), 0.3, 4.0, (), jnp.float32)
    out_cotangent = heavy_noise(streams_of[15], (TOKENS, D), 1.0, 6.0, ((0, 16),), (0, 1, 16, 2.0))
    return dict(images_in=images_in, small_counts=small_counts, large_counts=large_counts, norm1_gain=norm1_gain, norm1_bias=norm1_bias, qkv_weight=qkv_weight, qv_bias=qv_bias, out_weight=out_weight, out_bias=out_bias, norm2_gain=norm2_gain, norm2_bias=norm2_bias, up_weight=up_weight, up_bias=up_bias, down_weight=down_weight, down_bias=down_bias, out_cotangent=out_cotangent)


@jax.custom_vjp
def low(v):
    return lax.optimization_barrier(v.astype(jnp.bfloat16)).astype(jnp.float32)

@jax.custom_vjp
def low_back(v):
    return v

def low_keep(v):
    return (low(v), None)

def low_pass(kept, grad):
    return (grad,)

def back_keep(v):
    return (v, None)

def back_low(kept, grad):
    return (low(grad),)
low.defvjp(low_keep, low_pass)
low_back.defvjp(back_keep, back_low)
NORM_EPS = 1e-06

def layer_norm(values, gain, bias):
    row_mean = lax.optimization_barrier(jnp.mean(values, axis=-1, keepdims=True))
    centered = values - row_mean
    variance = lax.optimization_barrier(jnp.mean(centered * centered, axis=-1, keepdims=True))
    return centered * lax.rsqrt(variance + NORM_EPS) * gain + bias

def row_mask(small_count, large_count):
    small_live = (jnp.arange(SMALL_SLOTS) < small_count).astype(jnp.float32)
    large_live = (jnp.arange(LARGE_SLOTS) < large_count).astype(jnp.float32)
    small_rows = jnp.broadcast_to(small_live[:, None], (SMALL_SLOTS, SMALL_LEN)).reshape(-1)
    large_rows = jnp.broadcast_to(large_live[:, None], (LARGE_SLOTS, LARGE_LEN)).reshape(-1)
    return jnp.concatenate([small_rows, large_rows], axis=0)

def attend(queries, key_rows, value_rows):
    scaling = HEAD_DIM ** (-0.5)
    scores = jnp.einsum('blhe,bmhe->bhlm', queries, key_rows, precision=lax.Precision.HIGHEST) * scaling
    scores = low_back(scores)
    soft_low = low(jax.nn.softmax(scores, axis=-1))
    return jnp.einsum('bhlm,bmhe->blhe', soft_low, value_rows, precision=lax.Precision.HIGHEST)

def split_heads(rows, first_row, slots, length):
    piece = rows[first_row:first_row + slots * length]
    return piece.reshape(slots, length, HEADS, HEAD_DIM)

def block(inputs, live, params):
    gain_one, bias_one, qkv_w, qv_b, out_w, out_b, gain_two, bias_two, up_w, up_b, down_w, down_b = params
    high = lax.Precision.HIGHEST
    first_low = low(layer_norm(inputs, gain_one, bias_one))
    queries = low_back(low(jnp.dot(first_low, qkv_w[:, 0], precision=high) + qv_b[0]))
    key_rows = low_back(low(jnp.dot(first_low, qkv_w[:, 1], precision=high)))
    value_rows = low_back(low(jnp.dot(first_low, qkv_w[:, 2], precision=high) + qv_b[1]))
    split_at = SMALL_SLOTS * SMALL_LEN
    small_out = attend(split_heads(queries, 0, SMALL_SLOTS, SMALL_LEN), split_heads(key_rows, 0, SMALL_SLOTS, SMALL_LEN), split_heads(value_rows, 0, SMALL_SLOTS, SMALL_LEN))
    large_out = attend(split_heads(queries, split_at, LARGE_SLOTS, LARGE_LEN), split_heads(key_rows, split_at, LARGE_SLOTS, LARGE_LEN), split_heads(value_rows, split_at, LARGE_SLOTS, LARGE_LEN))
    mixed_heads = jnp.concatenate([small_out.reshape(-1, HH), large_out.reshape(-1, HH)], axis=0)
    mixed_heads = low_back(low(mixed_heads))
    attn_branch = low_back(jnp.dot(mixed_heads, out_w, precision=high) + out_b)
    hidden = inputs + live[:, None] * attn_branch
    second_low = low(layer_norm(hidden, gain_two, bias_two))
    pre_act = low_back(jnp.dot(second_low, up_w, precision=high) + up_b)
    act_low = low(jax.nn.gelu(pre_act, approximate=False))
    mlp_branch = low_back(jnp.dot(act_low, down_w, precision=high) + down_b)
    return hidden + live[:, None] * mlp_branch

def reference(images_in, small_counts, large_counts, norm1_gain, norm1_bias, qkv_weight, qv_bias, out_weight, out_bias, norm2_gain, norm2_bias, up_weight, up_bias, down_weight, down_bias, out_cotangent):
    groups = small_counts.shape[0]
    lives = jax.vmap(row_mask)(small_counts, large_counts)
    blocks = images_in.astype(jnp.float32).reshape(groups, -1, D)
    params = tuple((item.astype(jnp.float32) for item in (norm1_gain, norm1_bias, qkv_weight, qv_bias, out_weight, out_bias, norm2_gain, norm2_bias, up_weight, up_bias, down_weight, down_bias)))
    step_fn = jax.checkpoint(block)

    def forward(all_blocks, all_params):

        def scan_step(carry, item):
            return (carry, step_fn(item[0], item[1], all_params))
        unused, results = lax.scan(scan_step, jnp.zeros((), jnp.float32), (all_blocks, lives))
        return results
    results, pullback = jax.vjp(forward, blocks, params)
    cotangent = out_cotangent.astype(jnp.float32).reshape(groups, -1, D)
    grad_blocks, grad_params = pullback(cotangent)
    block_out = results.reshape(-1, D).astype(jnp.bfloat16)
    input_grad = grad_blocks.reshape(-1, D)
    return (block_out, input_grad, grad_params[0], grad_params[1], grad_params[2], grad_params[3], grad_params[4], grad_params[5], grad_params[6], grad_params[7], grad_params[8], grad_params[9], grad_params[10], grad_params[11])
```

```python
import functools

import jax
import jax.numpy as jnp
from jax import lax
from jax.experimental import pallas as pl
from jax.experimental.pallas import tpu as pltpu
from jax.sharding import PartitionSpec as P

HEAD_DIM = 64
PAIR = 2 * HEAD_DIM
LENGTHS = (197, 325)
PADDED = tuple(-(-length // 16) * 16 for length in LENGTHS)
NORM_EPS = 1e-06
F32 = jnp.float32
BF16 = jnp.bfloat16
VMEM_LIMIT = 56 * 1024 * 1024


def norm_parts(values):
    row_mean = jnp.mean(values, axis=-1, keepdims=True)
    centered = values - row_mean
    variance = jnp.mean(centered * centered, axis=-1, keepdims=True)
    inverse = lax.rsqrt(variance + NORM_EPS)
    return (centered * inverse, inverse)


def mm(left, right, dims=((1,), (0,))):
    return lax.dot_general(left, right, (dims, ((), ())), preferred_element_type=F32)


NT = ((1,), (1,))
TN = ((0,), (0,))


def col_sum(values):
    return jnp.sum(values, axis=0, keepdims=True)


def low_lanes(rows):
    return lax.broadcasted_iota(jnp.int32, (rows, PAIR), 1) < HEAD_DIM


def key_mask(padded, length):
    return lax.broadcasted_iota(jnp.int32, (padded, padded), 0) < length


def forward_kernel(x_ref, gain_ref, bias_ref, w_ref, qvb_ref, *outs):
    scaling = HEAD_DIM ** (-0.5)
    start = 0
    for group in range(2):
        first_ref, qkv_ref, mix_ref, lse_ref = outs[4 * group : 4 * group + 4]
        rows, length = PADDED[group], LENGTHS[group]
        normed, _ = norm_parts(x_ref[start : start + rows, :].astype(F32))
        start += rows
        first = (normed * gain_ref[...] + bias_ref[...]).astype(BF16)
        first_ref[...] = first
        qkv_ref[0] = (mm(first, w_ref[0]) + qvb_ref[0:1, :]).astype(BF16)
        qkv_ref[1] = mm(first, w_ref[1]).astype(BF16)
        qkv_ref[2] = (mm(first, w_ref[2]) + qvb_ref[1:2, :]).astype(BF16)
        low = low_lanes(rows)
        keep_keys = key_mask(rows, length)
        for pair in range(qkv_ref.shape[2] // PAIR):
            lanes = slice(pair * PAIR, (pair + 1) * PAIR)
            queries, keys = qkv_ref[0, :, lanes], qkv_ref[1, :, lanes]
            values_t = qkv_ref[2, :, lanes].T
            mixed_t = []
            for side in range(2):
                own = low if side == 0 else jnp.logical_not(low)
                scores = mm(keys, jnp.where(own, queries, jnp.zeros_like(queries)), NT) * scaling
                scores = jnp.where(keep_keys, scores, -jnp.inf)
                top = jnp.max(scores, axis=0, keepdims=True)
                exps = jnp.exp(scores - top)
                total = jnp.sum(exps, axis=0, keepdims=True)
                soft_low = (exps / total).astype(BF16)
                mixed_t.append(mm(values_t[side * HEAD_DIM : (side + 1) * HEAD_DIM], soft_low))
                head = 2 * pair + side
                lse_ref[head : head + 1, :] = top + jnp.log(total)
            mix_ref[:, lanes] = jnp.concatenate(mixed_t, axis=0).T.astype(BF16).astype(F32)


def mlp_kernel(
    group, info_ref, x_ref, ct_ref, mix_ref, mix2_ref, ow_ref, ow1_ref, ow2_ref, ob_ref,
    gain_ref, bias_ref, up_ref, upb_ref, down_ref,
    hidden_ref, second_ref, gmlp_ref, act_ref, gpre_ref, gs_ref, upsum_ref, downsum_ref,
    ow_all, mix_all,
):
    step = pl.program_id(0)

    @pl.when(step == 0)
    def _():
        side, core = info_ref[0], info_ref[1]
        live = (info_ref[2 + group] > 0).astype(F32)
        span, half = ow_ref.shape[0], ow1_ref.shape[0]
        mine, other = side * span, (1 - side) * span
        ow_all[pl.ds(pl.multiple_of(mine, span), span), :] = ow_ref[...]
        at1 = pl.multiple_of(other + core * half, half)
        at2 = pl.multiple_of(other + (1 - core) * half, half)
        ow_all[pl.ds(at1, half), :] = ow1_ref[...].astype(BF16)
        ow_all[pl.ds(at2, half), :] = ow2_ref[...].astype(BF16)
        mix_all[:, pl.ds(pl.multiple_of(mine, span), span)] = mix_ref[...].astype(BF16)
        mix_all[:, pl.ds(pl.multiple_of(other, span), span)] = mix2_ref[...].astype(BF16)
        branch = mm(mix_all[...], ow_all[...]) + ob_ref[...]
        hidden = x_ref[...].astype(F32) + live * branch
        hidden_ref[...] = hidden
        normed, _ = norm_parts(hidden)
        second_ref[...] = (normed * gain_ref[...] + bias_ref[...]).astype(BF16)
        gmlp = live * ct_ref[...].astype(F32)
        gmlp_ref[...] = gmlp.astype(BF16)
        downsum_ref[...] = col_sum(gmlp)

    pre = mm(second_ref[...], up_ref[...]) + upb_ref[...]
    cdf = 0.5 * (1.0 + lax.erf(pre * (0.5**0.5)))
    act_ref[...] = (pre * cdf).astype(BF16)
    slope = cdf + pre * (jnp.exp(-0.5 * pre * pre) * 0.3989422804014327)
    grad_act = mm(gmlp_ref[...], down_ref[...], NT)
    gpre = (grad_act * slope).astype(BF16)
    gpre_ref[...] = gpre
    upsum_ref[...] = col_sum(gpre.astype(F32))
    part = mm(gpre, up_ref[...], NT)

    @pl.when(step == 0)
    def _():
        gs_ref[...] = part

    @pl.when(step > 0)
    def _():
        gs_ref[...] += part


def scatter_rows(core, grad_ref, keep_ref, send_ref, cols):
    blocks, height = keep_ref.shape[0], keep_ref.shape[1]
    bits = blocks.bit_length() - 1
    for place in range(blocks):
        index = sum(((place >> (bits - 1 - b)) & 1) << b for b in range(bits))
        even = grad_ref[2 * index * height : (2 * index + 1) * height, :]
        odd = grad_ref[(2 * index + 1) * height : (2 * index + 2) * height, :]
        keep_ref[place, :, cols] = jnp.where(core == 0, even, odd)
        send_ref[place, :, cols] = jnp.where(core == 0, odd, even)


def mlp_weights_kernel(
    info_ref, seca_ref, secb_ref, gma_ref, gmb_ref, acta_ref, actb_ref, gpa_ref, gpb_ref,
    keepd_ref, sendd_ref, keepu_ref, sendu_ref, grad,
):
    core = info_ref[1]
    grad[...] = mm(gma_ref[...], acta_ref[...], TN) + mm(gmb_ref[...], actb_ref[...], TN)
    scatter_rows(core, grad, keepd_ref, sendd_ref, slice(None))
    grad[...] = mm(seca_ref[...], gpa_ref[...], TN) + mm(secb_ref[...], gpb_ref[...], TN)
    scatter_rows(core, grad, keepu_ref, sendu_ref, slice(None))


def attn_weights_kernel(
    info_ref, firsta_ref, firstb_ref, da_ref, db_ref, ga_ref, gb_ref, mixa_ref, mixb_ref,
    keep_ref, send_ref, grad,
):
    core = info_ref[1]
    width = grad.shape[1]
    for part in range(3):
        grad[...] = mm(firsta_ref[...], da_ref[part], TN) + mm(firstb_ref[...], db_ref[part], TN)
        scatter_rows(core, grad, keep_ref, send_ref, slice(part * width, (part + 1) * width))
    grad[...] = mm(ga_ref[...], mixa_ref[...].astype(BF16), TN) + mm(
        gb_ref[...], mixb_ref[...].astype(BF16), TN
    )
    scatter_rows(core, grad, keep_ref, send_ref, slice(3 * width, 4 * width))


def norm_back(grad, normed, inverse, gain):
    scaled = grad * gain
    row_inner = jnp.mean(scaled, axis=-1, keepdims=True)
    row_cross = jnp.mean(scaled * normed, axis=-1, keepdims=True)
    return inverse * (scaled - row_inner - normed * row_cross)


def backward_kernel(
    group, info_ref, gs_ref, gs2_ref, hidden_ref, ct_ref, gain_ref, ow_ref, qkv_ref, lse_ref, w_ref,
    act_ref, down_ref,
    dqkv_ref, gattn_ref, gh_ref, gf_ref, mlp_ref, sums_ref, gmix,
):
    scaling = HEAD_DIM ** (-0.5)
    rows, length = PADDED[group], LENGTHS[group]
    live = (info_ref[2 + group] > 0).astype(F32)
    grad_second = gs_ref[...] + gs2_ref[...]
    normed, inverse = norm_parts(hidden_ref[...])
    grad_hidden = ct_ref[...].astype(F32) + norm_back(grad_second, normed, inverse, gain_ref[...])
    gh_ref[...] = grad_hidden
    sums_ref[0:1, :] = col_sum(grad_second * normed)
    sums_ref[1:2, :] = col_sum(grad_second)
    gattn = (live * grad_hidden).astype(BF16)
    gattn_ref[...] = gattn
    sums_ref[2:3, :] = col_sum(gattn.astype(F32))
    gmix[...] = mm(gattn, ow_ref[...], NT).astype(BF16)
    low = low_lanes(rows)
    keep_keys = key_mask(rows, length)
    for pair in range(qkv_ref.shape[2] // PAIR):
        lanes = slice(pair * PAIR, (pair + 1) * PAIR)
        queries, keys, values = (qkv_ref[c, :, lanes] for c in range(3))
        grads = gmix[:, lanes]
        keys_t = keys.T
        zero = jnp.zeros_like(queries)
        dq_t, dk, dv = [], [], []
        for side in range(2):
            own = low if side == 0 else jnp.logical_not(low)
            head = 2 * pair + side
            scores = mm(keys, jnp.where(own, queries, zero), NT) * scaling
            soft = jnp.where(keep_keys, jnp.exp(scores - lse_ref[head : head + 1, :]), 0.0)
            grad_soft = mm(values, jnp.where(own, grads, zero), NT)
            inner = jnp.sum(grad_soft * soft, axis=0, keepdims=True)
            grad_scores = (soft * (grad_soft - inner)).astype(BF16)
            dv.append(mm(soft.astype(BF16), grads))
            dk.append(mm(grad_scores, queries))
            dq_t.append(mm(keys_t[side * HEAD_DIM : (side + 1) * HEAD_DIM], grad_scores))
        dqkv_ref[0, :, lanes] = (jnp.concatenate(dq_t, axis=0).T * scaling).astype(BF16)
        dqkv_ref[1, :, lanes] = (jnp.where(low, dk[0], dk[1]) * scaling).astype(BF16)
        dqkv_ref[2, :, lanes] = jnp.where(low, dv[0], dv[1]).astype(BF16)
    gf_ref[...] = (
        mm(dqkv_ref[0], w_ref[0], NT) + mm(dqkv_ref[1], w_ref[1], NT) + mm(dqkv_ref[2], w_ref[2], NT)
    )
    half = qkv_ref.shape[2]
    sums_ref[3:4, :half] = col_sum(dqkv_ref[0].astype(F32))
    sums_ref[3:4, half:] = col_sum(dqkv_ref[2].astype(F32))
    mlp_ref[...] = mm(act_ref[...], down_ref[...])


def input_kernel(
    xa_ref, gfa_ref, gfa2_ref, gha_ref, xb_ref, gfb_ref, gfb2_ref, ghb_ref, gain_ref,
    sa_ref, sb_ref, ua_ref, ub_ref, da_ref, db_ref, grad_ref, small_ref,
):
    start, gains, biases = 0, 0.0, 0.0
    for group, (x_ref, gf_ref, gf2_ref, gh_ref) in enumerate(
        ((xa_ref, gfa_ref, gfa2_ref, gha_ref), (xb_ref, gfb_ref, gfb2_ref, ghb_ref))
    ):
        length = LENGTHS[group]
        grad_first = gf_ref[...] + gf2_ref[...]
        normed, inverse = norm_parts(x_ref[...].astype(F32))
        value = gh_ref[...] + norm_back(grad_first, normed, inverse, gain_ref[...])
        grad_ref[start : start + length, :] = value[:length]
        start += length
        gains += col_sum(grad_first * normed)
        biases += col_sum(grad_first)
    width = grad_ref.shape[1]
    small_ref[...] = jnp.zeros_like(small_ref)
    small_ref[0:1, :] = gains
    small_ref[1:2, :] = biases
    small_ref[2:6, :] = sa_ref[0:4, :] + sb_ref[0:4, :]
    small_ref[6:7, :] = ua_ref[:, :width] + ub_ref[:, :width]
    small_ref[7:8, :] = ua_ref[:, width:] + ub_ref[:, width:]
    small_ref[8:9, :] = da_ref[...] + db_ref[...]


def output_kernel(
    info_ref, ha_ref, ma_ref, ma2_ref, hb_ref, mb_ref, mb2_ref, bias_ref, out_ref, rows_ref
):
    start = 0
    for group, (h_ref, m_ref, m2_ref) in enumerate(
        ((ha_ref, ma_ref, ma2_ref), (hb_ref, mb_ref, mb2_ref))
    ):
        live = (info_ref[2 + group] > 0).astype(F32)
        length = LENGTHS[group]
        value = h_ref[...] + live * (m_ref[...] + m2_ref[...] + bias_ref[...])
        rows_ref[start : start + length, :] = value[:length]
        start += length
    out_ref[...] = rows_ref[...].astype(BF16)


SMEM_SPEC = pl.BlockSpec(memory_space=pltpu.SMEM)


def whole(*shape):
    zeros = (0,) * len(shape)
    return pl.BlockSpec(shape, lambda *_: zeros)


def shaped(*shape, dtype=F32):
    return jax.ShapeDtypeStruct(shape, dtype)


def call(kernel, name, outs, flops, moved, exps=0, **kwargs):
    return pl.pallas_call(
        kernel,
        out_shape=outs,
        name=name,
        compiler_params=pltpu.CompilerParams(vmem_limit_bytes=VMEM_LIMIT),
        cost_estimate=pl.CostEstimate(
            flops=int(flops), bytes_accessed=int(moved), transcendentals=int(exps)
        ),
        **kwargs,
    )


def swap_sides(value):
    return lax.ppermute(value, "tensor", [(0, 1), (1, 0)])


def swap_bit(value, size, bit):
    return lax.ppermute(value, "dp", [(i, i ^ (1 << bit)) for i in range(size)])


def take(value, which):
    return lax.dynamic_index_in_dim(value, which, 0, keepdims=False)


def reduce_blocks(keep, send, size, index):
    bits = size.bit_length() - 1
    terms = [keep, swap_bit(send, size, 0)]
    for bit in range(1, bits):
        mine = (index >> bit) & 1
        halves = [t.reshape((2, t.shape[0] // 2) + t.shape[1:]) for t in terms]
        out = functools.reduce(jnp.add, [take(h, 1 - mine) for h in halves])
        terms = [take(h, mine) for h in halves]
        terms.append(swap_bit(out, size, bit))
    return functools.reduce(jnp.add, terms)[0]


def per_device(
    dp_size,
    images_in,
    small_counts,
    large_counts,
    norm1_gain,
    norm1_bias,
    qkv_weight,
    qv_bias,
    out_weight,
    out_bias,
    norm2_gain,
    norm2_bias,
    up_weight,
    up_bias,
    down_weight,
    down_bias,
    out_cotangent,
):
    width = images_in.shape[1]
    heads_width = out_weight.shape[0]
    units = down_weight.shape[0]
    index = lax.axis_index("dp")
    side = lax.axis_index("tensor")
    core = index & 1
    info = jnp.stack([side, core, small_counts[0], large_counts[0]]).astype(jnp.int32)
    row = lambda v: v.reshape(1, -1)

    half = heads_width // 2
    ow_send = lax.dynamic_slice_in_dim(out_weight, core * half, half, 0).astype(F32)
    ow_first = swap_sides(ow_send)
    ow_second = swap_bit(ow_first, dp_size, 0)

    def parts_of(array):
        pieces, at = [], 0
        for length, padded in zip(LENGTHS, PADDED):
            pieces.append(jnp.pad(array[at : at + length], ((0, padded - length), (0, 0))))
            at += length
        return pieces

    x_parts, ct_parts = parts_of(images_in), parts_of(out_cotangent)
    x_all = jnp.concatenate(x_parts, axis=0)
    weights = qkv_weight.transpose(1, 0, 2)
    total = sum(PADDED)
    head_count = heads_width // HEAD_DIM
    squares = sum(p * p for p in PADDED)
    outs = []
    for padded in PADDED:
        outs += [
            shaped(padded, width, dtype=BF16),
            shaped(3, padded, heads_width, dtype=BF16),
            shaped(padded, heads_width),
            shaped(head_count, padded),
        ]
    forward = call(
        forward_kernel, "attn_forward", tuple(outs),
        2 * total * width * 3 * heads_width + 4 * squares * heads_width, 8e6, squares * head_count,
    )(x_all, row(norm1_gain), row(norm1_bias), weights, qv_bias)
    firsts, qkvs, mixes, lses = (forward[i::4] for i in range(4))
    mixes2 = [swap_sides(m) for m in mixes]

    chunk = 512
    steps = units // chunk
    mlp = []
    for group, padded in enumerate(PADDED):
        blocks = lambda rows: pl.BlockSpec((rows, chunk), lambda i: (0, i))
        in_specs = [
            SMEM_SPEC, whole(padded, width), whole(padded, width), whole(padded, heads_width),
            whole(padded, heads_width), whole(heads_width, width), whole(half, width), whole(half, width),
            whole(1, width), whole(1, width), whole(1, width), blocks(width), blocks(1),
            pl.BlockSpec((chunk, width), lambda i: (i, 0)),
        ]
        mlp.append(
            call(
                functools.partial(mlp_kernel, group), "mlp_" + "ab"[group],
                (
                    shaped(padded, width), shaped(padded, width, dtype=BF16), shaped(padded, width, dtype=BF16),
                    shaped(padded, units, dtype=BF16), shaped(padded, units, dtype=BF16), shaped(padded, width),
                    shaped(1, units), shaped(1, width),
                ),
                2 * padded * width * (3 * units + 2 * heads_width), 12e6, padded * units,
                grid=(steps,), in_specs=in_specs,
                out_specs=(
                    whole(padded, width), whole(padded, width), whole(padded, width), blocks(padded),
                    blocks(padded), whole(padded, width), blocks(1), whole(1, width),
                ),
                scratch_shapes=[pltpu.VMEM((2 * heads_width, width), BF16), pltpu.VMEM((padded, 2 * heads_width), BF16)],
            )(
                info, x_parts[group], ct_parts[group], mixes[group], mixes2[group], out_weight, ow_first, ow_second,
                row(out_bias), row(norm2_gain), row(norm2_bias), up_weight, row(up_bias), down_weight,
            )
        )
    hidden, second, gmlp, act, gpre, gs, upsum, downsum = zip(*mlp)
    gs2 = [swap_sides(g) for g in gs]

    half_blocks, height = dp_size // 2, width // dp_size
    rows_spec = lambda n: [whole(p, n) for p in PADDED]
    cols_spec = lambda: [pl.BlockSpec((p, chunk), lambda i: (0, i)) for p in PADDED]
    grad_blocks = pl.BlockSpec((half_blocks, height, chunk), lambda i: (0, 0, i))
    keep_d, send_d, keep_u, send_u = call(
        mlp_weights_kernel, "mlp_weights", (shaped(half_blocks, height, units),) * 4,
        4 * total * width * units, 16e6, grid=(steps,),
        in_specs=[SMEM_SPEC, *rows_spec(width), *rows_spec(width), *cols_spec(), *cols_spec()],
        out_specs=(grad_blocks,) * 4,
        scratch_shapes=[pltpu.VMEM((width, chunk), F32)],
    )(info, *second, *gmlp, *act, *gpre)
    down_block = reduce_blocks(keep_d, send_d, dp_size, index)
    up_block = reduce_blocks(keep_u, send_u, dp_size, index)

    back = []
    for group, padded in enumerate(PADDED):
        back.append(
            call(
                functools.partial(backward_kernel, group), "attn_backward_" + "ab"[group],
                (
                    shaped(3, padded, heads_width, dtype=BF16), shaped(padded, width, dtype=BF16),
                    shaped(padded, width), shaped(padded, width), shaped(padded, width), shaped(8, width),
                ),
                2 * padded * width * (4 * heads_width + units) + 10 * padded * padded * heads_width, 10e6,
                padded * padded * head_count,
                in_specs=[SMEM_SPEC] + [pl.BlockSpec()] * 11,
                scratch_shapes=[pltpu.VMEM((padded, heads_width), BF16)],
            )(
                info, gs[group], gs2[group], hidden[group], ct_parts[group], row(norm2_gain), out_weight,
                qkvs[group], lses[group], weights, act[group], down_weight,
            )
        )
    dqkv, gattn, gh, gf, mlp_part, sums = zip(*back)
    gf2 = [swap_sides(g) for g in gf]
    mlp2 = [swap_sides(m) for m in mlp_part]

    keep_a, send_a = call(
        attn_weights_kernel, "attn_weights", (shaped(half_blocks, height, 4 * heads_width),) * 2,
        8 * total * width * heads_width, 8e6,
        in_specs=[SMEM_SPEC] + [pl.BlockSpec()] * 8,
        scratch_shapes=[pltpu.VMEM((width, heads_width), F32)],
    )(info, *firsts, *dqkv, *gattn, *mixes)
    attn_block = reduce_blocks(keep_a, send_a, dp_size, index)

    input_grad, small = call(
        input_kernel, "input_back", (shaped(*images_in.shape), shaped(16, width)), 30 * total * width, 8e6,
    )(
        x_parts[0], gf[0], gf2[0], gh[0], x_parts[1], gf[1], gf2[1], gh[1], row(norm1_gain),
        *sums, *upsum, *downsum,
    )
    block_out = call(
        output_kernel, "block_out", shaped(*images_in.shape, dtype=BF16), 5 * total * width, 6e6,
        in_specs=[SMEM_SPEC] + [pl.BlockSpec()] * 7,
        scratch_shapes=[pltpu.VMEM(images_in.shape, F32)],
    )(info, hidden[0], mlp_part[0], mlp2[0], hidden[1], mlp_part[1], mlp2[1], row(down_bias))
    for bit in range(dp_size.bit_length() - 1):
        small = small + swap_bit(small, dp_size, bit)

    return (
        block_out,
        input_grad,
        small[0],
        small[1],
        attn_block[:, : 3 * heads_width].reshape(height, 3, heads_width),
        small[5].reshape(2, heads_width),
        attn_block[:, 3 * heads_width :].T,
        small[4],
        small[2],
        small[3],
        up_block,
        small[6:8].reshape(-1),
        down_block.T,
        small[8],
    )


def solution(mesh):
    placed = (
        P("dp", None),
        P("dp"),
        P("dp"),
        P(),
        P(),
        P(None, None, "tensor"),
        P(None, "tensor"),
        P("tensor", None),
        P(),
        P(),
        P(),
        P(None, "tensor"),
        P("tensor"),
        P("tensor", None),
        P(),
        P("dp", None),
    )
    return jax.shard_map(
        functools.partial(per_device, mesh.shape["dp"]),
        mesh=mesh,
        in_specs=placed,
        out_specs=(
            P("dp", None),
            P("dp", None),
            P(),
            P(),
            P("dp", None, "tensor"),
            P(None, "tensor"),
            P("tensor", "dp"),
            P(),
            P(),
            P(),
            P("dp", "tensor"),
            P("tensor"),
            P("tensor", "dp"),
            P(),
        ),
        check_vma=False,
    )
```

```python
import functools

import jax
import jax.numpy as jnp
from jax import lax
from jax.experimental import pallas as pl
from jax.experimental.pallas import tpu as pltpu
from jax.sharding import PartitionSpec as P

HEAD_DIM = 64
PAIR = 2 * HEAD_DIM
LENGTHS = (197, 325)
PADDED = tuple(-(-length // 16) * 16 for length in LENGTHS)
SENT = tuple(-(-length // 8) * 8 for length in LENGTHS)
STARTS = (0, PADDED[0])
SENT_STARTS = (0, SENT[0])
ROWS = sum(PADDED)
SENT_ROWS = sum(SENT)
NORM_EPS = 1e-06
F32 = jnp.float32
BF16 = jnp.bfloat16
MIB = 1024 * 1024
NT = ((1,), (1,))
TN = ((0,), (0,))


def norm_parts(values):
    row_mean = jnp.mean(values, axis=-1, keepdims=True)
    centered = values - row_mean
    variance = jnp.mean(centered * centered, axis=-1, keepdims=True)
    inverse = lax.rsqrt(variance + NORM_EPS)
    return (centered * inverse, inverse)


def norm_back(grad, normed, inverse, gain):
    scaled = grad * gain
    row_inner = jnp.mean(scaled, axis=-1, keepdims=True)
    row_cross = jnp.mean(scaled * normed, axis=-1, keepdims=True)
    return inverse * (scaled - row_inner - normed * row_cross)


def mm(left, right, dims=((1,), (0,))):
    return lax.dot_general(left, right, (dims, ((), ())), preferred_element_type=F32)


def col_sum(values):
    return jnp.sum(values, axis=0, keepdims=True)


def row(ref):
    return ref[...].reshape(1, -1)


def low_lanes(rows):
    return lax.broadcasted_iota(jnp.int32, (rows, PAIR), 1) < HEAD_DIM


def key_mask(padded, length):
    return lax.broadcasted_iota(jnp.int32, (padded, padded), 0) < length


def of_group(group):
    return slice(STARTS[group], STARTS[group] + PADDED[group])


def sent_of(group):
    return slice(SENT_STARTS[group], SENT_STARTS[group] + SENT[group])


def filled(rows, padded):
    return jnp.concatenate([rows, jnp.zeros((padded - rows.shape[0], rows.shape[1]), rows.dtype)], axis=0)


def live_of(info_ref, group):
    return (info_ref[2 + group] > 0).astype(F32)


def forward_kernel(
    info_ref, x_ref, ct_ref, gain_ref, bias_ref, w_ref, qvb_ref,
    first_ref, qkv_ref, xpad_ref, ctpad_ref, lse0_ref, lse1_ref, mix0_ref, mix1_ref, wide,
):
    scaling = HEAD_DIM ** (-0.5)
    for source, target in ((ct_ref, ctpad_ref), (x_ref, xpad_ref)):
        wide[: source.shape[0], :] = source[...].astype(F32)
        start = 0
        for group in range(2):
            rows, length = PADDED[group], LENGTHS[group]
            real = lax.broadcasted_iota(jnp.int32, (rows, x_ref.shape[1]), 0) < length
            piece = jnp.where(real, wide[start : start + rows, :], 0.0)
            target[of_group(group), :] = piece.astype(BF16)
            start += length
    normed, _ = norm_parts(xpad_ref[...].astype(F32))
    first = (normed * row(gain_ref) + row(bias_ref)).astype(BF16)
    first_ref[...] = first
    qkv_ref[0] = (mm(first, w_ref[0]) + qvb_ref[0:1, :]).astype(BF16)
    qkv_ref[1] = mm(first, w_ref[1]).astype(BF16)
    qkv_ref[2] = (mm(first, w_ref[2]) + qvb_ref[1:2, :]).astype(BF16)
    for group, lse_ref, mix_ref in ((0, lse0_ref, mix0_ref), (1, lse1_ref, mix1_ref)):
        rows, length = PADDED[group], LENGTHS[group]
        low = low_lanes(rows)
        keep_keys = key_mask(rows, length)
        for pair in range(qkv_ref.shape[2] // PAIR):
            lanes = slice(pair * PAIR, (pair + 1) * PAIR)
            queries, keys, values = (qkv_ref[c, of_group(group), lanes] for c in range(3))
            values_t = values.T
            mixed_t = []
            for side in range(2):
                own = low if side == 0 else jnp.logical_not(low)
                scores = mm(keys, jnp.where(own, queries, jnp.zeros_like(queries)), NT) * scaling
                scores = jnp.where(keep_keys, scores, -jnp.inf)
                top = jnp.max(scores, axis=0, keepdims=True)
                exps = jnp.exp(scores - top)
                total = jnp.sum(exps, axis=0, keepdims=True)
                soft_low = (exps / total).astype(BF16)
                mixed_t.append(mm(values_t[side * HEAD_DIM : (side + 1) * HEAD_DIM], soft_low))
                head = 2 * pair + side
                lse_ref[head : head + 1, :] = top + jnp.log(total)
            mixed = jnp.concatenate(mixed_t, axis=0).T.astype(BF16).astype(F32)
            mix_ref[:, lanes] = mixed[: SENT[group]]


def relay_kernel(info_ref, in_ref, out_ref):
    out_ref[...] = in_ref[...]


def join_kernel(info_ref, ow_ref, one_ref, two_ref, got1_ref, got2_ref, ow_all):
    side, core, near = info_ref[0], info_ref[1], info_ref[5]
    span = ow_ref.shape[0]
    quarter = span // 4
    mine, other = side * span, (1 - side) * span
    ow_all[pl.ds(pl.multiple_of(mine, span), span), :] = ow_ref[...]
    for ref, where, x in (
        (one_ref, core, near), (two_ref, core, 1 - near), (got1_ref, 1 - core, near), (got2_ref, 1 - core, 1 - near),
    ):
        at = pl.multiple_of(other + (2 * where + x) * quarter, quarter)
        ow_all[pl.ds(at, quarter), :] = ref[...].astype(BF16)


def mlp_kernel(
    group, chunk, info_ref, x_ref, ct_ref, mix_ref, mix2_ref, ow_ref, ob_ref, gain_ref, bias_ref,
    up_ref, upb_ref, down_ref, *refs,
):
    *earlier, hidden_ref, second_ref, gmlp_ref, act_ref, gpre_ref, upsum_ref, downsum_ref, gs_ref, mix_all = refs
    side, live = info_ref[0], live_of(info_ref, group)
    span = mix_ref.shape[1]
    for which, ref in ((side, mix_ref), (1 - side, mix2_ref)):
        at = pl.ds(pl.multiple_of(which * span, span), span)
        mix_all[:, at] = filled(ref[...], PADDED[group]).astype(BF16)
    branch = mm(mix_all[...], ow_ref[...]) + row(ob_ref)
    hidden = x_ref[of_group(group), :].astype(F32) + live * branch
    hidden_ref[...] = hidden
    normed, _ = norm_parts(hidden)
    second = (normed * row(gain_ref) + row(bias_ref)).astype(BF16)
    second_ref[...] = second
    gmlp = live * ct_ref[of_group(group), :].astype(F32)
    downsum_ref[...] = col_sum(gmlp)
    gmlp = gmlp.astype(BF16)
    gmlp_ref[...] = gmlp
    bias = row(upb_ref)
    rows = slice(None)
    if earlier:
        gs_ref[sent_of(1 - group), :] = earlier[0][...]
        rows = sent_of(group)
    for step in range(up_ref.shape[1] // chunk):
        cols = slice(step * chunk, (step + 1) * chunk)
        pre = mm(second, up_ref[:, cols]) + bias[:, cols]
        cdf = 0.5 * (1.0 + lax.erf(pre * (0.5**0.5)))
        act_ref[:, cols] = (pre * cdf).astype(BF16)
        slope = cdf + pre * (jnp.exp(-0.5 * pre * pre) * 0.3989422804014327)
        gpre = (mm(gmlp, down_ref[cols, :], NT) * slope).astype(BF16)
        gpre_ref[:, cols] = gpre
        upsum_ref[:, cols] = col_sum(gpre.astype(F32))
        part = mm(gpre, up_ref[:, cols], NT)[: SENT[group]]
        gs_ref[rows, :] = part if step == 0 else gs_ref[rows, :] + part


def pick_blocks(wide, parity, height, length, order):
    count, bits = 1 << len(order), len(order)
    found = []
    for place in range(count):
        index = sum(((place >> (bits - 1 - n)) & 1) << (bit - 1) for n, bit in enumerate(order))
        even = wide[2 * index * height : (2 * index + 1) * height, :length]
        odd = wide[(2 * index + 1) * height : (2 * index + 2) * height, :length]
        found.append(jnp.where(parity == 0, even, odd))
    return jnp.concatenate(found, axis=0).astype(BF16)


def turned(core, height, order, left, wide):
    length = left.shape[0]
    wide[:, :length] = left.astype(F32).T
    return tuple(pick_blocks(wide, parity, height, length, order) for parity in (core, 1 - core))


def weights_kernel(height, piece, order, info_ref, l0_ref, l1_ref, r0_ref, r1_ref, keep_ref, *refs):
    *send_refs, wide = refs
    core = info_ref[1]
    keep0, send0 = turned(core, height, order, l0_ref[...], wide)
    keep1, send1 = turned(core, height, order, l1_ref[...], wide)
    for step, send_ref in enumerate(send_refs):
        cols = slice(step * piece, (step + 1) * piece)
        right0, right1 = r0_ref[:, cols], r1_ref[:, cols]
        send_ref[...] = mm(send0, right0) + mm(send1, right1)
        keep_ref[:, cols] = mm(keep0, right0) + mm(keep1, right1)


def attn_weights_kernel(
    height, order1, order2, info_ref, first_ref, dqkv0_ref, dqkv1_ref, ga0_ref, ga1_ref, mix0_ref, mix1_ref,
    s0_ref, s1_ref, u0_ref, u1_ref, d0_ref, d1_ref,
    keep1_ref, keep2_ref, small_ref, send1_ref, send2_ref, send3_ref, send4_ref, wide,
):
    core = info_ref[1]
    span = mix0_ref.shape[1]
    both = s0_ref[...] + s1_ref[...]
    up = u0_ref[...] + u1_ref[...]
    down = d0_ref[...] + d1_ref[...]
    width = small_ref.shape[1]
    small_ref[...] = jnp.zeros_like(small_ref)
    for at, value in enumerate((both[4:6], both[0:4], up[:, :width], up[:, width:], down)):
        at = (0, 2, 6, 7, 8)[at]
        small_ref[at : at + value.shape[0], :] = value
    rows = keep1_ref.shape[0]
    send1_ref[rows : rows + 16, :] = small_ref[:, :span]
    send1_ref[rows + 16 :, :] = small_ref[:, span:]
    sends = (send1_ref, send2_ref, send3_ref, send4_ref)
    for part in range(4):
        order = order1 if part < 2 else order2
        if part in (0, 2):
            left = [turned(core, height, order, first_ref[of_group(g), :], wide) for g in range(2)]
        if part < 3:
            right = [r[part] for r in (dqkv0_ref, dqkv1_ref)]
        else:
            left = [turned(core, height, order, r[...], wide) for r in (ga0_ref, ga1_ref)]
            right = [filled(r[...], p).astype(BF16) for r, p in zip((mix0_ref, mix1_ref), PADDED)]
        sends[part][: keep1_ref.shape[0], :] = mm(left[0][1], right[0]) + mm(left[1][1], right[1])
        base = part % 2 * span
        keep_ref = keep1_ref if part < 2 else keep2_ref
        keep_ref[:, base : base + span] = mm(left[0][0], right[0]) + mm(left[1][0], right[1])


def backward_kernel(
    group, info_ref, gs_ref, gs2_ref, x_ref, hidden_ref, ct_ref, gain_ref, ow_ref, qkv_ref, lse_ref, w_ref,
    *refs,
):
    *earlier, dqkv_ref, gattn_ref, gh_ref, sums_ref, gf_ref, gmix = refs
    scaling = HEAD_DIM ** (-0.5)
    rows, length = PADDED[group], LENGTHS[group]
    mine = of_group(group)
    live = live_of(info_ref, group)
    sent = sent_of(group)
    grad_second = filled(gs_ref[sent, :] + gs2_ref[sent, :], rows)
    normed, inverse = norm_parts(hidden_ref[...])
    grad_hidden = ct_ref[mine, :].astype(F32) + norm_back(grad_second, normed, inverse, row(gain_ref))
    gh_ref[...] = grad_hidden
    sums_ref[0:1, :] = col_sum(grad_second * normed)
    sums_ref[1:2, :] = col_sum(grad_second)
    gattn = (live * grad_hidden).astype(BF16)
    gattn_ref[...] = gattn
    sums_ref[2:3, :] = col_sum(gattn.astype(F32))
    gmix[...] = mm(gattn, ow_ref[...], NT).astype(BF16)
    low = low_lanes(rows)
    keep_keys = key_mask(rows, length)
    for pair in range(qkv_ref.shape[2] // PAIR):
        lanes = slice(pair * PAIR, (pair + 1) * PAIR)
        queries, keys, values = (qkv_ref[c, mine, lanes] for c in range(3))
        grads = gmix[:, lanes]
        keys_t = keys.T
        zero = jnp.zeros_like(queries)
        dq_t, dk, dv = [], [], []
        for side in range(2):
            own = low if side == 0 else jnp.logical_not(low)
            head = 2 * pair + side
            scores = mm(keys, jnp.where(own, queries, zero), NT) * scaling
            soft = jnp.where(keep_keys, jnp.exp(scores - lse_ref[head : head + 1, :]), 0.0)
            grad_soft = mm(values, jnp.where(own, grads, zero), NT)
            inner = jnp.sum(grad_soft * soft, axis=0, keepdims=True)
            grad_scores = (soft * (grad_soft - inner)).astype(BF16)
            dv.append(mm(soft.astype(BF16), grads))
            dk.append(mm(grad_scores, queries))
            dq_t.append(mm(keys_t[side * HEAD_DIM : (side + 1) * HEAD_DIM], grad_scores))
        dqkv_ref[0, :, lanes] = (jnp.concatenate(dq_t, axis=0).T * scaling).astype(BF16)
        dqkv_ref[1, :, lanes] = (jnp.where(low, dk[0], dk[1]) * scaling).astype(BF16)
        dqkv_ref[2, :, lanes] = jnp.where(low, dv[0], dv[1]).astype(BF16)
    part = mm(dqkv_ref[0], w_ref[0], NT) + mm(dqkv_ref[1], w_ref[1], NT) + mm(dqkv_ref[2], w_ref[2], NT)
    if earlier:
        gf_ref[sent_of(1 - group), :] = earlier[0][...]
        gf_ref[sent, :] = part[: SENT[group]]
    else:
        gf_ref[...] = part[: SENT[group]]
    first_normed, _ = norm_parts(x_ref[mine, :].astype(F32))
    sums_ref[4:5, :] = col_sum(part * first_normed)
    sums_ref[5:6, :] = col_sum(part)
    half = qkv_ref.shape[2]
    sums_ref[3:4, :half] = col_sum(dqkv_ref[0].astype(F32))
    sums_ref[3:4, half:] = col_sum(dqkv_ref[2].astype(F32))


def mlp_part_kernel(info_ref, act0_ref, act1_ref, down_ref, out_ref):
    for group, act_ref in enumerate((act0_ref, act1_ref)):
        out_ref[sent_of(group), :] = mm(act_ref[...], down_ref[...])[: SENT[group]]


def small_end_kernel(info_ref, small_ref, other_ref, gain1, bias1, gain2, bias2, outb, qvb, upb, downb):
    total = small_ref[...]
    width = total.shape[1]
    total = jnp.concatenate([total[0:2] + other_ref[0:2, :], total[2:]], axis=0)
    for n, ref in enumerate((gain1, bias1, gain2, bias2, outb)):
        ref[...] = total[n].reshape(width)
    qvb[0:1, :] = total[5:6, : width // 2]
    qvb[1:2, :] = total[5:6, width // 2 :]
    upb[:width] = total[6].reshape(width)
    upb[width:] = total[7].reshape(width)
    downb[...] = total[8].reshape(width)


def input_kernel(info_ref, x_ref, gh0_ref, gh1_ref, gain_ref, gf_ref, gf2_ref, grad_ref):
    start = 0
    for group, gh_ref in enumerate((gh0_ref, gh1_ref)):
        length, sent = LENGTHS[group], sent_of(group)
        grad_first = gf_ref[sent, :] + gf2_ref[sent, :]
        normed, inverse = norm_parts(x_ref[of_group(group), :].astype(F32)[: SENT[group]])
        value = gh_ref[: SENT[group], :] + norm_back(grad_first, normed, inverse, row(gain_ref))
        grad_ref[start : start + length, :] = value[:length]
        start += length


def output_kernel(info_ref, h0_ref, h1_ref, m_ref, m2_ref, bias_ref, out_ref, wide):
    start = 0
    for group, h_ref in enumerate((h0_ref, h1_ref)):
        length, mine = LENGTHS[group], sent_of(group)
        value = h_ref[: SENT[group], :] + live_of(info_ref, group) * (
            m_ref[mine, :] + m2_ref[mine, :] + row(bias_ref)
        )
        wide[start : start + length, :] = value[:length]
        start += length
    out_ref[...] = wide[...].astype(BF16)


def stage_kernel(bit, count, info_ref, keep_ref, *refs):
    pieces, (send_ref, rest_ref) = refs[:count], refs[count:]
    mine = info_ref[4 + bit]
    half = keep_ref.shape[0] // 2
    at = 0
    for piece in pieces:
        cols = slice(at, at + piece.shape[1])
        at += piece.shape[1]
        low = keep_ref[:half, cols] + piece[:half, :]
        high = keep_ref[half:, cols] + piece[half:, :]
        send_ref[:, cols] = jnp.where(mine == 0, high, low)
        rest_ref[:, cols] = jnp.where(mine == 0, low, high)


def stage_both_kernel(bit, info_ref, keep1_ref, keep2_ref, got1_ref, got2_ref, send_ref, rest_ref):
    cols = keep1_ref.shape[1]
    for n, (keep_ref, got_ref) in enumerate(((keep1_ref, got1_ref), (keep2_ref, got2_ref))):
        at = pl.ds(n * cols, cols)
        stage_kernel(bit, 1, info_ref, keep_ref, got_ref, send_ref.at[:, at], rest_ref.at[:, at])


def both_end_kernel(info_ref, keep_ref, got_ref, down_ref, up_ref):
    cols = down_ref.shape[1]
    down_ref[...] = keep_ref[:, :cols] + got_ref[:, :cols]
    up_ref[...] = keep_ref[:, cols:] + got_ref[:, cols:]


def stage_small_kernel(bit, count, last, info_ref, keep_ref, small_ref, *refs):
    pieces, outs = refs[:count], refs[count:]
    rows, span = keep_ref.shape[0], pieces[0].shape[1]
    if count == 2:
        other = jnp.concatenate([pieces[0][rows : rows + 16, :], pieces[0][rows + 16 :, :]], axis=1)
    else:
        other = pieces[0][rows:, :]
    small = small_ref[...] + other
    if last:
        out_ref, total_ref = outs
        total_ref[...] = small
        out_ref[...] = keep_ref[...] + pieces[0][:rows, :]
        return
    send_ref, rest_ref, total_ref = outs
    total_ref[...] = small
    mine, half, at = info_ref[4 + bit], rows // 2, 0
    for piece in pieces:
        cols = slice(at, at + piece.shape[1])
        at += piece.shape[1]
        low = keep_ref[:half, cols] + piece[:half, :]
        high = keep_ref[half:, cols] + piece[half:rows, :]
        send_ref[:half, cols] = jnp.where(mine == 0, high, low)
        rest_ref[:, cols] = jnp.where(mine == 0, low, high)
    send_ref[half:, :] = small


def last_kernel(info_ref, keep_ref, piece_ref, out_ref):
    out_ref[...] = keep_ref[...] + piece_ref[...]


def attn_last_kernel(info_ref, done1_ref, keep2_ref, got2_ref, qkv_ref, out_ref):
    span = out_ref.shape[1]
    qkv_ref[0] = done1_ref[:, :span]
    qkv_ref[1] = done1_ref[:, span:]
    qkv_ref[2] = keep2_ref[:, :span] + got2_ref[:, :span]
    out_ref[...] = keep2_ref[:, span:] + got2_ref[:, span:]


SMEM_SPEC = pl.BlockSpec(memory_space=pltpu.SMEM)
VMEM_SPEC = pl.BlockSpec(memory_space=pltpu.VMEM)
LATER = pl.BlockSpec(memory_space=pl.ANY)


def held(*shape, dtype=F32):
    return pltpu.VMEM(shape, dtype)


def shaped(*shape, dtype=F32):
    return jax.ShapeDtypeStruct(shape, dtype)


def in_vmem(value):
    return pltpu.with_memory_space_constraint(value, pltpu.VMEM)


def in_hbm(value):
    return pltpu.with_memory_space_constraint(value, pltpu.HBM)


class Order:
    def __init__(self, info, always):
        self.info = info
        self.always = always
        self.last = None

    def together(self, part, *watched):
        before = self.last
        states = [(v, dict(vars(v))) for v in watched]
        shapes = jax.eval_shape(part)
        self.last = before
        for value, state in states:
            vars(value).update(state)
        results = lax.cond(self.always, part, lambda: jax.tree.map(lambda v: jnp.zeros(v.shape, v.dtype), shapes))
        self.last = jax.tree.leaves(results)[0]
        return results

    def call(self, kernel, name, outs, operands, room=3, plain=False, after=(), **kwargs):
        many = isinstance(outs, (tuple, list))
        outs = tuple(outs) if many else (outs,)
        count = len(operands) + 1
        extra = [*after] if self.last is None else [*after, self.last]

        def body(*refs):
            kernel(*refs[:count], *refs[count + len(extra) :])

        results = pl.pallas_call(
            body,
            out_shape=outs,
            name=name,
            in_specs=[SMEM_SPEC] + [pl.BlockSpec() if plain else VMEM_SPEC] * (count - 1) + [LATER] * len(extra),
            out_specs=(VMEM_SPEC,) * len(outs),
            compiler_params=pltpu.CompilerParams(vmem_limit_bytes=room * MIB),
            cost_estimate=pl.CostEstimate(flops=1, bytes_accessed=1, transcendentals=0),
            **kwargs,
        )(self.info, *map(in_hbm if plain else in_vmem, operands), *extra)
        self.last = results[0]
        return results if many else results[0]


def swap_sides(value):
    return lax.ppermute(value, "tensor", [(0, 1), (1, 0)])


def swap_bit(value, size, bit):
    return lax.ppermute(value, "dp", [(i, i ^ (1 << bit)) for i in range(size)])


class Scatter:
    def __init__(self, order, size, bits, keep, send, small=None):
        self.small = small
        self.order, self.size, self.bits, self.keep, self.level = order, size, bits, keep, 0
        self.got = [swap_bit(piece, size, 0) for piece in send]

    def stage(self, name):
        bit = self.bits[self.level]
        self.level += 1
        half = (self.keep.shape[0] // 2, self.keep.shape[1])
        if self.small is not None:
            send, self.keep, self.small = self.order.call(
                functools.partial(stage_small_kernel, bit, len(self.got), False), f"{name}_{self.level}",
                (held(half[0] + 16, half[1]), held(*half), held(16, half[1])), [self.keep, self.small, *self.got],
            )
            self.got = [swap_bit(send, self.size, bit)]
            return
        send, self.keep = self.order.call(
            functools.partial(stage_kernel, bit, len(self.got)), f"{name}_{self.level}",
            (held(*half), held(*half)), [self.keep, *self.got],
        )
        self.got = [swap_bit(send, self.size, bit)]

    def last(self, name):
        return self.order.call(last_kernel, name, shaped(*self.keep.shape), [self.keep, *self.got])


def per_device(
    dp_size,
    images_in,
    small_counts,
    large_counts,
    norm1_gain,
    norm1_bias,
    qkv_weight,
    qv_bias,
    out_weight,
    out_bias,
    norm2_gain,
    norm2_bias,
    up_weight,
    up_bias,
    down_weight,
    down_bias,
    out_cotangent,
):
    width = images_in.shape[1]
    span = out_weight.shape[0]
    units = down_weight.shape[0]
    index = lax.axis_index("dp")
    side = lax.axis_index("tensor")
    core = index & 1
    bits = dp_size.bit_length() - 1
    height = width // dp_size
    order = Order(
        jnp.stack(
            [side, core, small_counts[0], large_counts[0]] + [(index >> b) & 1 for b in range(bits)]
        ).astype(jnp.int32),
        index < dp_size,
    )

    quarter = span // 4
    near = (index >> 1) & 1
    ow_send = lax.dynamic_slice_in_dim(out_weight, (2 * core + near) * quarter, quarter, 0).astype(F32)
    ow_one = swap_sides(ow_send)

    weights = qkv_weight.transpose(1, 0, 2)
    heads = span // HEAD_DIM
    first, qkv, x_pad, ct_pad, *rest = order.call(
        forward_kernel, "attn_forward",
        (
            held(ROWS, width, dtype=BF16), held(3, ROWS, span, dtype=BF16), held(ROWS, width, dtype=BF16),
            held(ROWS, width, dtype=BF16), *(held(heads, p) for p in PADDED), *(held(p, span) for p in SENT),
        ),
        [images_in, out_cotangent, norm1_gain, norm1_bias, weights, qv_bias], room=24, plain=True,
        scratch_shapes=[pltpu.VMEM((LENGTHS[0] + PADDED[1] + 3, width), F32)],
    )
    lse, mix = rest[:2], rest[2:]
    mix2 = [swap_sides(m) for m in mix]
    ow_one = order.call(relay_kernel, "out_weight_relay", held(quarter, width), [ow_one])
    ow_two = swap_bit(ow_one, dp_size, 1)
    ow_got1 = swap_bit(ow_one, dp_size, 0)
    ow_two = order.call(relay_kernel, "out_weight_next", held(quarter, width), [ow_two])
    ow_got2 = swap_bit(ow_two, dp_size, 0)
    ow_all = order.call(
        join_kernel, "out_weight_join", held(2 * span, width, dtype=BF16),
        [out_weight, ow_one, ow_two, ow_got1, ow_got2],
    )

    mlp, gs = [None, None], []
    for group in (1, 0):
        padded = PADDED[group]
        tall = SENT[group] + sum(g.shape[0] for g in gs)
        *mlp[group], total = order.call(
            functools.partial(mlp_kernel, group, 512), "mlp_" + "ab"[group],
            (
                held(padded, width), held(padded, width, dtype=BF16), held(padded, width, dtype=BF16),
                held(padded, units, dtype=BF16), held(padded, units, dtype=BF16),
                held(1, units), held(1, width), held(tall, width),
            ),
            [
                x_pad, ct_pad, mix[group], mix2[group], ow_all, out_bias, norm2_gain, norm2_bias,
                up_weight, up_bias, down_weight, *gs,
            ],
            room=16, scratch_shapes=[pltpu.VMEM((padded, 2 * span), BF16)],
        )
        gs = [total]
    gs = gs[0]
    gs2 = swap_sides(gs)
    hidden, second, gmlp, act, gpre, upsum, downsum = zip(*mlp)

    first_x = tuple(range(1, bits))
    first_z = (2, 1) + first_x[2:]

    def weight_grads(name, bit_order, left, right, piece):
        count = units // piece
        keep, *send = order.call(
            functools.partial(weights_kernel, height, piece, bit_order), name,
            (held(width // 2, units),) + (held(width // 2, piece),) * count, [*left, *right], room=12,
            scratch_shapes=[pltpu.VMEM((width, max(PADDED)), F32)],
        )
        return Scatter(order, dp_size, bit_order, keep, send)

    down_sum = weight_grads("down_weights", first_z, gmlp, act, 768)
    up_sum = weight_grads("up_weights", first_x, second, gpre, 768)
    down_sum.stage("down")
    up_sum.stage("up")
    mlp_part = order.call(mlp_part_kernel, "mlp_part", held(SENT_ROWS, width), [*act, down_weight], room=8)

    def go_back(group, *earlier):
        padded = PADDED[group]
        tall = SENT[group] + sum(e.shape[0] for e in earlier)
        return order.call(
            functools.partial(backward_kernel, group), "attn_backward_" + "ab"[group],
            (
                held(3, padded, span, dtype=BF16), held(padded, width, dtype=BF16),
                held(padded, width), held(8, width), held(tall, width),
            ),
            [
                gs, gs2, x_pad, hidden[group], ct_pad, norm2_gain, out_weight, qkv, lse[group], weights, *earlier,
            ],
            scratch_shapes=[pltpu.VMEM((padded, span), BF16)], room=16,
        )

    down_sum.stage("down")
    up_sum.stage("up")
    mlp_part = order.call(relay_kernel, "mlp_relay", held(SENT_ROWS, width), [mlp_part], after=[gs2])
    mlp2 = swap_sides(mlp_part)
    *back1, gf = go_back(1)
    *back0, gf = go_back(0, gf)
    gf2 = swap_sides(gf)
    dqkv, gattn, gh, sums = zip(back0, back1)

    for n in range(3, bits - 1):
        down_sum.stage("down")
        up_sum.stage("up")
    half = (down_sum.keep.shape[0] // 2, 2 * units)
    both, keep_both = order.call(
        functools.partial(stage_both_kernel, first_x[-1]), "mlp_3", (held(*half), held(*half)),
        [down_sum.keep, up_sum.keep, *down_sum.got, *up_sum.got],
    )
    got_both = swap_bit(both, dp_size, first_x[-1])
    rows = width // 2
    keep1, keep2, small, *send = order.call(
        functools.partial(attn_weights_kernel, height, first_x, first_z), "attn_weights",
        (
            held(rows, 2 * span), held(rows, 2 * span), held(16, width),
            held(rows + 32, span), held(rows, span), held(rows, span), held(rows, span),
        ),
        [first, *dqkv, *gattn, *mix, *sums, *upsum, *downsum], room=12,
        scratch_shapes=[pltpu.VMEM((width, max(PADDED)), F32)],
    )
    attn1 = Scatter(order, dp_size, first_x, keep1, send[:2], small)
    attn2 = Scatter(order, dp_size, first_z, keep2, send[2:])
    attn1.stage("attn1")
    attn2.stage("attn2")
    block_out = order.call(
        output_kernel, "block_out", shaped(*images_in.shape, dtype=BF16),
        [*hidden, mlp_part, mlp2, down_bias], room=8, scratch_shapes=[pltpu.VMEM(images_in.shape, F32)],
    )

    def attn_rest():
        for n in range(1, bits - 1):
            attn1.stage("attn1")
            attn2.stage("attn2")
        done1, total = order.call(
            functools.partial(stage_small_kernel, 0, 1, True), "attn1_end", (held(height, width), held(16, width)),
            [attn1.keep, attn1.small, *attn1.got],
        )
        ends = order.call(
            attn_last_kernel, "attn_end", (held(3, height, span), held(height, span)),
            [done1, attn2.keep, *attn2.got],
        )
        return (*ends, total)

    qkv_block, out_block, small = order.together(attn_rest, attn1, attn2)
    small2 = swap_sides(small)
    down_block, up_block = order.call(
        both_end_kernel, "mlp_end", (shaped(height, units),) * 2, [keep_both, got_both]
    )
    input_grad = order.call(
        input_kernel, "input_back", shaped(*images_in.shape), [x_pad, *gh, norm1_gain, gf, gf2], room=8
    )
    vector = shaped(width)
    small_out = order.call(
        small_end_kernel, "small_end",
        (vector, vector, vector, vector, vector, shaped(2, span), shaped(units), vector),
        [small, small2],
    )

    return (
        block_out,
        input_grad,
        small_out[0],
        small_out[1],
        qkv_block.transpose(1, 0, 2),
        small_out[5],
        out_block.T,
        small_out[4],
        small_out[2],
        small_out[3],
        up_block,
        small_out[6],
        down_block.T,
        small_out[7],
    )


def solution(mesh):
    placed = (
        P("dp", None),
        P("dp"),
        P("dp"),
        P(),
        P(),
        P(None, None, "tensor"),
        P(None, "tensor"),
        P("tensor", None),
        P(),
        P(),
        P(),
        P(None, "tensor"),
        P("tensor"),
        P("tensor", None),
        P(),
        P("dp", None),
    )
    return jax.shard_map(
        functools.partial(per_device, mesh.shape["dp"]),
        mesh=mesh,
        in_specs=placed,
        out_specs=(
            P("dp", None),
            P("dp", None),
            P(),
            P(),
            P("dp", None, "tensor"),
            P(None, "tensor"),
            P("tensor", "dp"),
            P(),
            P(),
            P(),
            P("dp", "tensor"),
            P("tensor"),
            P("tensor", "dp"),
            P(),
        ),
        check_vma=False,
    )
```

```python
import functools

import jax
import jax.numpy as jnp
from jax import lax
from jax.experimental import pallas as pl
from jax.experimental.pallas import tpu as pltpu
from jax.sharding import PartitionSpec as P

HEAD_DIM = 64
PAIR = 2 * HEAD_DIM
LENGTHS = (197, 325)
PADDED = tuple(-(-length // 16) * 16 for length in LENGTHS)
SENT = tuple(-(-length // 8) * 8 for length in LENGTHS)
STARTS = (0, PADDED[0])
SENT_STARTS = (0, SENT[0])
ROWS = sum(PADDED)
SENT_ROWS = sum(SENT)
NORM_EPS = 1e-06
F32 = jnp.float32
BF16 = jnp.bfloat16
MIB = 1024 * 1024
COST = {'attn_backward_b': 100000000000, 'block_out': 100000000000, 'mlp_3': 7000000000}
OPT = {'tail': 0, 's2': 1, 's3': 1, 'block': 0, 'relay': 0, 'mlp': 1, 'dpiece': 768, 'upiece': 768, 'apiece': 384, 'both': 2, 'input': 0, 'z': 'u'}
NT = ((1,), (1,))
TN = ((0,), (0,))


def norm_parts(values):
    row_mean = jnp.mean(values, axis=-1, keepdims=True)
    centered = values - row_mean
    variance = jnp.mean(centered * centered, axis=-1, keepdims=True)
    inverse = lax.rsqrt(variance + NORM_EPS)
    return (centered * inverse, inverse)


def norm_back(grad, normed, inverse, gain):
    scaled = grad * gain
    row_inner = jnp.mean(scaled, axis=-1, keepdims=True)
    row_cross = jnp.mean(scaled * normed, axis=-1, keepdims=True)
    return inverse * (scaled - row_inner - normed * row_cross)


def mm(left, right, dims=((1,), (0,))):
    return lax.dot_general(left, right, (dims, ((), ())), preferred_element_type=F32)


def col_sum(values):
    return jnp.sum(values, axis=0, keepdims=True)


def row(ref):
    return ref[...].reshape(1, -1)


def low_lanes(rows):
    return lax.broadcasted_iota(jnp.int32, (rows, PAIR), 1) < HEAD_DIM


def key_mask(padded, length):
    return lax.broadcasted_iota(jnp.int32, (padded, padded), 0) < length


def of_group(group):
    return slice(STARTS[group], STARTS[group] + PADDED[group])


def sent_of(group):
    return slice(SENT_STARTS[group], SENT_STARTS[group] + SENT[group])


def filled(rows, padded):
    return jnp.concatenate([rows, jnp.zeros((padded - rows.shape[0], rows.shape[1]), rows.dtype)], axis=0)


def live_of(info_ref, group):
    return (info_ref[2 + group] > 0).astype(F32)


def forward_kernel(
    info_ref, x_ref, ct_ref, gain_ref, bias_ref, w_ref, qvb_ref,
    first_ref, qkv_ref, xpad_ref, ctpad_ref, lse0_ref, lse1_ref, mix0_ref, mix1_ref, wide,
):
    scaling = HEAD_DIM ** (-0.5)
    for source, target in ((ct_ref, ctpad_ref), (x_ref, xpad_ref)):
        wide[: source.shape[0], :] = source[...].astype(F32)
        start = 0
        for group in range(2):
            rows, length = PADDED[group], LENGTHS[group]
            real = lax.broadcasted_iota(jnp.int32, (rows, x_ref.shape[1]), 0) < length
            piece = jnp.where(real, wide[start : start + rows, :], 0.0)
            target[of_group(group), :] = piece.astype(BF16)
            start += length
    normed, _ = norm_parts(xpad_ref[...].astype(F32))
    first = (normed * row(gain_ref) + row(bias_ref)).astype(BF16)
    first_ref[...] = first
    qkv_ref[0] = (mm(first, w_ref[0]) + qvb_ref[0:1, :]).astype(BF16)
    qkv_ref[1] = mm(first, w_ref[1]).astype(BF16)
    qkv_ref[2] = (mm(first, w_ref[2]) + qvb_ref[1:2, :]).astype(BF16)
    for group, lse_ref, mix_ref in ((0, lse0_ref, mix0_ref), (1, lse1_ref, mix1_ref)):
        rows, length = PADDED[group], LENGTHS[group]
        low = low_lanes(rows)
        keep_keys = key_mask(rows, length)
        for pair in range(qkv_ref.shape[2] // PAIR):
            lanes = slice(pair * PAIR, (pair + 1) * PAIR)
            queries, keys, values = (qkv_ref[c, of_group(group), lanes] for c in range(3))
            values_t = values.T
            mixed_t = []
            for side in range(2):
                own = low if side == 0 else jnp.logical_not(low)
                scores = mm(keys, jnp.where(own, queries, jnp.zeros_like(queries)), NT) * scaling
                scores = jnp.where(keep_keys, scores, -jnp.inf)
                top = jnp.max(scores, axis=0, keepdims=True)
                exps = jnp.exp(scores - top)
                total = jnp.sum(exps, axis=0, keepdims=True)
                soft_low = (exps / total).astype(BF16)
                mixed_t.append(mm(values_t[side * HEAD_DIM : (side + 1) * HEAD_DIM], soft_low))
                head = 2 * pair + side
                lse_ref[head : head + 1, :] = top + jnp.log(total)
            mixed = jnp.concatenate(mixed_t, axis=0).T.astype(BF16).astype(F32)
            mix_ref[:, lanes] = mixed[: SENT[group]]


def relay_kernel(info_ref, in_ref, out_ref):
    out_ref[...] = in_ref[...]


def join_kernel(info_ref, ow_ref, one_ref, two_ref, got1_ref, got2_ref, ow_all):
    side, core, near = info_ref[0], info_ref[1], info_ref[5]
    span = ow_ref.shape[0]
    quarter = span // 4
    mine, other = side * span, (1 - side) * span
    ow_all[pl.ds(pl.multiple_of(mine, span), span), :] = ow_ref[...]
    for ref, where, x in (
        (one_ref, core, near), (two_ref, core, 1 - near), (got1_ref, 1 - core, near), (got2_ref, 1 - core, 1 - near),
    ):
        at = pl.multiple_of(other + (2 * where + x) * quarter, quarter)
        ow_all[pl.ds(at, quarter), :] = ref[...].astype(BF16)


def mlp_kernel(
    group, chunk, info_ref, x_ref, ct_ref, mix_ref, mix2_ref, ow_ref, ob_ref, gain_ref, bias_ref,
    up_ref, upb_ref, down_ref, *refs,
):
    *earlier, hidden_ref, second_ref, gmlp_ref, act_ref, gpre_ref, upsum_ref, downsum_ref, gs_ref, mix_all = refs
    side, live = info_ref[0], live_of(info_ref, group)
    span = mix_ref.shape[1]
    for which, ref in ((side, mix_ref), (1 - side, mix2_ref)):
        at = pl.ds(pl.multiple_of(which * span, span), span)
        mix_all[:, at] = filled(ref[...], PADDED[group]).astype(BF16)
    branch = mm(mix_all[...], ow_ref[...]) + row(ob_ref)
    hidden = x_ref[of_group(group), :].astype(F32) + live * branch
    hidden_ref[...] = hidden
    normed, _ = norm_parts(hidden)
    second = (normed * row(gain_ref) + row(bias_ref)).astype(BF16)
    second_ref[...] = second
    gmlp = live * ct_ref[of_group(group), :].astype(F32)
    downsum_ref[...] = col_sum(gmlp)
    gmlp = gmlp.astype(BF16)
    gmlp_ref[...] = gmlp
    bias = row(upb_ref)
    rows = slice(None)
    if earlier:
        gs_ref[sent_of(1 - group), :] = earlier[0][...]
        rows = sent_of(group)
    for step in range(up_ref.shape[1] // chunk):
        cols = slice(step * chunk, (step + 1) * chunk)
        pre = mm(second, up_ref[:, cols]) + bias[:, cols]
        cdf = 0.5 * (1.0 + lax.erf(pre * (0.5**0.5)))
        act_ref[:, cols] = (pre * cdf).astype(BF16)
        slope = cdf + pre * (jnp.exp(-0.5 * pre * pre) * 0.3989422804014327)
        gpre = (mm(gmlp, down_ref[cols, :], NT) * slope).astype(BF16)
        gpre_ref[:, cols] = gpre
        upsum_ref[:, cols] = col_sum(gpre.astype(F32))
        part = mm(gpre, up_ref[:, cols], NT)[: SENT[group]]
        gs_ref[rows, :] = part if step == 0 else gs_ref[rows, :] + part


def pick_blocks(wide, parity, height, length, order):
    count, bits = 1 << len(order), len(order)
    found = []
    for place in range(count):
        index = sum(((place >> (bits - 1 - n)) & 1) << (bit - 1) for n, bit in enumerate(order))
        even = wide[2 * index * height : (2 * index + 1) * height, :length]
        odd = wide[(2 * index + 1) * height : (2 * index + 2) * height, :length]
        found.append(jnp.where(parity == 0, even, odd))
    return jnp.concatenate(found, axis=0).astype(BF16)


def turned(core, height, order, left, wide):
    length = left.shape[0]
    wide[:, :length] = left.astype(F32).T
    return tuple(pick_blocks(wide, parity, height, length, order) for parity in (core, 1 - core))


def weights_kernel(height, piece, order, info_ref, l0_ref, l1_ref, r0_ref, r1_ref, keep_ref, *refs):
    *send_refs, wide = refs
    core = info_ref[1]
    keep0, send0 = turned(core, height, order, l0_ref[...], wide)
    keep1, send1 = turned(core, height, order, l1_ref[...], wide)
    for step, send_ref in enumerate(send_refs):
        cols = slice(step * piece, (step + 1) * piece)
        right0, right1 = r0_ref[:, cols], r1_ref[:, cols]
        send_ref[...] = mm(send0, right0) + mm(send1, right1)
        keep_ref[:, cols] = mm(keep0, right0) + mm(keep1, right1)


def attn_weights_kernel(
    height, order1, order2, info_ref, first_ref, dqkv0_ref, dqkv1_ref, ga0_ref, ga1_ref, mix0_ref, mix1_ref,
    s0_ref, s1_ref, u0_ref, u1_ref, d0_ref, d1_ref,
    keep1_ref, keep2_ref, small_ref, *send_refs,
):
    *send_refs, wide = send_refs
    core = info_ref[1]
    span = mix0_ref.shape[1]
    both = s0_ref[...] + s1_ref[...]
    up = u0_ref[...] + u1_ref[...]
    down = d0_ref[...] + d1_ref[...]
    width = small_ref.shape[1]
    small_ref[...] = jnp.zeros_like(small_ref)
    for at, value in enumerate((both[4:6], both[0:4], up[:, :width], up[:, width:], down)):
        at = (0, 2, 6, 7, 8)[at]
        small_ref[at : at + value.shape[0], :] = value
    rows = keep1_ref.shape[0]
    piece = send_refs[0].shape[1]
    for n in range(width // piece):
        send_refs[0][rows + 16 * n : rows + 16 * (n + 1), :] = small_ref[:, n * piece : (n + 1) * piece]
    for part in range(4):
        order = order1 if part < 2 else order2
        if part == 0 or (part == 2 and order1 != order2):
            left = [turned(core, height, order, first_ref[of_group(g), :], wide) for g in range(2)]
        if part < 3:
            right = [r[part] for r in (dqkv0_ref, dqkv1_ref)]
        else:
            left = [turned(core, height, order, r[...], wide) for r in (ga0_ref, ga1_ref)]
            right = [filled(r[...], p).astype(BF16) for r, p in zip((mix0_ref, mix1_ref), PADDED)]
        at = part * span
        out = mm(left[0][1], right[0]) + mm(left[1][1], right[1])
        begin = 0
        while begin < span:
            inner = (at + begin) % piece
            count = min(span - begin, piece - inner)
            send_refs[(at + begin) // piece][:rows, inner : inner + count] = out[:, begin : begin + count]
            begin += count
        base = part % 2 * span
        keep_ref = keep1_ref if part < 2 else keep2_ref
        keep_ref[:, base : base + span] = mm(left[0][0], right[0]) + mm(left[1][0], right[1])


def backward_kernel(
    group, info_ref, gs_ref, gs2_ref, x_ref, hidden_ref, ct_ref, gain_ref, ow_ref, qkv_ref, lse_ref, w_ref,
    *refs,
):
    *earlier, dqkv_ref, gattn_ref, gh_ref, sums_ref, gf_ref, gmix = refs
    scaling = HEAD_DIM ** (-0.5)
    rows, length = PADDED[group], LENGTHS[group]
    mine = of_group(group)
    live = live_of(info_ref, group)
    sent = sent_of(group)
    grad_second = filled(gs_ref[sent, :] + gs2_ref[sent, :], rows)
    normed, inverse = norm_parts(hidden_ref[...])
    grad_hidden = ct_ref[mine, :].astype(F32) + norm_back(grad_second, normed, inverse, row(gain_ref))
    gh_ref[...] = grad_hidden
    sums_ref[0:1, :] = col_sum(grad_second * normed)
    sums_ref[1:2, :] = col_sum(grad_second)
    gattn = (live * grad_hidden).astype(BF16)
    gattn_ref[...] = gattn
    sums_ref[2:3, :] = col_sum(gattn.astype(F32))
    gmix[...] = mm(gattn, ow_ref[...], NT).astype(BF16)
    low = low_lanes(rows)
    keep_keys = key_mask(rows, length)
    for pair in range(qkv_ref.shape[2] // PAIR):
        lanes = slice(pair * PAIR, (pair + 1) * PAIR)
        queries, keys, values = (qkv_ref[c, mine, lanes] for c in range(3))
        grads = gmix[:, lanes]
        keys_t = keys.T
        zero = jnp.zeros_like(queries)
        dq_t, dk, dv = [], [], []
        for side in range(2):
            own = low if side == 0 else jnp.logical_not(low)
            head = 2 * pair + side
            scores = mm(keys, jnp.where(own, queries, zero), NT) * scaling
            soft = jnp.where(keep_keys, jnp.exp(scores - lse_ref[head : head + 1, :]), 0.0)
            grad_soft = mm(values, jnp.where(own, grads, zero), NT)
            inner = jnp.sum(grad_soft * soft, axis=0, keepdims=True)
            grad_scores = (soft * (grad_soft - inner)).astype(BF16)
            dv.append(mm(soft.astype(BF16), grads))
            dk.append(mm(grad_scores, queries))
            dq_t.append(mm(keys_t[side * HEAD_DIM : (side + 1) * HEAD_DIM], grad_scores))
        dqkv_ref[0, :, lanes] = (jnp.concatenate(dq_t, axis=0).T * scaling).astype(BF16)
        dqkv_ref[1, :, lanes] = (jnp.where(low, dk[0], dk[1]) * scaling).astype(BF16)
        dqkv_ref[2, :, lanes] = jnp.where(low, dv[0], dv[1]).astype(BF16)
    part = mm(dqkv_ref[0], w_ref[0], NT) + mm(dqkv_ref[1], w_ref[1], NT) + mm(dqkv_ref[2], w_ref[2], NT)
    if earlier:
        gf_ref[sent_of(1 - group), :] = earlier[0][...]
        gf_ref[sent, :] = part[: SENT[group]]
    else:
        gf_ref[...] = part[: SENT[group]]
    first_normed, _ = norm_parts(x_ref[mine, :].astype(F32))
    sums_ref[4:5, :] = col_sum(part * first_normed)
    sums_ref[5:6, :] = col_sum(part)
    half = qkv_ref.shape[2]
    sums_ref[3:4, :half] = col_sum(dqkv_ref[0].astype(F32))
    sums_ref[3:4, half:] = col_sum(dqkv_ref[2].astype(F32))


def mlp_part_kernel(info_ref, act0_ref, act1_ref, down_ref, out_ref):
    for group, act_ref in enumerate((act0_ref, act1_ref)):
        out_ref[sent_of(group), :] = mm(act_ref[...], down_ref[...])[: SENT[group]]


def small_end_kernel(info_ref, small_ref, other_ref, gain1, bias1, gain2, bias2, outb, qvb, upb, downb):
    total = small_ref[...]
    width = total.shape[1]
    total = jnp.concatenate([total[0:2] + other_ref[0:2, :], total[2:]], axis=0)
    for n, ref in enumerate((gain1, bias1, gain2, bias2, outb)):
        ref[...] = total[n].reshape(width)
    qvb[0:1, :] = total[5:6, : width // 2]
    qvb[1:2, :] = total[5:6, width // 2 :]
    upb[:width] = total[6].reshape(width)
    upb[width:] = total[7].reshape(width)
    downb[...] = total[8].reshape(width)


def input_kernel(info_ref, x_ref, gh0_ref, gh1_ref, gain_ref, gf_ref, gf2_ref, grad_ref):
    start = 0
    for group, gh_ref in enumerate((gh0_ref, gh1_ref)):
        length, sent = LENGTHS[group], sent_of(group)
        grad_first = gf_ref[sent, :] + gf2_ref[sent, :]
        normed, inverse = norm_parts(x_ref[of_group(group), :].astype(F32)[: SENT[group]])
        value = gh_ref[: SENT[group], :] + norm_back(grad_first, normed, inverse, row(gain_ref))
        grad_ref[start : start + length, :] = value[:length]
        start += length


def output_kernel(info_ref, h0_ref, h1_ref, m_ref, m2_ref, bias_ref, out_ref, wide):
    start = 0
    for group, h_ref in enumerate((h0_ref, h1_ref)):
        length, mine = LENGTHS[group], sent_of(group)
        value = h_ref[: SENT[group], :] + live_of(info_ref, group) * (
            m_ref[mine, :] + m2_ref[mine, :] + row(bias_ref)
        )
        wide[start : start + length, :] = value[:length]
        start += length
    out_ref[...] = wide[...].astype(BF16)


def stage_kernel(bit, count, info_ref, keep_ref, *refs):
    pieces, (send_ref, rest_ref) = refs[:count], refs[count:]
    mine = info_ref[4 + bit]
    half = keep_ref.shape[0] // 2
    at = 0
    for piece in pieces:
        cols = slice(at, at + piece.shape[1])
        at += piece.shape[1]
        low = keep_ref[:half, cols] + piece[:half, :]
        high = keep_ref[half:, cols] + piece[half:, :]
        send_ref[:, cols] = jnp.where(mine == 0, high, low)
        rest_ref[:, cols] = jnp.where(mine == 0, low, high)


def stage_both_kernel(bit, info_ref, keep1_ref, keep2_ref, got1_ref, got2_ref, send_ref, rest_ref):
    cols = keep1_ref.shape[1]
    for n, (keep_ref, got_ref) in enumerate(((keep1_ref, got1_ref), (keep2_ref, got2_ref))):
        at = pl.ds(n * cols, cols)
        stage_kernel(bit, 1, info_ref, keep_ref, got_ref, send_ref.at[:, at], rest_ref.at[:, at])


def both_end_kernel(info_ref, keep_ref, got_ref, down_ref, up_ref):
    cols = down_ref.shape[1]
    down_ref[...] = keep_ref[:, :cols] + got_ref[:, :cols]
    up_ref[...] = keep_ref[:, cols:] + got_ref[:, cols:]


def stage_small_kernel(bit, count, last, info_ref, keep_ref, small_ref, *refs):
    pieces, outs = refs[:count], refs[count:]
    rows = keep_ref.shape[0]
    parts = [pieces[0][at : at + 16, :] for at in range(rows, pieces[0].shape[0], 16)]
    small = small_ref[...] + jnp.concatenate(parts, axis=1)
    if last:
        out_ref, total_ref = outs
        total_ref[...] = small
        out_ref[...] = keep_ref[...] + pieces[0][:rows, :]
        return
    send_ref, rest_ref, total_ref = outs
    total_ref[...] = small
    mine, half, at = info_ref[4 + bit], rows // 2, 0
    for piece in pieces:
        cols = slice(at, at + piece.shape[1])
        at += piece.shape[1]
        low = keep_ref[:half, cols] + piece[:half, :]
        high = keep_ref[half:, cols] + piece[half:rows, :]
        send_ref[:half, cols] = jnp.where(mine == 0, high, low)
        rest_ref[:, cols] = jnp.where(mine == 0, low, high)
    send_ref[half:, :] = small


def last_kernel(info_ref, keep_ref, piece_ref, out_ref):
    out_ref[...] = keep_ref[...] + piece_ref[...]


def attn_last_kernel(info_ref, done1_ref, keep2_ref, got2_ref, qkv_ref, out_ref):
    span = out_ref.shape[1]
    qkv_ref[0] = done1_ref[:, :span]
    qkv_ref[1] = done1_ref[:, span:]
    qkv_ref[2] = keep2_ref[:, :span] + got2_ref[:, :span]
    out_ref[...] = keep2_ref[:, span:] + got2_ref[:, span:]


SMEM_SPEC = pl.BlockSpec(memory_space=pltpu.SMEM)
VMEM_SPEC = pl.BlockSpec(memory_space=pltpu.VMEM)
LATER = pl.BlockSpec(memory_space=pl.ANY)


def held(*shape, dtype=F32):
    return pltpu.VMEM(shape, dtype)


def shaped(*shape, dtype=F32):
    return pltpu.HBM(shape, dtype)


def in_vmem(value):
    return pltpu.with_memory_space_constraint(value, pltpu.VMEM)


def in_hbm(value):
    return pltpu.with_memory_space_constraint(value, pltpu.HBM)


class Order:
    def __init__(self, info, always):
        self.info = info
        self.always = always
        self.last = None

    def together(self, part, *watched):
        before = self.last
        states = [(v, dict(vars(v))) for v in watched]
        shapes = jax.eval_shape(part)
        self.last = before
        for value, state in states:
            vars(value).update(state)
        results = lax.cond(self.always, part, lambda: jax.tree.map(lambda v: jnp.zeros(v.shape, v.dtype), shapes))
        self.last = jax.tree.leaves(results)[0]
        return results

    def call(self, kernel, name, outs, operands, room=3, plain=False, after=(), **kwargs):
        many = isinstance(outs, (tuple, list))
        outs = tuple(outs) if many else (outs,)
        count = len(operands) + 1
        extra = [*after] if self.last is None else [*after, self.last]

        def body(*refs):
            kernel(*refs[:count], *refs[count + len(extra) :])

        results = pl.pallas_call(
            body,
            out_shape=outs,
            name=name,
            in_specs=[SMEM_SPEC] + [pl.BlockSpec() if plain else VMEM_SPEC] * (count - 1) + [LATER] * len(extra),
            out_specs=tuple(VMEM_SPEC if o.memory_space == pltpu.VMEM else pl.BlockSpec() for o in outs),
            compiler_params=pltpu.CompilerParams(vmem_limit_bytes=room * MIB),
            cost_estimate=pl.CostEstimate(flops=COST.get(name, 1), bytes_accessed=1, transcendentals=0),
            **kwargs,
        )(self.info, *map(in_hbm if plain else in_vmem, operands), *extra)
        self.last = results[0]
        return results if many else results[0]


def swap_sides(value):
    return lax.ppermute(value, "tensor", [(0, 1), (1, 0)])


def swap_bit(value, size, bit):
    return lax.ppermute(value, "dp", [(i, i ^ (1 << bit)) for i in range(size)])


class Scatter:
    def __init__(self, order, size, bits, keep, send, small=None):
        self.small = small
        self.order, self.size, self.bits, self.keep, self.level = order, size, bits, keep, 0
        self.got = [swap_bit(piece, size, 0) for piece in send]

    def stage(self, name):
        bit = self.bits[self.level]
        self.level += 1
        half = (self.keep.shape[0] // 2, self.keep.shape[1])
        if self.small is not None:
            send, self.keep, self.small = self.order.call(
                functools.partial(stage_small_kernel, bit, len(self.got), False), f"{name}_{self.level}",
                (held(half[0] + 16, half[1]), held(*half), held(16, half[1])), [self.keep, self.small, *self.got],
            )
            self.got = [swap_bit(send, self.size, bit)]
            return
        send, self.keep = self.order.call(
            functools.partial(stage_kernel, bit, len(self.got)), f"{name}_{self.level}",
            (held(*half), held(*half)), [self.keep, *self.got],
        )
        self.got = [swap_bit(send, self.size, bit)]

    def last(self, name):
        return self.order.call(last_kernel, name, shaped(*self.keep.shape), [self.keep, *self.got])


def per_device(
    dp_size,
    images_in,
    small_counts,
    large_counts,
    norm1_gain,
    norm1_bias,
    qkv_weight,
    qv_bias,
    out_weight,
    out_bias,
    norm2_gain,
    norm2_bias,
    up_weight,
    up_bias,
    down_weight,
    down_bias,
    out_cotangent,
):
    width = images_in.shape[1]
    span = out_weight.shape[0]
    units = down_weight.shape[0]
    index = lax.axis_index("dp")
    side = lax.axis_index("tensor")
    core = index & 1
    bits = dp_size.bit_length() - 1
    height = width // dp_size
    order = Order(
        jnp.stack(
            [side, core, small_counts[0], large_counts[0]] + [(index >> b) & 1 for b in range(bits)]
        ).astype(jnp.int32),
        index < dp_size,
    )

    quarter = span // 4
    near = (index >> 1) & 1
    ow_send = lax.dynamic_slice_in_dim(out_weight, (2 * core + near) * quarter, quarter, 0).astype(F32)
    ow_one = swap_sides(ow_send)

    weights = qkv_weight.transpose(1, 0, 2)
    heads = span // HEAD_DIM
    first, qkv, x_pad, ct_pad, *rest = order.call(
        forward_kernel, "attn_forward",
        (
            held(ROWS, width, dtype=BF16), held(3, ROWS, span, dtype=BF16), held(ROWS, width, dtype=BF16),
            held(ROWS, width, dtype=BF16), *(held(heads, p) for p in PADDED), *(held(p, span) for p in SENT),
        ),
        [images_in, out_cotangent, norm1_gain, norm1_bias, weights, qv_bias], room=24, plain=True,
        scratch_shapes=[pltpu.VMEM((LENGTHS[0] + PADDED[1] + 3, width), F32)],
    )
    lse, mix = rest[:2], rest[2:]
    mix2 = [swap_sides(m) for m in mix]
    ow_one = order.call(relay_kernel, "out_weight_relay", held(quarter, width), [ow_one])
    ow_two = swap_bit(ow_one, dp_size, 1)
    ow_got1 = swap_bit(ow_one, dp_size, 0)
    ow_two = order.call(relay_kernel, "out_weight_next", held(quarter, width), [ow_two])
    ow_got2 = swap_bit(ow_two, dp_size, 0)
    ow_all = order.call(
        join_kernel, "out_weight_join", held(2 * span, width, dtype=BF16),
        [out_weight, ow_one, ow_two, ow_got1, ow_got2],
    )

    mlp, gs = [None, None], []
    for group in (1, 0):
        padded = PADDED[group]
        tall = SENT[group] + sum(g.shape[0] for g in gs)
        *mlp[group], total = order.call(
            functools.partial(mlp_kernel, group, 512), "mlp_" + "ab"[group],
            (
                held(padded, width), held(padded, width, dtype=BF16), held(padded, width, dtype=BF16),
                held(padded, units, dtype=BF16), held(padded, units, dtype=BF16),
                held(1, units), held(1, width), held(tall, width),
            ),
            [
                x_pad, ct_pad, mix[group], mix2[group], ow_all, out_bias, norm2_gain, norm2_bias,
                up_weight, up_bias, down_weight, *gs,
            ],
            room=16, scratch_shapes=[pltpu.VMEM((padded, 2 * span), BF16)],
        )
        gs = [total]
    gs = gs[0]
    gs2 = swap_sides(gs)
    hidden, second, gmlp, act, gpre, upsum, downsum = zip(*mlp)

    first_x = tuple(range(1, bits))
    first_z = (2, 1) + first_x[2:]

    def weight_grads(name, bit_order, left, right, piece):
        count = units // piece
        keep, *send = order.call(
            functools.partial(weights_kernel, height, piece, bit_order), name,
            (held(width // 2, units),) + (held(width // 2, piece),) * count, [*left, *right], room=12,
            scratch_shapes=[pltpu.VMEM((width, max(PADDED)), F32)],
        )
        return Scatter(order, dp_size, bit_order, keep, send)

    mlp_box = []

    def do_mlp():
        mlp_box[:] = [order.call(mlp_part_kernel, "mlp_part", held(SENT_ROWS, width), [*act, down_weight], room=8)]
        if not OPT["relay"]:
            mlp_box.append(swap_sides(mlp_box[0]))

    if OPT["mlp"] == 0:
        do_mlp()
    orders = {k: first_z if k in OPT["z"] else first_x for k in "du12"}
    down_sum = weight_grads("down_weights", orders["d"], gmlp, act, OPT["dpiece"])
    up_sum = weight_grads("up_weights", orders["u"], second, gpre, OPT["upiece"])
    down_sum.stage("down")
    up_sum.stage("up")
    if OPT["mlp"] == 1:
        do_mlp()

    def second_stage():
        down_sum.stage("down")
        up_sum.stage("up")

    if OPT["s2"] == 0:
        second_stage()
    if OPT["mlp"] == 2:
        do_mlp()
    if OPT["relay"]:
        mlp_box[:] = [order.call(relay_kernel, "mlp_relay", held(SENT_ROWS, width), mlp_box, after=[gs2])]
        mlp_box.append(swap_sides(mlp_box[0]))
    mlp_part, mlp2 = mlp_box

    def go_back(group, *earlier):
        padded = PADDED[group]
        tall = SENT[group] + sum(e.shape[0] for e in earlier)
        return order.call(
            functools.partial(backward_kernel, group), "attn_backward_" + "ab"[group],
            (
                held(3, padded, span, dtype=BF16), held(padded, width, dtype=BF16),
                held(padded, width), held(8, width), held(tall, width),
            ),
            [
                gs, gs2, x_pad, hidden[group], ct_pad, norm2_gain, out_weight, qkv, lse[group], weights, *earlier,
            ],
            scratch_shapes=[pltpu.VMEM((padded, span), BF16)], room=16,
        )

    *back1, gf = go_back(1)
    if OPT["s2"] == 1:
        second_stage()
    *back0, gf = go_back(0, gf)
    gf2 = swap_sides(gf)
    dqkv, gattn, gh, sums = zip(back0, back1)
    if OPT["s2"] == 2:
        second_stage()
    both_box = []

    def third_stage():
        for n in range(3, bits - 1):
            down_sum.stage("down")
            up_sum.stage("up")
        half = (down_sum.keep.shape[0] // 2, 2 * units)
        both, keep_both = order.call(
            functools.partial(stage_both_kernel, first_x[-1]), "mlp_3", (held(*half), held(*half)),
            [down_sum.keep, up_sum.keep, *down_sum.got, *up_sum.got],
        )
        both_box[:] = [keep_both, swap_bit(both, dp_size, first_x[-1])]

    if OPT["s3"] == 0:
        third_stage()
    rows = width // 2
    piece = OPT["apiece"]
    keep1, keep2, small, *send = order.call(
        functools.partial(attn_weights_kernel, height, orders["1"], orders["2"]), "attn_weights",
        (
            held(rows, 2 * span), held(rows, 2 * span), held(16, width),
            held(rows + 16 * (2 * span // piece), piece), *(held(rows, piece),) * (4 * span // piece - 1),
        ),
        [first, *dqkv, *gattn, *mix, *sums, *upsum, *downsum], room=12,
        scratch_shapes=[pltpu.VMEM((width, max(PADDED)), F32)],
    )
    count = len(send) // 2
    attn1 = Scatter(order, dp_size, orders["1"], keep1, send[:count], small)
    if OPT["s3"] == 1:
        third_stage()
    attn1.stage("attn1")
    attn2 = Scatter(order, dp_size, orders["2"], keep2, send[count:])
    attn2.stage("attn2")
    if OPT["s3"] == 2:
        third_stage()

    def do_block():
        return order.call(
            output_kernel, "block_out", shaped(*images_in.shape, dtype=BF16),
            [*hidden, mlp_part, mlp2, down_bias], room=8, scratch_shapes=[pltpu.VMEM(images_in.shape, F32)],
        )

    def do_input():
        return order.call(
            input_kernel, "input_back", shaped(*images_in.shape), [x_pad, *gh, norm1_gain, gf, gf2], room=8
        )

    def do_both():
        return order.call(both_end_kernel, "mlp_end", (shaped(height, units),) * 2, both_box)

    if OPT["block"] == 0:
        block_out = do_block()

    def attn_more():
        for n in range(1, bits - 1):
            attn1.stage("attn1")
            attn2.stage("attn2")
            if n == 1 and OPT["block"] == 1:
                boxes.append(do_block())
            if n == 1 and OPT["both"] == 1:
                boxes2.append(do_both())

    boxes, boxes2 = [], []

    def attn_rest():
        attn_more()
        done1, total = order.call(
            functools.partial(stage_small_kernel, 0, 1, True), "attn1_end", (held(height, width), held(16, width)),
            [attn1.keep, attn1.small, *attn1.got],
        )
        ends = order.call(
            attn_last_kernel, "attn_end", (held(3, height, span), held(height, span)),
            [done1, attn2.keep, *attn2.got],
        )
        return (*ends, total)

    if OPT["tail"]:
        qkv_block, out_block, small = order.together(attn_rest, attn1, attn2)
    else:
        attn_more()
        if OPT["both"] == 2:
            boxes2.append(do_both())
        if OPT["input"] == 0:
            input_grad = do_input()
        done1, small = order.call(
            functools.partial(stage_small_kernel, 0, 1, True), "attn1_end", (held(height, width), held(16, width)),
            [attn1.keep, attn1.small, *attn1.got],
        )
        if OPT["block"] == 1:
            block_out = boxes[0]
    small2 = swap_sides(small)
    if OPT["block"] == 2:
        block_out = do_block()
    down_block, up_block = boxes2[0] if boxes2 else do_both()
    if OPT["tail"] or OPT["input"] == 1:
        input_grad = do_input()
    if not OPT["tail"]:
        qkv_block, out_block = order.call(
            attn_last_kernel, "attn_end", (shaped(3, height, span), shaped(height, span)),
            [done1, attn2.keep, *attn2.got],
        )
    vector = shaped(width)
    small_out = order.call(
        small_end_kernel, "small_end",
        (vector, vector, vector, vector, vector, shaped(2, span), shaped(units), vector),
        [small, small2],
    )

    return (
        block_out,
        input_grad,
        small_out[0],
        small_out[1],
        qkv_block.transpose(1, 0, 2),
        small_out[5],
        out_block.T,
        small_out[4],
        small_out[2],
        small_out[3],
        up_block,
        small_out[6],
        down_block.T,
        small_out[7],
    )


def solution(mesh):
    placed = (
        P("dp", None),
        P("dp"),
        P("dp"),
        P(),
        P(),
        P(None, None, "tensor"),
        P(None, "tensor"),
        P("tensor", None),
        P(),
        P(),
        P(),
        P(None, "tensor"),
        P("tensor"),
        P("tensor", None),
        P(),
        P("dp", None),
    )
    return jax.shard_map(
        functools.partial(per_device, mesh.shape["dp"]),
        mesh=mesh,
        in_specs=placed,
        out_specs=(
            P("dp", None),
            P("dp", None),
            P(),
            P(),
            P("dp", None, "tensor"),
            P(None, "tensor"),
            P("tensor", "dp"),
            P(),
            P(),
            P(),
            P("dp", "tensor"),
            P("tensor"),
            P("tensor", "dp"),
            P(),
        ),
        check_vma=False,
    )
```

```python
import functools

import jax
import jax.numpy as jnp
from jax import lax
from jax.experimental import pallas as pl
from jax.experimental.pallas import tpu as pltpu
from jax.sharding import PartitionSpec as P

HEAD_DIM = 64
PAIR = 2 * HEAD_DIM
LENGTHS = (197, 325)
PADDED = tuple(-(-length // 16) * 16 for length in LENGTHS)
SENT = tuple(-(-length // 8) * 8 for length in LENGTHS)
STARTS = (0, PADDED[0])
SENT_STARTS = (0, SENT[0])
ROWS = sum(PADDED)
SENT_ROWS = sum(SENT)
NORM_EPS = 1e-06
F32 = jnp.float32
BF16 = jnp.bfloat16
MIB = 1024 * 1024
COST = {"attn_backward_b": 10**11, "block_out": 10**11, "mlp_3": 7 * 10**9}
NT = ((1,), (1,))
TN = ((0,), (0,))


def norm_parts(values):
    row_mean = jnp.mean(values, axis=-1, keepdims=True)
    centered = values - row_mean
    variance = jnp.mean(centered * centered, axis=-1, keepdims=True)
    inverse = lax.rsqrt(variance + NORM_EPS)
    return (centered * inverse, inverse)


def norm_back(grad, normed, inverse, gain):
    scaled = grad * gain
    row_inner = jnp.mean(scaled, axis=-1, keepdims=True)
    row_cross = jnp.mean(scaled * normed, axis=-1, keepdims=True)
    return inverse * (scaled - row_inner - normed * row_cross)


def mm(left, right, dims=((1,), (0,))):
    return lax.dot_general(left, right, (dims, ((), ())), preferred_element_type=F32)


def col_sum(values):
    return jnp.sum(values, axis=0, keepdims=True)


def row(ref):
    return ref[...].reshape(1, -1)


def low_lanes(rows):
    return lax.broadcasted_iota(jnp.int32, (rows, PAIR), 1) < HEAD_DIM


def key_mask(padded, length):
    return lax.broadcasted_iota(jnp.int32, (padded, padded), 0) < length


def of_group(group):
    return slice(STARTS[group], STARTS[group] + PADDED[group])


def sent_of(group):
    return slice(SENT_STARTS[group], SENT_STARTS[group] + SENT[group])


def filled(rows, padded):
    return jnp.concatenate([rows, jnp.zeros((padded - rows.shape[0], rows.shape[1]), rows.dtype)], axis=0)


def live_of(info_ref, group):
    return (info_ref[2 + group] > 0).astype(F32)


def forward_kernel(
    info_ref, x_ref, ct_ref, gain_ref, bias_ref, w_ref, qvb_ref,
    first_ref, qkv_ref, xpad_ref, ctpad_ref, lse0_ref, lse1_ref, mix0_ref, mix1_ref, wide,
):
    scaling = HEAD_DIM ** (-0.5)
    for source, target in ((ct_ref, ctpad_ref), (x_ref, xpad_ref)):
        wide[: source.shape[0], :] = source[...].astype(F32)
        start = 0
        for group in range(2):
            rows, length = PADDED[group], LENGTHS[group]
            real = lax.broadcasted_iota(jnp.int32, (rows, x_ref.shape[1]), 0) < length
            piece = jnp.where(real, wide[start : start + rows, :], 0.0)
            target[of_group(group), :] = piece.astype(BF16)
            start += length
    normed, _ = norm_parts(xpad_ref[...].astype(F32))
    first = (normed * row(gain_ref) + row(bias_ref)).astype(BF16)
    first_ref[...] = first
    qkv_ref[0] = (mm(first, w_ref[0]) + qvb_ref[0:1, :]).astype(BF16)
    qkv_ref[1] = mm(first, w_ref[1]).astype(BF16)
    qkv_ref[2] = (mm(first, w_ref[2]) + qvb_ref[1:2, :]).astype(BF16)
    for group, lse_ref, mix_ref in ((0, lse0_ref, mix0_ref), (1, lse1_ref, mix1_ref)):
        rows, length = PADDED[group], LENGTHS[group]
        low = low_lanes(rows)
        keep_keys = key_mask(rows, length)
        for pair in range(qkv_ref.shape[2] // PAIR):
            lanes = slice(pair * PAIR, (pair + 1) * PAIR)
            queries, keys, values = (qkv_ref[c, of_group(group), lanes] for c in range(3))
            values_t = values.T
            mixed_t = []
            for side in range(2):
                own = low if side == 0 else jnp.logical_not(low)
                scores = mm(keys, jnp.where(own, queries, jnp.zeros_like(queries)), NT) * scaling
                scores = jnp.where(keep_keys, scores, -jnp.inf)
                top = jnp.max(scores, axis=0, keepdims=True)
                exps = jnp.exp(scores - top)
                total = jnp.sum(exps, axis=0, keepdims=True)
                soft_low = (exps / total).astype(BF16)
                mixed_t.append(mm(values_t[side * HEAD_DIM : (side + 1) * HEAD_DIM], soft_low))
                head = 2 * pair + side
                lse_ref[head : head + 1, :] = top + jnp.log(total)
            mixed = jnp.concatenate(mixed_t, axis=0).T.astype(BF16).astype(F32)
            mix_ref[:, lanes] = mixed[: SENT[group]]


def relay_kernel(info_ref, in_ref, out_ref):
    out_ref[...] = in_ref[...]


def join_kernel(info_ref, ow_ref, one_ref, two_ref, got1_ref, got2_ref, ow_all):
    side, core, near = info_ref[0], info_ref[1], info_ref[5]
    span = ow_ref.shape[0]
    quarter = span // 4
    mine, other = side * span, (1 - side) * span
    ow_all[pl.ds(pl.multiple_of(mine, span), span), :] = ow_ref[...]
    for ref, where, x in (
        (one_ref, core, near), (two_ref, core, 1 - near), (got1_ref, 1 - core, near), (got2_ref, 1 - core, 1 - near),
    ):
        at = pl.multiple_of(other + (2 * where + x) * quarter, quarter)
        ow_all[pl.ds(at, quarter), :] = ref[...].astype(BF16)


def grad_act_kernel(info_ref, ct_ref, down_ref, *refs):
    for group in range(2):
        gmlp_ref, gact_ref, downsum_ref = refs[3 * group : 3 * group + 3]
        gmlp = live_of(info_ref, group) * ct_ref[of_group(group), :].astype(F32)
        downsum_ref[...] = col_sum(gmlp)
        gmlp = gmlp.astype(BF16)
        gmlp_ref[...] = gmlp
        gact_ref[...] = mm(gmlp, down_ref[...], NT)


def mlp_kernel(
    group, chunk, info_ref, x_ref, gact_ref, mix_ref, mix2_ref, ow_ref, ob_ref, gain_ref, bias_ref,
    up_ref, upb_ref, *refs,
):
    *earlier, hidden_ref, second_ref, act_ref, gpre_ref, upsum_ref, gs_ref, mix_all = refs
    side, live = info_ref[0], live_of(info_ref, group)
    span = mix_ref.shape[1]
    for which, ref in ((side, mix_ref), (1 - side, mix2_ref)):
        at = pl.ds(pl.multiple_of(which * span, span), span)
        mix_all[:, at] = filled(ref[...], PADDED[group]).astype(BF16)
    branch = mm(mix_all[...], ow_ref[...]) + row(ob_ref)
    hidden = x_ref[of_group(group), :].astype(F32) + live * branch
    hidden_ref[...] = hidden
    normed, _ = norm_parts(hidden)
    second = (normed * row(gain_ref) + row(bias_ref)).astype(BF16)
    second_ref[...] = second
    bias = row(upb_ref)
    rows = slice(None)
    if earlier:
        gs_ref[sent_of(1 - group), :] = earlier[0][...]
        rows = sent_of(group)
    for step in range(up_ref.shape[1] // chunk):
        cols = slice(step * chunk, (step + 1) * chunk)
        pre = mm(second, up_ref[:, cols]) + bias[:, cols]
        cdf = 0.5 * (1.0 + lax.erf(pre * (0.5**0.5)))
        act_ref[:, cols] = (pre * cdf).astype(BF16)
        slope = cdf + pre * (jnp.exp(-0.5 * pre * pre) * 0.3989422804014327)
        gpre = (gact_ref[:, cols] * slope).astype(BF16)
        gpre_ref[:, cols] = gpre
        upsum_ref[:, cols] = col_sum(gpre.astype(F32))
        part = mm(gpre, up_ref[:, cols], NT)[: SENT[group]]
        gs_ref[rows, :] = part if step == 0 else gs_ref[rows, :] + part


def pick_blocks(wide, parity, height, length, order):
    count, bits = 1 << len(order), len(order)
    found = []
    for place in range(count):
        index = sum(((place >> (bits - 1 - n)) & 1) << (bit - 1) for n, bit in enumerate(order))
        even = wide[2 * index * height : (2 * index + 1) * height, :length]
        odd = wide[(2 * index + 1) * height : (2 * index + 2) * height, :length]
        found.append(jnp.where(parity == 0, even, odd))
    return jnp.concatenate(found, axis=0).astype(BF16)


def turned(core, height, order, left, wide):
    length = left.shape[0]
    wide[:, :length] = left.astype(F32).T
    return tuple(pick_blocks(wide, parity, height, length, order) for parity in (core, 1 - core))


def weights_kernel(height, piece, order, info_ref, l0_ref, l1_ref, r0_ref, r1_ref, keep_ref, *refs):
    *send_refs, wide = refs
    core = info_ref[1]
    keep0, send0 = turned(core, height, order, l0_ref[...], wide)
    keep1, send1 = turned(core, height, order, l1_ref[...], wide)
    for step, send_ref in enumerate(send_refs):
        cols = slice(step * piece, (step + 1) * piece)
        right0, right1 = r0_ref[:, cols], r1_ref[:, cols]
        send_ref[...] = mm(send0, right0) + mm(send1, right1)
        keep_ref[:, cols] = mm(keep0, right0) + mm(keep1, right1)


def attn_weights_kernel(
    height, order, info_ref, first_ref, dqkv0_ref, dqkv1_ref, ga0_ref, ga1_ref, mix0_ref, mix1_ref,
    s0_ref, s1_ref, u0_ref, u1_ref, d0_ref, d1_ref,
    keep1_ref, keep2_ref, small_ref, send1_ref, send2_ref, wide,
):
    core = info_ref[1]
    rows, span = keep1_ref.shape[0], mix0_ref.shape[1]
    both = s0_ref[...] + s1_ref[...]
    up = u0_ref[...] + u1_ref[...]
    width = small_ref.shape[1]
    small_ref[...] = jnp.zeros_like(small_ref)
    small_ref[0:2, :] = both[4:6]
    small_ref[2:6, :] = both[0:4]
    small_ref[6:7, :] = up[:, :width]
    small_ref[7:8, :] = up[:, width:]
    small_ref[8:9, :] = d0_ref[...] + d1_ref[...]
    send1_ref[rows:, :] = small_ref[...]
    left = [turned(core, height, order, first_ref[of_group(g), :], wide) for g in range(2)]
    for part in range(4):
        if part < 3:
            right = [r[part] for r in (dqkv0_ref, dqkv1_ref)]
        else:
            left = [turned(core, height, order, r[...], wide) for r in (ga0_ref, ga1_ref)]
            right = [filled(r[...], p).astype(BF16) for r, p in zip((mix0_ref, mix1_ref), PADDED)]
        keep_ref, send_ref = ((keep1_ref, send1_ref), (keep2_ref, send2_ref))[part // 2]
        cols = slice(part % 2 * span, (part % 2 + 1) * span)
        send_ref[:rows, cols] = mm(left[0][1], right[0]) + mm(left[1][1], right[1])
        keep_ref[:, cols] = mm(left[0][0], right[0]) + mm(left[1][0], right[1])


def again_kernel(
    info_ref, qkv_ref, lse0_ref, lse1_ref, hidden0_ref, hidden1_ref, x_ref,
    soft0_ref, soft1_ref, normed0_ref, normed1_ref, inverse0_ref, inverse1_ref, first_ref,
):
    scaling = HEAD_DIM ** (-0.5)
    first_ref[...] = norm_parts(x_ref[...].astype(F32))[0]
    for group, lse_ref, hidden_ref, soft_ref, normed_ref, inverse_ref in (
        (0, lse0_ref, hidden0_ref, soft0_ref, normed0_ref, inverse0_ref),
        (1, lse1_ref, hidden1_ref, soft1_ref, normed1_ref, inverse1_ref),
    ):
        normed_ref[...], inverse_ref[...] = norm_parts(hidden_ref[...])
        rows, mine = PADDED[group], of_group(group)
        low = low_lanes(rows)
        keep_keys = key_mask(rows, LENGTHS[group])
        for head in range(soft_ref.shape[0]):
            lanes = slice(head // 2 * PAIR, (head // 2 + 1) * PAIR)
            own = low if head % 2 == 0 else jnp.logical_not(low)
            queries = qkv_ref[0, mine, lanes]
            queries = jnp.where(own, queries, jnp.zeros_like(queries))
            scores = mm(qkv_ref[1, mine, lanes], queries, NT) * scaling
            soft_ref[head] = jnp.where(keep_keys, jnp.exp(scores - lse_ref[head : head + 1, :]), 0.0)


def backward_kernel(
    group, info_ref, gs_ref, gs2_ref, first_ref, normed_ref, inverse_ref, ct_ref, gain_ref, ow_ref, qkv_ref,
    soft_ref, w_ref,
    *refs,
):
    *earlier, dqkv_ref, gattn_ref, gh_ref, sums_ref, gf_ref, gmix = refs
    scaling = HEAD_DIM ** (-0.5)
    rows = PADDED[group]
    mine = of_group(group)
    live = live_of(info_ref, group)
    sent = sent_of(group)
    grad_second = filled(gs_ref[sent, :] + gs2_ref[sent, :], rows)
    normed, inverse = normed_ref[...], inverse_ref[...]
    grad_hidden = ct_ref[mine, :].astype(F32) + norm_back(grad_second, normed, inverse, row(gain_ref))
    gh_ref[...] = grad_hidden
    sums_ref[0:1, :] = col_sum(grad_second * normed)
    sums_ref[1:2, :] = col_sum(grad_second)
    gattn = (live * grad_hidden).astype(BF16)
    gattn_ref[...] = gattn
    sums_ref[2:3, :] = col_sum(gattn.astype(F32))
    gmix[...] = mm(gattn, ow_ref[...], NT).astype(BF16)
    low = low_lanes(rows)
    for pair in range(qkv_ref.shape[2] // PAIR):
        lanes = slice(pair * PAIR, (pair + 1) * PAIR)
        queries, keys, values = (qkv_ref[c, mine, lanes] for c in range(3))
        grads = gmix[:, lanes]
        keys_t = keys.T
        zero = jnp.zeros_like(queries)
        dq_t, dk, dv = [], [], []
        for side in range(2):
            own = low if side == 0 else jnp.logical_not(low)
            head = 2 * pair + side
            soft = soft_ref[head]
            grad_soft = mm(values, jnp.where(own, grads, zero), NT)
            inner = jnp.sum(grad_soft * soft, axis=0, keepdims=True)
            grad_scores = (soft * (grad_soft - inner)).astype(BF16)
            dv.append(mm(soft.astype(BF16), grads))
            dk.append(mm(grad_scores, queries))
            dq_t.append(mm(keys_t[side * HEAD_DIM : (side + 1) * HEAD_DIM], grad_scores))
        dqkv_ref[0, :, lanes] = (jnp.concatenate(dq_t, axis=0).T * scaling).astype(BF16)
        dqkv_ref[1, :, lanes] = (jnp.where(low, dk[0], dk[1]) * scaling).astype(BF16)
        dqkv_ref[2, :, lanes] = jnp.where(low, dv[0], dv[1]).astype(BF16)
    part = mm(dqkv_ref[0], w_ref[0], NT) + mm(dqkv_ref[1], w_ref[1], NT) + mm(dqkv_ref[2], w_ref[2], NT)
    if earlier:
        gf_ref[sent_of(1 - group), :] = earlier[0][...]
        gf_ref[sent, :] = part[: SENT[group]]
    else:
        gf_ref[...] = part[: SENT[group]]
    first_normed = first_ref[mine, :]
    sums_ref[4:5, :] = col_sum(part * first_normed)
    sums_ref[5:6, :] = col_sum(part)
    half = qkv_ref.shape[2]
    sums_ref[3:4, :half] = col_sum(dqkv_ref[0].astype(F32))
    sums_ref[3:4, half:] = col_sum(dqkv_ref[2].astype(F32))


def mlp_part_kernel(info_ref, act0_ref, act1_ref, down_ref, out_ref):
    for group, act_ref in enumerate((act0_ref, act1_ref)):
        out_ref[sent_of(group), :] = mm(act_ref[...], down_ref[...])[: SENT[group]]


def small_end_kernel(info_ref, small_ref, other_ref, gain1, bias1, gain2, bias2, outb, qvb, upb, downb):
    total = small_ref[...]
    width = total.shape[1]
    total = jnp.concatenate([total[0:2] + other_ref[0:2, :], total[2:]], axis=0)
    for n, ref in enumerate((gain1, bias1, gain2, bias2, outb)):
        ref[...] = total[n].reshape(width)
    qvb[0:1, :] = total[5:6, : width // 2]
    qvb[1:2, :] = total[5:6, width // 2 :]
    upb[:width] = total[6].reshape(width)
    upb[width:] = total[7].reshape(width)
    downb[...] = total[8].reshape(width)


def input_kernel(info_ref, x_ref, gh0_ref, gh1_ref, gain_ref, gf_ref, gf2_ref, grad_ref):
    start = 0
    for group, gh_ref in enumerate((gh0_ref, gh1_ref)):
        length, sent = LENGTHS[group], sent_of(group)
        grad_first = gf_ref[sent, :] + gf2_ref[sent, :]
        normed, inverse = norm_parts(x_ref[of_group(group), :].astype(F32)[: SENT[group]])
        value = gh_ref[: SENT[group], :] + norm_back(grad_first, normed, inverse, row(gain_ref))
        grad_ref[start : start + length, :] = value[:length]
        start += length


def output_kernel(info_ref, h0_ref, h1_ref, m_ref, m2_ref, bias_ref, out_ref, wide):
    start = 0
    for group, h_ref in enumerate((h0_ref, h1_ref)):
        length, mine = LENGTHS[group], sent_of(group)
        value = h_ref[: SENT[group], :] + live_of(info_ref, group) * (
            m_ref[mine, :] + m2_ref[mine, :] + row(bias_ref)
        )
        wide[start : start + length, :] = value[:length]
        start += length
    out_ref[...] = wide[...].astype(BF16)


def stage_kernel(bit, count, info_ref, keep_ref, *refs):
    pieces, (send_ref, rest_ref) = refs[:count], refs[count:]
    mine = info_ref[4 + bit]
    half = keep_ref.shape[0] // 2
    at = 0
    for piece in pieces:
        cols = slice(at, at + piece.shape[1])
        at += piece.shape[1]
        low = keep_ref[:half, cols] + piece[:half, :]
        high = keep_ref[half:, cols] + piece[half:, :]
        send_ref[:, cols] = jnp.where(mine == 0, high, low)
        rest_ref[:, cols] = jnp.where(mine == 0, low, high)


def stage_both_kernel(bit, info_ref, keep1_ref, keep2_ref, got1_ref, got2_ref, send_ref, rest_ref):
    cols = keep1_ref.shape[1]
    for n, (keep_ref, got_ref) in enumerate(((keep1_ref, got1_ref), (keep2_ref, got2_ref))):
        at = pl.ds(n * cols, cols)
        stage_kernel(bit, 1, info_ref, keep_ref, got_ref, send_ref.at[:, at], rest_ref.at[:, at])


def both_end_kernel(info_ref, keep_ref, got_ref, down_ref, up_ref):
    cols = down_ref.shape[1]
    down_ref[...] = keep_ref[:, :cols] + got_ref[:, :cols]
    up_ref[...] = keep_ref[:, cols:] + got_ref[:, cols:]


def stage_small_kernel(bit, info_ref, keep_ref, small_ref, piece_ref, send_ref, rest_ref, total_ref):
    rows = keep_ref.shape[0]
    mine, half = info_ref[4 + bit], rows // 2
    total = small_ref[...] + piece_ref[rows:, :]
    total_ref[...] = total
    low = keep_ref[:half, :] + piece_ref[:half, :]
    high = keep_ref[half:, :] + piece_ref[half:rows, :]
    send_ref[:half, :] = jnp.where(mine == 0, high, low)
    send_ref[half:, :] = total
    rest_ref[...] = jnp.where(mine == 0, low, high)


def attn_done_kernel(info_ref, keep_ref, small_ref, piece_ref, out_ref, total_ref):
    rows = keep_ref.shape[0]
    out_ref[...] = keep_ref[...] + piece_ref[:rows, :]
    total_ref[...] = small_ref[...] + piece_ref[rows:, :]


def attn_last_kernel(info_ref, done1_ref, keep2_ref, got2_ref, qkv_ref, out_ref):
    span = out_ref.shape[1]
    qkv_ref[0] = done1_ref[:, :span]
    qkv_ref[1] = done1_ref[:, span:]
    qkv_ref[2] = keep2_ref[:, :span] + got2_ref[:, :span]
    out_ref[...] = keep2_ref[:, span:] + got2_ref[:, span:]


SMEM_SPEC = pl.BlockSpec(memory_space=pltpu.SMEM)
VMEM_SPEC = pl.BlockSpec(memory_space=pltpu.VMEM)
LATER = pl.BlockSpec(memory_space=pl.ANY)


def held(*shape, dtype=F32):
    return pltpu.VMEM(shape, dtype)


def shaped(*shape, dtype=F32):
    return pltpu.HBM(shape, dtype)


def in_vmem(value):
    return pltpu.with_memory_space_constraint(value, pltpu.VMEM)


def in_hbm(value):
    return pltpu.with_memory_space_constraint(value, pltpu.HBM)


class Order:
    def __init__(self, info):
        self.info = info
        self.last = None

    def call(self, kernel, name, outs, operands, room=3, plain=False, **kwargs):
        many = isinstance(outs, (tuple, list))
        outs = tuple(outs) if many else (outs,)
        count = len(operands) + 1
        extra = [] if self.last is None else [self.last]

        def body(*refs):
            kernel(*refs[:count], *refs[count + len(extra) :])

        results = pl.pallas_call(
            body,
            out_shape=outs,
            name=name,
            in_specs=[SMEM_SPEC] + [pl.BlockSpec() if plain else VMEM_SPEC] * (count - 1) + [LATER] * len(extra),
            out_specs=tuple(VMEM_SPEC if o.memory_space == pltpu.VMEM else pl.BlockSpec() for o in outs),
            compiler_params=pltpu.CompilerParams(vmem_limit_bytes=room * MIB),
            cost_estimate=pl.CostEstimate(flops=COST.get(name, 1), bytes_accessed=1, transcendentals=0),
            **kwargs,
        )(self.info, *map(in_hbm if plain else in_vmem, operands), *extra)
        self.last = results[0]
        return results if many else results[0]


def swap_sides(value):
    return lax.ppermute(value, "tensor", [(0, 1), (1, 0)])


def swap_bit(value, size, bit):
    return lax.ppermute(value, "dp", [(i, i ^ (1 << bit)) for i in range(size)])


class Scatter:
    def __init__(self, order, size, bits, keep, send, small=None):
        self.small = small
        self.order, self.size, self.bits, self.keep, self.level = order, size, bits, keep, 0
        self.got = [swap_bit(piece, size, 0) for piece in send]

    def stage(self, name):
        bit = self.bits[self.level]
        self.level += 1
        half = (self.keep.shape[0] // 2, self.keep.shape[1])
        if self.small is not None:
            send, self.keep, self.small = self.order.call(
                functools.partial(stage_small_kernel, bit), f"{name}_{self.level}",
                (held(half[0] + 16, half[1]), held(*half), held(16, half[1])), [self.keep, self.small, *self.got],
            )
            self.got = [swap_bit(send, self.size, bit)]
            return
        send, self.keep = self.order.call(
            functools.partial(stage_kernel, bit, len(self.got)), f"{name}_{self.level}",
            (held(*half), held(*half)), [self.keep, *self.got],
        )
        self.got = [swap_bit(send, self.size, bit)]


def per_device(
    dp_size,
    images_in,
    small_counts,
    large_counts,
    norm1_gain,
    norm1_bias,
    qkv_weight,
    qv_bias,
    out_weight,
    out_bias,
    norm2_gain,
    norm2_bias,
    up_weight,
    up_bias,
    down_weight,
    down_bias,
    out_cotangent,
):
    width = images_in.shape[1]
    span = out_weight.shape[0]
    units = down_weight.shape[0]
    index = lax.axis_index("dp")
    side = lax.axis_index("tensor")
    core = index & 1
    bits = dp_size.bit_length() - 1
    height = width // dp_size
    order = Order(
        jnp.stack(
            [side, core, small_counts[0], large_counts[0]] + [(index >> b) & 1 for b in range(bits)]
        ).astype(jnp.int32)
    )

    quarter = span // 4
    near = (index >> 1) & 1
    ow_send = lax.dynamic_slice_in_dim(out_weight, (2 * core + near) * quarter, quarter, 0).astype(F32)
    ow_one = swap_sides(ow_send)

    weights = qkv_weight.transpose(1, 0, 2)
    heads = span // HEAD_DIM
    first, qkv, x_pad, ct_pad, *rest = order.call(
        forward_kernel, "attn_forward",
        (
            held(ROWS, width, dtype=BF16), held(3, ROWS, span, dtype=BF16), held(ROWS, width, dtype=BF16),
            held(ROWS, width, dtype=BF16), *(held(heads, p) for p in PADDED), *(held(p, span) for p in SENT),
        ),
        [images_in, out_cotangent, norm1_gain, norm1_bias, weights, qv_bias], room=24, plain=True,
        scratch_shapes=[pltpu.VMEM((LENGTHS[0] + PADDED[1] + 3, width), F32)],
    )
    lse, mix = rest[:2], rest[2:]
    mix2 = [swap_sides(m) for m in mix]
    ow_one = order.call(relay_kernel, "out_weight_relay", held(quarter, width), [ow_one])
    ow_two = swap_bit(ow_one, dp_size, 1)
    ow_got1 = swap_bit(ow_one, dp_size, 0)
    ow_two = order.call(relay_kernel, "out_weight_next", held(quarter, width), [ow_two])
    ow_got2 = swap_bit(ow_two, dp_size, 0)
    ow_all = order.call(
        join_kernel, "out_weight_join", held(2 * span, width, dtype=BF16),
        [out_weight, ow_one, ow_two, ow_got1, ow_got2],
    )

    early = order.call(
        grad_act_kernel, "grad_act",
        tuple(
            spec
            for p in PADDED
            for spec in (held(p, width, dtype=BF16), held(p, units), held(1, width))
        ),
        [ct_pad, down_weight], room=8,
    )
    gmlp, gact, downsum = (early[i::3] for i in range(3))
    mlp, gs = [None, None], []
    for group in (1, 0):
        padded = PADDED[group]
        tall = SENT[group] + sum(g.shape[0] for g in gs)
        *mlp[group], total = order.call(
            functools.partial(mlp_kernel, group, 512), "mlp_" + "ab"[group],
            (
                held(padded, width), held(padded, width, dtype=BF16),
                held(padded, units, dtype=BF16), held(padded, units, dtype=BF16),
                held(1, units), held(tall, width),
            ),
            [
                x_pad, gact[group], mix[group], mix2[group], ow_all, out_bias, norm2_gain, norm2_bias,
                up_weight, up_bias, *gs,
            ],
            room=16, scratch_shapes=[pltpu.VMEM((padded, 2 * span), BF16)],
        )
        gs = [total]
    gs = gs[0]
    gs2 = swap_sides(gs)
    hidden, second, act, gpre, upsum = zip(*mlp)

    first_x = tuple(range(1, bits))
    first_z = (2, 1) + first_x[2:]

    def weight_grads(name, bit_order, left, right, piece):
        count = units // piece
        keep, *send = order.call(
            functools.partial(weights_kernel, height, piece, bit_order), name,
            (held(width // 2, units),) + (held(width // 2, piece),) * count, [*left, *right], room=12,
            scratch_shapes=[pltpu.VMEM((width, max(PADDED)), F32)],
        )
        return Scatter(order, dp_size, bit_order, keep, send)

    down_sum = weight_grads("down_weights", first_x, gmlp, act, units // 2)
    up_sum = weight_grads("up_weights", first_z, second, gpre, units // 2)
    down_sum.stage("down")
    up_sum.stage("up")
    mlp_part = order.call(mlp_part_kernel, "mlp_part", held(SENT_ROWS, width), [*act, down_weight], room=8)
    mlp2 = swap_sides(mlp_part)

    again = order.call(
        again_kernel, "attn_again",
        (
            *(held(heads, p, p) for p in PADDED), *(held(p, width) for p in PADDED), *(held(p, 1) for p in PADDED),
            held(ROWS, width),
        ),
        [qkv, *lse, *hidden, x_pad], room=8,
    )
    soft, normed, inverse, first_normed = again[:2], again[2:4], again[4:6], again[6]

    def go_back(group, *earlier):
        padded = PADDED[group]
        tall = SENT[group] + sum(e.shape[0] for e in earlier)
        return order.call(
            functools.partial(backward_kernel, group), "attn_backward_" + "ab"[group],
            (
                held(3, padded, span, dtype=BF16), held(padded, width, dtype=BF16),
                held(padded, width), held(8, width), held(tall, width),
            ),
            [
                gs, gs2, first_normed, normed[group], inverse[group], ct_pad, norm2_gain, out_weight, qkv, soft[group],
                weights, *earlier,
            ],
            scratch_shapes=[pltpu.VMEM((padded, span), BF16)], room=16,
        )

    *back1, gf = go_back(1)
    down_sum.stage("down")
    up_sum.stage("up")
    *back0, gf = go_back(0, gf)
    gf2 = swap_sides(gf)
    dqkv, gattn, gh, sums = zip(back0, back1)

    for n in range(3, bits - 1):
        down_sum.stage("down")
        up_sum.stage("up")
    rows = width // 2
    keep1, keep2, small, *send = order.call(
        functools.partial(attn_weights_kernel, height, first_x), "attn_weights",
        (
            held(rows, 2 * span), held(rows, 2 * span), held(16, width),
            held(rows + 16, 2 * span), held(rows, 2 * span),
        ),
        [first, *dqkv, *gattn, *mix, *sums, *upsum, *downsum], room=12,
        scratch_shapes=[pltpu.VMEM((width, max(PADDED)), F32)],
    )
    attn1 = Scatter(order, dp_size, first_x, keep1, send[:1], small)
    half = (down_sum.keep.shape[0] // 2, 2 * units)
    both, keep_both = order.call(
        functools.partial(stage_both_kernel, first_x[-1]), "mlp_3", (held(*half), held(*half)),
        [down_sum.keep, up_sum.keep, *down_sum.got, *up_sum.got],
    )
    got_both = swap_bit(both, dp_size, first_x[-1])
    attn1.stage("attn1")
    attn2 = Scatter(order, dp_size, first_x, keep2, send[1:])
    attn2.stage("attn2")
    block_out = order.call(
        output_kernel, "block_out", shaped(*images_in.shape, dtype=BF16),
        [*hidden, mlp_part, mlp2, down_bias], room=8, scratch_shapes=[pltpu.VMEM(images_in.shape, F32)],
    )
    for _ in range(1, bits - 1):
        attn1.stage("attn1")
        attn2.stage("attn2")
    down_block, up_block = order.call(
        both_end_kernel, "mlp_end", (shaped(height, units),) * 2, [keep_both, got_both]
    )
    input_grad = order.call(
        input_kernel, "input_back", shaped(*images_in.shape), [x_pad, *gh, norm1_gain, gf, gf2], room=8
    )
    done1, small = order.call(
        attn_done_kernel, "attn1_end", (held(height, width), held(16, width)),
        [attn1.keep, attn1.small, *attn1.got],
    )
    small2 = swap_sides(small)
    qkv_block, out_block = order.call(
        attn_last_kernel, "attn_end", (shaped(3, height, span), shaped(height, span)),
        [done1, attn2.keep, *attn2.got],
    )
    vector = shaped(width)
    small_out = order.call(
        small_end_kernel, "small_end",
        (vector, vector, vector, vector, vector, shaped(2, span), shaped(units), vector),
        [small, small2],
    )

    return (
        block_out,
        input_grad,
        small_out[0],
        small_out[1],
        qkv_block.transpose(1, 0, 2),
        small_out[5],
        out_block.T,
        small_out[4],
        small_out[2],
        small_out[3],
        up_block,
        small_out[6],
        down_block.T,
        small_out[7],
    )


def solution(mesh):
    placed = (
        P("dp", None),
        P("dp"),
        P("dp"),
        P(),
        P(),
        P(None, None, "tensor"),
        P(None, "tensor"),
        P("tensor", None),
        P(),
        P(),
        P(),
        P(None, "tensor"),
        P("tensor"),
        P("tensor", None),
        P(),
        P("dp", None),
    )
    return jax.shard_map(
        functools.partial(per_device, mesh.shape["dp"]),
        mesh=mesh,
        in_specs=placed,
        out_specs=(
            P("dp", None),
            P("dp", None),
            P(),
            P(),
            P("dp", None, "tensor"),
            P(None, "tensor"),
            P("tensor", "dp"),
            P(),
            P(),
            P(),
            P("dp", "tensor"),
            P("tensor"),
            P("tensor", "dp"),
            P(),
        ),
        check_vma=False,
    )
```

```python
import functools

import jax
import jax.numpy as jnp
from jax import lax
from jax.experimental import pallas as pl
from jax.experimental.pallas import tpu as pltpu
from jax.sharding import PartitionSpec as P

HEAD_DIM = 64
PAIR = 2 * HEAD_DIM
LENGTHS = (197, 325)
PADDED = tuple(-(-length // 16) * 16 for length in LENGTHS)
SENT = tuple(-(-length // 8) * 8 for length in LENGTHS)
STARTS = (0, PADDED[0])
SENT_STARTS = (0, SENT[0])
ROWS = sum(PADDED)
SENT_ROWS = sum(SENT)
NORM_EPS = 1e-06
F32 = jnp.float32
BF16 = jnp.bfloat16
MIB = 1024 * 1024
COST = {"attn_backward_b": 9 * 10**9, "block_out": 10**11, "mlp_3": 7 * 10**9}
NT = ((1,), (1,))
TN = ((0,), (0,))


def norm_parts(values):
    row_mean = jnp.mean(values, axis=-1, keepdims=True)
    centered = values - row_mean
    variance = jnp.mean(centered * centered, axis=-1, keepdims=True)
    inverse = lax.rsqrt(variance + NORM_EPS)
    return (centered * inverse, inverse)


def norm_back(grad, normed, inverse, gain):
    scaled = grad * gain
    row_inner = jnp.mean(scaled, axis=-1, keepdims=True)
    row_cross = jnp.mean(scaled * normed, axis=-1, keepdims=True)
    return inverse * (scaled - row_inner - normed * row_cross)


def mm(left, right, dims=((1,), (0,))):
    return lax.dot_general(left, right, (dims, ((), ())), preferred_element_type=F32)


def col_sum(values):
    return jnp.sum(values, axis=0, keepdims=True)


def row(ref):
    return ref[...].reshape(1, -1)


def low_lanes(rows):
    return lax.broadcasted_iota(jnp.int32, (rows, PAIR), 1) < HEAD_DIM


def key_mask(padded, length):
    return lax.broadcasted_iota(jnp.int32, (padded, padded), 0) < length


def of_group(group):
    return slice(STARTS[group], STARTS[group] + PADDED[group])


def sent_of(group):
    return slice(SENT_STARTS[group], SENT_STARTS[group] + SENT[group])


def filled(rows, padded):
    return jnp.concatenate([rows, jnp.zeros((padded - rows.shape[0], rows.shape[1]), rows.dtype)], axis=0)


def live_of(info_ref, group):
    return (info_ref[2 + group] > 0).astype(F32)


def forward_kernel(
    info_ref, x_ref, ct_ref, gain_ref, bias_ref, w_ref, qvb_ref,
    first_ref, qkv_ref, xpad_ref, ctpad_ref, lse0_ref, lse1_ref, mix0_ref, mix1_ref, wide,
):
    scaling = HEAD_DIM ** (-0.5)
    for source, target in ((ct_ref, ctpad_ref), (x_ref, xpad_ref)):
        wide[: source.shape[0], :] = source[...].astype(F32)
        start = 0
        for group in range(2):
            rows, length = PADDED[group], LENGTHS[group]
            real = lax.broadcasted_iota(jnp.int32, (rows, x_ref.shape[1]), 0) < length
            piece = jnp.where(real, wide[start : start + rows, :], 0.0)
            target[of_group(group), :] = piece.astype(BF16)
            start += length
    normed, _ = norm_parts(xpad_ref[...].astype(F32))
    first = (normed * row(gain_ref) + row(bias_ref)).astype(BF16)
    first_ref[...] = first
    qkv_ref[0] = (mm(first, w_ref[0]) + qvb_ref[0:1, :]).astype(BF16)
    qkv_ref[1] = mm(first, w_ref[1]).astype(BF16)
    qkv_ref[2] = (mm(first, w_ref[2]) + qvb_ref[1:2, :]).astype(BF16)
    for group, lse_ref, mix_ref in ((0, lse0_ref, mix0_ref), (1, lse1_ref, mix1_ref)):
        rows, length = PADDED[group], LENGTHS[group]
        low = low_lanes(rows)
        keep_keys = key_mask(rows, length)
        for pair in range(qkv_ref.shape[2] // PAIR):
            lanes = slice(pair * PAIR, (pair + 1) * PAIR)
            queries, keys, values = (qkv_ref[c, of_group(group), lanes] for c in range(3))
            values_t = values.T
            mixed_t = []
            for side in range(2):
                own = low if side == 0 else jnp.logical_not(low)
                scores = mm(keys, jnp.where(own, queries, jnp.zeros_like(queries)), NT) * scaling
                scores = jnp.where(keep_keys, scores, -jnp.inf)
                top = jnp.max(scores, axis=0, keepdims=True)
                exps = jnp.exp(scores - top)
                total = jnp.sum(exps, axis=0, keepdims=True)
                soft_low = (exps / total).astype(BF16)
                mixed_t.append(mm(values_t[side * HEAD_DIM : (side + 1) * HEAD_DIM], soft_low))
                head = 2 * pair + side
                lse_ref[head : head + 1, :] = top + jnp.log(total)
            mixed = jnp.concatenate(mixed_t, axis=0).T.astype(BF16).astype(F32)
            mix_ref[:, lanes] = mixed[: SENT[group]]


def relay_kernel(info_ref, in_ref, out_ref, *halves):
    out_ref[...] = in_ref[...]
    for n, ref in enumerate(halves):
        ref[...] = in_ref[:, n * ref.shape[1] : (n + 1) * ref.shape[1]]


def next_kernel(info_ref, in1_ref, in2_ref, out1_ref, out2_ref):
    out1_ref[...] = in1_ref[...]
    out2_ref[...] = in2_ref[...]


def join_kernel(info_ref, ow_ref, one_ref, two1_ref, two2_ref, got_ref, got1_ref, got2_ref, ow_all):
    side, core, near = info_ref[0], info_ref[1], info_ref[5]
    span, width = ow_ref.shape
    quarter = span // 4
    mine, other = side * span, (1 - side) * span
    ow_all[pl.ds(pl.multiple_of(mine, span), span), :] = ow_ref[...]
    for refs, where, x in (
        ((one_ref,), core, near), ((two1_ref, two2_ref), core, 1 - near),
        ((got_ref,), 1 - core, near), ((got1_ref, got2_ref), 1 - core, 1 - near),
    ):
        at = pl.multiple_of(other + (2 * where + x) * quarter, quarter)
        for n, ref in enumerate(refs):
            cols = ref.shape[1]
            ow_all[pl.ds(at, quarter), n * cols : (n + 1) * cols] = ref[...].astype(BF16)


def grad_act_kernel(info_ref, ct_ref, down_ref, *refs):
    for group in range(2):
        gmlp_ref, gact_ref, downsum_ref = refs[3 * group : 3 * group + 3]
        gmlp = live_of(info_ref, group) * ct_ref[of_group(group), :].astype(F32)
        downsum_ref[...] = col_sum(gmlp)
        gmlp = gmlp.astype(BF16)
        gmlp_ref[...] = gmlp
        gact_ref[...] = mm(gmlp, down_ref[...], NT)


def mlp_kernel(
    group, chunk, info_ref, x_ref, gact_ref, mix_ref, mix2_ref, ow_ref, ob_ref, gain_ref, bias_ref,
    up_ref, upb_ref, *refs,
):
    *earlier, hidden_ref, second_ref, act_ref, gpre_ref, upsum_ref, gs_ref, mix_all = refs
    side, live = info_ref[0], live_of(info_ref, group)
    span = mix_ref.shape[1]
    for which, ref in ((side, mix_ref), (1 - side, mix2_ref)):
        at = pl.ds(pl.multiple_of(which * span, span), span)
        mix_all[:, at] = filled(ref[...], PADDED[group]).astype(BF16)
    branch = mm(mix_all[...], ow_ref[...]) + row(ob_ref)
    hidden = x_ref[of_group(group), :].astype(F32) + live * branch
    hidden_ref[...] = hidden
    normed, _ = norm_parts(hidden)
    second = (normed * row(gain_ref) + row(bias_ref)).astype(BF16)
    second_ref[...] = second
    bias = row(upb_ref)
    rows = slice(None)
    if earlier:
        gs_ref[sent_of(1 - group), :] = earlier[0][...]
        rows = sent_of(group)
    for step in range(up_ref.shape[1] // chunk):
        cols = slice(step * chunk, (step + 1) * chunk)
        pre = mm(second, up_ref[:, cols]) + bias[:, cols]
        cdf = 0.5 * (1.0 + lax.erf(pre * (0.5**0.5)))
        act_ref[:, cols] = (pre * cdf).astype(BF16)
        slope = cdf + pre * (jnp.exp(-0.5 * pre * pre) * 0.3989422804014327)
        gpre = (gact_ref[:, cols] * slope).astype(BF16)
        gpre_ref[:, cols] = gpre
        upsum_ref[:, cols] = col_sum(gpre.astype(F32))
        part = mm(gpre, up_ref[:, cols], NT)[: SENT[group]]
        gs_ref[rows, :] = part if step == 0 else gs_ref[rows, :] + part


def pick_blocks(wide, parity, height, length, order):
    count, bits = 1 << len(order), len(order)
    found = []
    for place in range(count):
        index = sum(((place >> (bits - 1 - n)) & 1) << (bit - 1) for n, bit in enumerate(order))
        even = wide[2 * index * height : (2 * index + 1) * height, :length]
        odd = wide[(2 * index + 1) * height : (2 * index + 2) * height, :length]
        found.append(jnp.where(parity == 0, even, odd))
    return jnp.concatenate(found, axis=0).astype(BF16)


def turned(core, height, order, left, wide):
    length = left.shape[0]
    wide[:, :length] = left.astype(F32).T
    return tuple(pick_blocks(wide, parity, height, length, order) for parity in (core, 1 - core))


def weights_kernel(height, piece, order, info_ref, l0_ref, l1_ref, r0_ref, r1_ref, keep_ref, *refs):
    *send_refs, wide = refs
    core = info_ref[1]
    keep0, send0 = turned(core, height, order, l0_ref[...], wide)
    keep1, send1 = turned(core, height, order, l1_ref[...], wide)
    for step, send_ref in enumerate(send_refs):
        cols = slice(step * piece, (step + 1) * piece)
        right0, right1 = r0_ref[:, cols], r1_ref[:, cols]
        send_ref[...] = mm(send0, right0) + mm(send1, right1)
        keep_ref[:, cols] = mm(keep0, right0) + mm(keep1, right1)


def attn_weights_kernel(
    height, order, info_ref, first_ref, dqkv0_ref, dqkv1_ref, ga0_ref, ga1_ref, mix0_ref, mix1_ref,
    s0_ref, s1_ref, u0_ref, u1_ref, d0_ref, d1_ref,
    keep1_ref, keep2_ref, small_ref, send1_ref, send2_ref, wide,
):
    core = info_ref[1]
    rows, span = keep1_ref.shape[0], mix0_ref.shape[1]
    both = s0_ref[...] + s1_ref[...]
    up = u0_ref[...] + u1_ref[...]
    width = small_ref.shape[1]
    small_ref[...] = jnp.zeros_like(small_ref)
    small_ref[0:2, :] = both[4:6]
    small_ref[2:6, :] = both[0:4]
    small_ref[6:7, :] = up[:, :width]
    small_ref[7:8, :] = up[:, width:]
    small_ref[8:9, :] = d0_ref[...] + d1_ref[...]
    send1_ref[rows:, :] = small_ref[...]
    left = [turned(core, height, order, first_ref[of_group(g), :], wide) for g in range(2)]
    for part in range(4):
        if part < 3:
            right = [r[part] for r in (dqkv0_ref, dqkv1_ref)]
        else:
            left = [turned(core, height, order, r[...], wide) for r in (ga0_ref, ga1_ref)]
            right = [filled(r[...], p).astype(BF16) for r, p in zip((mix0_ref, mix1_ref), PADDED)]
        keep_ref, send_ref = ((keep1_ref, send1_ref), (keep2_ref, send2_ref))[part // 2]
        cols = slice(part % 2 * span, (part % 2 + 1) * span)
        send_ref[:rows, cols] = mm(left[0][1], right[0]) + mm(left[1][1], right[1])
        keep_ref[:, cols] = mm(left[0][0], right[0]) + mm(left[1][0], right[1])


def again_kernel(
    info_ref, qkv_ref, lse0_ref, lse1_ref, hidden0_ref, hidden1_ref, x_ref,
    soft0_ref, soft1_ref, normed0_ref, normed1_ref, inverse0_ref, inverse1_ref, first_ref,
    first_inverse_ref,
):
    scaling = HEAD_DIM ** (-0.5)
    first_ref[...], first_inverse_ref[...] = norm_parts(x_ref[...].astype(F32))
    for group, lse_ref, hidden_ref, soft_ref, normed_ref, inverse_ref in (
        (0, lse0_ref, hidden0_ref, soft0_ref, normed0_ref, inverse0_ref),
        (1, lse1_ref, hidden1_ref, soft1_ref, normed1_ref, inverse1_ref),
    ):
        normed_ref[...], inverse_ref[...] = norm_parts(hidden_ref[...])
        rows, mine = PADDED[group], of_group(group)
        low = low_lanes(rows)
        keep_keys = key_mask(rows, LENGTHS[group])
        for head in range(soft_ref.shape[0]):
            lanes = slice(head // 2 * PAIR, (head // 2 + 1) * PAIR)
            own = low if head % 2 == 0 else jnp.logical_not(low)
            queries = qkv_ref[0, mine, lanes]
            queries = jnp.where(own, queries, jnp.zeros_like(queries))
            scores = mm(qkv_ref[1, mine, lanes], queries, NT) * scaling
            soft_ref[head] = jnp.where(keep_keys, jnp.exp(scores - lse_ref[head : head + 1, :]), 0.0)


def backward_kernel(
    group, info_ref, gs_ref, gs2_ref, first_ref, normed_ref, inverse_ref, ct_ref, gain_ref, ow_ref, qkv_ref,
    soft_ref, w_ref,
    *refs,
):
    *earlier, dqkv_ref, gattn_ref, gh_ref, sums_ref, gf_ref, gmix = refs
    scaling = HEAD_DIM ** (-0.5)
    rows = PADDED[group]
    mine = of_group(group)
    live = live_of(info_ref, group)
    sent = sent_of(group)
    grad_second = filled(gs_ref[sent, :] + gs2_ref[sent, :], rows)
    normed, inverse = normed_ref[...], inverse_ref[...]
    grad_hidden = ct_ref[mine, :].astype(F32) + norm_back(grad_second, normed, inverse, row(gain_ref))
    gh_ref[...] = grad_hidden
    sums_ref[0:1, :] = col_sum(grad_second * normed)
    sums_ref[1:2, :] = col_sum(grad_second)
    gattn = (live * grad_hidden).astype(BF16)
    gattn_ref[...] = gattn
    sums_ref[2:3, :] = col_sum(gattn.astype(F32))
    gmix[...] = mm(gattn, ow_ref[...], NT).astype(BF16)
    low = low_lanes(rows)
    for pair in range(qkv_ref.shape[2] // PAIR):
        lanes = slice(pair * PAIR, (pair + 1) * PAIR)
        queries, keys, values = (qkv_ref[c, mine, lanes] for c in range(3))
        grads = gmix[:, lanes]
        keys_t = keys.T
        zero = jnp.zeros_like(queries)
        dq_t, dk, dv = [], [], []
        for side in range(2):
            own = low if side == 0 else jnp.logical_not(low)
            head = 2 * pair + side
            soft = soft_ref[head]
            grad_soft = mm(values, jnp.where(own, grads, zero), NT)
            inner = jnp.sum(grad_soft * soft, axis=0, keepdims=True)
            grad_scores = (soft * (grad_soft - inner)).astype(BF16)
            dv.append(mm(soft.astype(BF16), grads))
            dk.append(mm(grad_scores, queries))
            dq_t.append(mm(keys_t[side * HEAD_DIM : (side + 1) * HEAD_DIM], grad_scores))
        dqkv_ref[0, :, lanes] = (jnp.concatenate(dq_t, axis=0).T * scaling).astype(BF16)
        dqkv_ref[1, :, lanes] = (jnp.where(low, dk[0], dk[1]) * scaling).astype(BF16)
        dqkv_ref[2, :, lanes] = jnp.where(low, dv[0], dv[1]).astype(BF16)
    part = mm(dqkv_ref[0], w_ref[0], NT) + mm(dqkv_ref[1], w_ref[1], NT) + mm(dqkv_ref[2], w_ref[2], NT)
    if earlier:
        gf_ref[sent_of(1 - group), :] = earlier[0][...]
        gf_ref[sent, :] = part[: SENT[group]]
    else:
        gf_ref[...] = part[: SENT[group]]
    first_normed = first_ref[mine, :]
    sums_ref[4:5, :] = col_sum(part * first_normed)
    sums_ref[5:6, :] = col_sum(part)
    half = qkv_ref.shape[2]
    sums_ref[3:4, :half] = col_sum(dqkv_ref[0].astype(F32))
    sums_ref[3:4, half:] = col_sum(dqkv_ref[2].astype(F32))


def mlp_part_kernel(info_ref, act0_ref, act1_ref, down_ref, out_ref):
    for group, act_ref in enumerate((act0_ref, act1_ref)):
        out_ref[sent_of(group), :] = mm(act_ref[...], down_ref[...])[: SENT[group]]


def small_end_kernel(info_ref, small_ref, gain2, bias2, outb, qvb, upb, downb):
    total = small_ref[...]
    width = total.shape[1]
    for n, ref in enumerate((gain2, bias2, outb)):
        ref[...] = total[2 + n].reshape(width)
    qvb[0:1, :] = total[5:6, : width // 2]
    qvb[1:2, :] = total[5:6, width // 2 :]
    upb[:width] = total[6].reshape(width)
    upb[width:] = total[7].reshape(width)
    downb[...] = total[8].reshape(width)


def norm1_end_kernel(info_ref, small_ref, other_ref, gain1, bias1):
    for n, ref in enumerate((gain1, bias1)):
        ref[...] = (small_ref[n] + other_ref[n]).reshape(small_ref.shape[1])


def input_kernel(info_ref, first_ref, inverse_ref, gh0_ref, gh1_ref, gain_ref, gf_ref, gf2_ref, grad_ref):
    start = 0
    for group, gh_ref in enumerate((gh0_ref, gh1_ref)):
        length, sent = LENGTHS[group], sent_of(group)
        grad_first = gf_ref[sent, :] + gf2_ref[sent, :]
        mine = slice(STARTS[group], STARTS[group] + SENT[group])
        normed, inverse = first_ref[mine, :], inverse_ref[mine, :]
        value = gh_ref[: SENT[group], :] + norm_back(grad_first, normed, inverse, row(gain_ref))
        grad_ref[start : start + length, :] = value[:length]
        start += length


def output_kernel(info_ref, h0_ref, h1_ref, m_ref, m2_ref, bias_ref, out_ref, wide):
    start = 0
    for group, h_ref in enumerate((h0_ref, h1_ref)):
        length, mine = LENGTHS[group], sent_of(group)
        value = h_ref[: SENT[group], :] + live_of(info_ref, group) * (
            m_ref[mine, :] + m2_ref[mine, :] + row(bias_ref)
        )
        wide[start : start + length, :] = value[:length]
        start += length
    out_ref[...] = wide[...].astype(BF16)


def stage_kernel(bit, count, info_ref, keep_ref, *refs):
    pieces, (send_ref, rest_ref) = refs[:count], refs[count:]
    mine = info_ref[4 + bit]
    half = keep_ref.shape[0] // 2
    at = 0
    for piece in pieces:
        cols = slice(at, at + piece.shape[1])
        at += piece.shape[1]
        low = keep_ref[:half, cols] + piece[:half, :]
        high = keep_ref[half:, cols] + piece[half:, :]
        send_ref[:, cols] = jnp.where(mine == 0, high, low)
        rest_ref[:, cols] = jnp.where(mine == 0, low, high)


def stage_both_kernel(bit, info_ref, keep1_ref, keep2_ref, got1_ref, got2_ref, send_ref, rest_ref):
    cols = keep1_ref.shape[1]
    for n, (keep_ref, got_ref) in enumerate(((keep1_ref, got1_ref), (keep2_ref, got2_ref))):
        at = pl.ds(n * cols, cols)
        stage_kernel(bit, 1, info_ref, keep_ref, got_ref, send_ref.at[:, at], rest_ref.at[:, at])


def both_end_kernel(info_ref, keep_ref, got_ref, down_ref, up_ref):
    cols = down_ref.shape[1]
    down_ref[...] = keep_ref[:, :cols] + got_ref[:, :cols]
    up_ref[...] = keep_ref[:, cols:] + got_ref[:, cols:]


def stage_small_kernel(bit, info_ref, keep_ref, small_ref, piece_ref, send_ref, rest_ref, total_ref):
    rows = keep_ref.shape[0]
    mine, half = info_ref[4 + bit], rows // 2
    total = small_ref[...] + piece_ref[rows:, :]
    total_ref[...] = total
    low = keep_ref[:half, :] + piece_ref[:half, :]
    high = keep_ref[half:, :] + piece_ref[half:rows, :]
    send_ref[:half, :] = jnp.where(mine == 0, high, low)
    send_ref[half:, :] = total
    rest_ref[...] = jnp.where(mine == 0, low, high)


def attn_done_kernel(info_ref, keep_ref, small_ref, piece_ref, out_ref, total_ref):
    rows = keep_ref.shape[0]
    out_ref[...] = keep_ref[...] + piece_ref[:rows, :]
    total_ref[...] = small_ref[...] + piece_ref[rows:, :]


def attn_last_kernel(info_ref, done1_ref, keep2_ref, got2_ref, qkv_ref, out_ref):
    span = out_ref.shape[1]
    qkv_ref[0] = done1_ref[:, :span]
    qkv_ref[1] = done1_ref[:, span:]
    qkv_ref[2] = keep2_ref[:, :span] + got2_ref[:, :span]
    out_ref[...] = keep2_ref[:, span:] + got2_ref[:, span:]


SMEM_SPEC = pl.BlockSpec(memory_space=pltpu.SMEM)
VMEM_SPEC = pl.BlockSpec(memory_space=pltpu.VMEM)
LATER = pl.BlockSpec(memory_space=pl.ANY)


def held(*shape, dtype=F32):
    return pltpu.VMEM(shape, dtype)


def shaped(*shape, dtype=F32):
    return pltpu.HBM(shape, dtype)


def in_vmem(value):
    return pltpu.with_memory_space_constraint(value, pltpu.VMEM)


def in_hbm(value):
    return pltpu.with_memory_space_constraint(value, pltpu.HBM)


class Order:
    def __init__(self, info):
        self.info = info
        self.last = None

    def call(self, kernel, name, outs, operands, room=3, plain=False, **kwargs):
        many = isinstance(outs, (tuple, list))
        outs = tuple(outs) if many else (outs,)
        count = len(operands) + 1
        extra = [] if self.last is None else [self.last]

        def body(*refs):
            kernel(*refs[:count], *refs[count + len(extra) :])

        results = pl.pallas_call(
            body,
            out_shape=outs,
            name=name,
            in_specs=[SMEM_SPEC] + [pl.BlockSpec() if plain else VMEM_SPEC] * (count - 1) + [LATER] * len(extra),
            out_specs=tuple(VMEM_SPEC if o.memory_space == pltpu.VMEM else pl.BlockSpec() for o in outs),
            compiler_params=pltpu.CompilerParams(vmem_limit_bytes=room * MIB),
            cost_estimate=pl.CostEstimate(flops=COST.get(name, 1), bytes_accessed=1, transcendentals=0),
            **kwargs,
        )(self.info, *map(in_hbm if plain else in_vmem, operands), *extra)
        self.last = results[0]
        return results if many else results[0]


def swap_sides(value):
    return lax.ppermute(value, "tensor", [(0, 1), (1, 0)])


def swap_bit(value, size, bit):
    return lax.ppermute(value, "dp", [(i, i ^ (1 << bit)) for i in range(size)])


class Scatter:
    def __init__(self, order, size, bits, keep, send, small=None):
        self.small = small
        self.order, self.size, self.bits, self.keep, self.level = order, size, bits, keep, 0
        self.got = [swap_bit(piece, size, 0) for piece in send]

    def stage(self, name):
        bit = self.bits[self.level]
        self.level += 1
        half = (self.keep.shape[0] // 2, self.keep.shape[1])
        if self.small is not None:
            send, self.keep, self.small = self.order.call(
                functools.partial(stage_small_kernel, bit), f"{name}_{self.level}",
                (held(half[0] + 16, half[1]), held(*half), held(16, half[1])), [self.keep, self.small, *self.got],
            )
            self.got = [swap_bit(send, self.size, bit)]
            return
        send, self.keep = self.order.call(
            functools.partial(stage_kernel, bit, len(self.got)), f"{name}_{self.level}",
            (held(*half), held(*half)), [self.keep, *self.got],
        )
        self.got = [swap_bit(send, self.size, bit)]


def per_device(
    dp_size,
    images_in,
    small_counts,
    large_counts,
    norm1_gain,
    norm1_bias,
    qkv_weight,
    qv_bias,
    out_weight,
    out_bias,
    norm2_gain,
    norm2_bias,
    up_weight,
    up_bias,
    down_weight,
    down_bias,
    out_cotangent,
):
    width = images_in.shape[1]
    span = out_weight.shape[0]
    units = down_weight.shape[0]
    index = lax.axis_index("dp")
    side = lax.axis_index("tensor")
    core = index & 1
    bits = dp_size.bit_length() - 1
    height = width // dp_size
    order = Order(
        jnp.stack(
            [side, core, small_counts[0], large_counts[0]] + [(index >> b) & 1 for b in range(bits)]
        ).astype(jnp.int32)
    )

    quarter = span // 4
    near = (index >> 1) & 1
    ow_send = lax.dynamic_slice_in_dim(out_weight, (2 * core + near) * quarter, quarter, 0).astype(F32)
    ow_one = swap_sides(ow_send)

    weights = qkv_weight.transpose(1, 0, 2)
    heads = span // HEAD_DIM
    first, qkv, x_pad, ct_pad, *rest = order.call(
        forward_kernel, "attn_forward",
        (
            held(ROWS, width, dtype=BF16), held(3, ROWS, span, dtype=BF16), held(ROWS, width, dtype=BF16),
            held(ROWS, width, dtype=BF16), *(held(heads, p) for p in PADDED), *(held(p, span) for p in SENT),
        ),
        [images_in, out_cotangent, norm1_gain, norm1_bias, weights, qv_bias], room=24, plain=True,
        scratch_shapes=[pltpu.VMEM((LENGTHS[0] + PADDED[1] + 3, width), F32)],
    )
    lse, mix = rest[:2], rest[2:]
    mix2 = [swap_sides(m) for m in mix]
    ow_one, *halves = order.call(
        relay_kernel, "out_weight_relay",
        (held(quarter, width), held(quarter, width // 2), held(quarter, width // 2)), [ow_one],
    )
    ow_two = [swap_bit(v, dp_size, 1) for v in halves]
    ow_got1 = swap_bit(ow_one, dp_size, 0)
    early = order.call(
        grad_act_kernel, "grad_act",
        tuple(
            spec
            for p in PADDED
            for spec in (held(p, width, dtype=BF16), held(p, units), held(1, width))
        ),
        [ct_pad, down_weight], room=8,
    )
    gmlp, gact, downsum = (early[i::3] for i in range(3))
    ow_two = order.call(next_kernel, "out_weight_next", (held(quarter, width // 2),) * 2, ow_two)
    ow_got2 = [swap_bit(v, dp_size, 0) for v in ow_two]
    ow_all = order.call(
        join_kernel, "out_weight_join", held(2 * span, width, dtype=BF16),
        [out_weight, ow_one, *ow_two, ow_got1, *ow_got2],
    )

    mlp, gs = [None, None], []
    for group in (1, 0):
        padded = PADDED[group]
        tall = SENT[group] + sum(g.shape[0] for g in gs)
        *mlp[group], total = order.call(
            functools.partial(mlp_kernel, group, 512), "mlp_" + "ab"[group],
            (
                held(padded, width), held(padded, width, dtype=BF16),
                held(padded, units, dtype=BF16), held(padded, units, dtype=BF16),
                held(1, units), held(tall, width),
            ),
            [
                x_pad, gact[group], mix[group], mix2[group], ow_all, out_bias, norm2_gain, norm2_bias,
                up_weight, up_bias, *gs,
            ],
            room=16, scratch_shapes=[pltpu.VMEM((padded, 2 * span), BF16)],
        )
        gs = [total]
    gs = gs[0]
    gs2 = swap_sides(gs)
    hidden, second, act, gpre, upsum = zip(*mlp)

    first_x = tuple(range(1, bits))
    first_z = (2, 1) + first_x[2:]

    def weight_grads(name, bit_order, left, right, piece):
        count = units // piece
        keep, *send = order.call(
            functools.partial(weights_kernel, height, piece, bit_order), name,
            (held(width // 2, units),) + (held(width // 2, piece),) * count, [*left, *right], room=12,
            scratch_shapes=[pltpu.VMEM((width, max(PADDED)), F32)],
        )
        return Scatter(order, dp_size, bit_order, keep, send)

    down_sum = weight_grads("down_weights", first_x, gmlp, act, units // 2)
    up_sum = weight_grads("up_weights", first_z, second, gpre, units // 2)
    down_sum.stage("down")
    up_sum.stage("up")
    mlp_part = order.call(mlp_part_kernel, "mlp_part", held(SENT_ROWS, width), [*act, down_weight], room=8)
    mlp2 = swap_sides(mlp_part)

    again = order.call(
        again_kernel, "attn_again",
        (
            *(held(heads, p, p) for p in PADDED), *(held(p, width) for p in PADDED), *(held(p, 1) for p in PADDED),
            held(ROWS, width), held(ROWS, 1),
        ),
        [qkv, *lse, *hidden, x_pad], room=8,
    )
    soft, normed, inverse, first_normed = again[:2], again[2:4], again[4:6], again[6]
    first_inverse = again[7]

    def go_back(group, *earlier):
        padded = PADDED[group]
        tall = SENT[group] + sum(e.shape[0] for e in earlier)
        return order.call(
            functools.partial(backward_kernel, group), "attn_backward_" + "ab"[group],
            (
                held(3, padded, span, dtype=BF16), held(padded, width, dtype=BF16),
                held(padded, width), held(8, width), held(tall, width),
            ),
            [
                gs, gs2, first_normed, normed[group], inverse[group], ct_pad, norm2_gain, out_weight, qkv, soft[group],
                weights, *earlier,
            ],
            scratch_shapes=[pltpu.VMEM((padded, span), BF16)], room=16,
        )

    *back1, gf = go_back(1)
    down_sum.stage("down")
    up_sum.stage("up")
    *back0, gf = go_back(0, gf)
    gf2 = swap_sides(gf)
    dqkv, gattn, gh, sums = zip(back0, back1)

    for n in range(3, bits - 1):
        down_sum.stage("down")
        up_sum.stage("up")
    rows = width // 2
    keep1, keep2, small, *send = order.call(
        functools.partial(attn_weights_kernel, height, first_x), "attn_weights",
        (
            held(rows, 2 * span), held(rows, 2 * span), held(16, width),
            held(rows + 16, 2 * span), held(rows, 2 * span),
        ),
        [first, *dqkv, *gattn, *mix, *sums, *upsum, *downsum], room=12,
        scratch_shapes=[pltpu.VMEM((width, max(PADDED)), F32)],
    )
    attn1 = Scatter(order, dp_size, first_x, keep1, send[:1], small)
    half = (down_sum.keep.shape[0] // 2, 2 * units)
    both, keep_both = order.call(
        functools.partial(stage_both_kernel, first_x[-1]), "mlp_3", (held(*half), held(*half)),
        [down_sum.keep, up_sum.keep, *down_sum.got, *up_sum.got],
    )
    got_both = swap_bit(both, dp_size, first_x[-1])
    attn1.stage("attn1")
    attn2 = Scatter(order, dp_size, first_x, keep2, send[1:])
    attn2.stage("attn2")
    block_out = order.call(
        output_kernel, "block_out", shaped(*images_in.shape, dtype=BF16),
        [*hidden, mlp_part, mlp2, down_bias], room=8, scratch_shapes=[pltpu.VMEM(images_in.shape, F32)],
    )
    for _ in range(1, bits - 1):
        attn1.stage("attn1")
        attn2.stage("attn2")
    down_block, up_block = order.call(
        both_end_kernel, "mlp_end", (shaped(height, units),) * 2, [keep_both, got_both]
    )
    input_grad = order.call(
        input_kernel, "input_back", shaped(*images_in.shape), [first_normed, first_inverse, *gh, norm1_gain, gf, gf2], room=8
    )
    done1, small = order.call(
        attn_done_kernel, "attn1_end", (held(height, width), held(16, width)),
        [attn1.keep, attn1.small, *attn1.got],
    )
    small2 = swap_sides(small)
    qkv_block, out_block = order.call(
        attn_last_kernel, "attn_end", (shaped(3, height, span), shaped(height, span)),
        [done1, attn2.keep, *attn2.got],
    )
    vector = shaped(width)
    small_out = order.call(
        small_end_kernel, "small_end", (vector, vector, vector, shaped(2, span), shaped(units), vector), [small]
    )
    norm1_out = order.call(norm1_end_kernel, "norm1_end", (vector, vector), [small, small2])

    return (
        block_out,
        input_grad,
        *norm1_out,
        qkv_block.transpose(1, 0, 2),
        small_out[3],
        out_block.T,
        small_out[2],
        small_out[0],
        small_out[1],
        up_block,
        small_out[4],
        down_block.T,
        small_out[5],
    )


def solution(mesh):
    placed = (
        P("dp", None),
        P("dp"),
        P("dp"),
        P(),
        P(),
        P(None, None, "tensor"),
        P(None, "tensor"),
        P("tensor", None),
        P(),
        P(),
        P(),
        P(None, "tensor"),
        P("tensor"),
        P("tensor", None),
        P(),
        P("dp", None),
    )
    return jax.shard_map(
        functools.partial(per_device, mesh.shape["dp"]),
        mesh=mesh,
        in_specs=placed,
        out_specs=(
            P("dp", None),
            P("dp", None),
            P(),
            P(),
            P("dp", None, "tensor"),
            P(None, "tensor"),
            P("tensor", "dp"),
            P(),
            P(),
            P(),
            P("dp", "tensor"),
            P("tensor"),
            P("tensor", "dp"),
            P(),
        ),
        check_vma=False,
    )
```

```python
import functools

import jax
import jax.numpy as jnp
from jax import lax
from jax.experimental import pallas as pl
from jax.experimental.pallas import tpu as pltpu
from jax.sharding import PartitionSpec as P

HEAD_DIM = 64
PAIR = 2 * HEAD_DIM
LENGTHS = (197, 325)
PADDED = tuple(-(-length // 16) * 16 for length in LENGTHS)
SENT = tuple(-(-length // 8) * 8 for length in LENGTHS)
STARTS = (0, PADDED[0])
SENT_STARTS = (0, SENT[0])
ROWS = sum(PADDED)
SENT_ROWS = sum(SENT)
NORM_EPS = 1e-06
F32 = jnp.float32
BF16 = jnp.bfloat16
MIB = 1024 * 1024
COST = {"attn_backward_b": 9 * 10**9, "block_out": 10**11, "mlp_3": 7 * 10**9}
NT = ((1,), (1,))
TN = ((0,), (0,))


def norm_parts(values):
    row_mean = jnp.mean(values, axis=-1, keepdims=True)
    centered = values - row_mean
    variance = jnp.mean(centered * centered, axis=-1, keepdims=True)
    inverse = lax.rsqrt(variance + NORM_EPS)
    return (centered * inverse, inverse)


def norm_back(grad, normed, inverse, gain):
    scaled = grad * gain
    row_inner = jnp.mean(scaled, axis=-1, keepdims=True)
    row_cross = jnp.mean(scaled * normed, axis=-1, keepdims=True)
    return inverse * (scaled - row_inner - normed * row_cross)


def mm(left, right, dims=((1,), (0,))):
    return lax.dot_general(left, right, (dims, ((), ())), preferred_element_type=F32)


def col_sum(values):
    return jnp.sum(values, axis=0, keepdims=True)


def row(ref):
    return ref[...].reshape(1, -1)


def low_lanes(rows):
    return lax.broadcasted_iota(jnp.int32, (rows, PAIR), 1) < HEAD_DIM


def key_mask(padded, length):
    return lax.broadcasted_iota(jnp.int32, (padded, padded), 0) < length


def of_group(group):
    return slice(STARTS[group], STARTS[group] + PADDED[group])


def sent_of(group):
    return slice(SENT_STARTS[group], SENT_STARTS[group] + SENT[group])


def filled(rows, padded):
    return jnp.concatenate([rows, jnp.zeros((padded - rows.shape[0], rows.shape[1]), rows.dtype)], axis=0)


def live_of(info_ref, group):
    return (info_ref[2 + group] > 0).astype(F32)


def forward_kernel(
    info_ref, x_ref, ct_ref, gain_ref, bias_ref, w_ref, qvb_ref,
    first_ref, qkv_ref, xpad_ref, ctpad_ref, lse0_ref, lse1_ref, mix0_ref, mix1_ref, wide,
):
    scaling = HEAD_DIM ** (-0.5)
    for source, target in ((ct_ref, ctpad_ref), (x_ref, xpad_ref)):
        wide[: source.shape[0], :] = source[...].astype(F32)
        start = 0
        for group in range(2):
            rows, length = PADDED[group], LENGTHS[group]
            real = lax.broadcasted_iota(jnp.int32, (rows, x_ref.shape[1]), 0) < length
            piece = jnp.where(real, wide[start : start + rows, :], 0.0)
            target[of_group(group), :] = piece.astype(BF16)
            start += length
    normed, _ = norm_parts(xpad_ref[...].astype(F32))
    first = (normed * row(gain_ref) + row(bias_ref)).astype(BF16)
    first_ref[...] = first
    qkv_ref[0] = (mm(first, w_ref[0]) + qvb_ref[0:1, :]).astype(BF16)
    qkv_ref[1] = mm(first, w_ref[1]).astype(BF16)
    qkv_ref[2] = (mm(first, w_ref[2]) + qvb_ref[1:2, :]).astype(BF16)
    for group, lse_ref, mix_ref in ((0, lse0_ref, mix0_ref), (1, lse1_ref, mix1_ref)):
        rows, length = PADDED[group], LENGTHS[group]
        low = low_lanes(rows)
        keep_keys = key_mask(rows, length)
        for pair in range(qkv_ref.shape[2] // PAIR):
            lanes = slice(pair * PAIR, (pair + 1) * PAIR)
            queries, keys, values = (qkv_ref[c, of_group(group), lanes] for c in range(3))
            values_t = values.T
            mixed_t = []
            for side in range(2):
                own = low if side == 0 else jnp.logical_not(low)
                scores = mm(keys, jnp.where(own, queries, jnp.zeros_like(queries)), NT) * scaling
                scores = jnp.where(keep_keys, scores, -jnp.inf)
                top = jnp.max(scores, axis=0, keepdims=True)
                exps = jnp.exp(scores - top)
                total = jnp.sum(exps, axis=0, keepdims=True)
                soft_low = (exps / total).astype(BF16)
                mixed_t.append(mm(values_t[side * HEAD_DIM : (side + 1) * HEAD_DIM], soft_low))
                head = 2 * pair + side
                lse_ref[head : head + 1, :] = top + jnp.log(total)
            mixed = jnp.concatenate(mixed_t, axis=0).T.astype(BF16).astype(F32)
            mix_ref[:, lanes] = mixed[: SENT[group]]


def relay_kernel(info_ref, in_ref, out_ref, *halves):
    out_ref[...] = in_ref[...]
    for n, ref in enumerate(halves):
        ref[...] = in_ref[:, n * ref.shape[1] : (n + 1) * ref.shape[1]]


def next_kernel(info_ref, in1_ref, in2_ref, out1_ref, out2_ref):
    out1_ref[...] = in1_ref[...]
    out2_ref[...] = in2_ref[...]


def join_kernel(info_ref, ow_ref, one_ref, two1_ref, two2_ref, got_ref, got1_ref, got2_ref, ow_all):
    side, core, near = info_ref[0], info_ref[1], info_ref[5]
    span, width = ow_ref.shape
    quarter = span // 4
    mine, other = side * span, (1 - side) * span
    ow_all[pl.ds(pl.multiple_of(mine, span), span), :] = ow_ref[...]
    for refs, where, x in (
        ((one_ref,), core, near), ((two1_ref, two2_ref), core, 1 - near),
        ((got_ref,), 1 - core, near), ((got1_ref, got2_ref), 1 - core, 1 - near),
    ):
        at = pl.multiple_of(other + (2 * where + x) * quarter, quarter)
        for n, ref in enumerate(refs):
            cols = ref.shape[1]
            ow_all[pl.ds(at, quarter), n * cols : (n + 1) * cols] = ref[...].astype(BF16)


def grad_act_kernel(info_ref, ct_ref, down_ref, *refs):
    for group in range(2):
        gmlp_ref, gact_ref, downsum_ref = refs[3 * group : 3 * group + 3]
        gmlp = live_of(info_ref, group) * ct_ref[of_group(group), :].astype(F32)
        downsum_ref[...] = col_sum(gmlp)
        gmlp = gmlp.astype(BF16)
        gmlp_ref[...] = gmlp
        gact_ref[...] = mm(gmlp, down_ref[...], NT)


def mlp_kernel(
    group, chunk, info_ref, x_ref, gact_ref, mix_ref, mix2_ref, ow_ref, ob_ref, gain_ref, bias_ref,
    up_ref, upb_ref, *refs,
):
    *earlier, hidden_ref, second_ref, act_ref, gpre_ref, upsum_ref, gs_ref, mix_all = refs
    side, live = info_ref[0], live_of(info_ref, group)
    span = mix_ref.shape[1]
    for which, ref in ((side, mix_ref), (1 - side, mix2_ref)):
        at = pl.ds(pl.multiple_of(which * span, span), span)
        mix_all[:, at] = filled(ref[...], PADDED[group]).astype(BF16)
    branch = mm(mix_all[...], ow_ref[...]) + row(ob_ref)
    hidden = x_ref[of_group(group), :].astype(F32) + live * branch
    hidden_ref[...] = hidden
    normed, _ = norm_parts(hidden)
    second = (normed * row(gain_ref) + row(bias_ref)).astype(BF16)
    second_ref[...] = second
    bias = row(upb_ref)
    rows = slice(None)
    if earlier:
        gs_ref[sent_of(1 - group), :] = earlier[0][...]
        rows = sent_of(group)
    for step in range(up_ref.shape[1] // chunk):
        cols = slice(step * chunk, (step + 1) * chunk)
        pre = mm(second, up_ref[:, cols]) + bias[:, cols]
        cdf = 0.5 * (1.0 + lax.erf(pre * (0.5**0.5)))
        act_ref[:, cols] = (pre * cdf).astype(BF16)
        slope = cdf + pre * (jnp.exp(-0.5 * pre * pre) * 0.3989422804014327)
        gpre = (gact_ref[:, cols] * slope).astype(BF16)
        gpre_ref[:, cols] = gpre
        upsum_ref[:, cols] = col_sum(gpre.astype(F32))
        part = mm(gpre, up_ref[:, cols], NT)[: SENT[group]]
        gs_ref[rows, :] = part if step == 0 else gs_ref[rows, :] + part


def pick_blocks(wide, parity, height, length, order):
    count, bits = 1 << len(order), len(order)
    found = []
    for place in range(count):
        index = sum(((place >> (bits - 1 - n)) & 1) << (bit - 1) for n, bit in enumerate(order))
        even = wide[2 * index * height : (2 * index + 1) * height, :length]
        odd = wide[(2 * index + 1) * height : (2 * index + 2) * height, :length]
        found.append(jnp.where(parity == 0, even, odd))
    return jnp.concatenate(found, axis=0).astype(BF16)


def turned(core, height, order, left, wide):
    length = left.shape[0]
    wide[:, :length] = left.astype(F32).T
    return tuple(pick_blocks(wide, parity, height, length, order) for parity in (core, 1 - core))


def weights_kernel(height, piece, order, info_ref, l0_ref, l1_ref, r0_ref, r1_ref, keep_ref, *refs):
    *send_refs, wide = refs
    core = info_ref[1]
    keep0, send0 = turned(core, height, order, l0_ref[...], wide)
    keep1, send1 = turned(core, height, order, l1_ref[...], wide)
    for step, send_ref in enumerate(send_refs):
        cols = slice(step * piece, (step + 1) * piece)
        right0, right1 = r0_ref[:, cols], r1_ref[:, cols]
        send_ref[...] = mm(send0, right0) + mm(send1, right1)
        keep_ref[:, cols] = mm(keep0, right0) + mm(keep1, right1)


def attn_weights_kernel(
    height, order, info_ref, first_ref, dqkv0_ref, dqkv1_ref, ga0_ref, ga1_ref, mix0_ref, mix1_ref,
    s0_ref, s1_ref, u0_ref, u1_ref, d0_ref, d1_ref,
    keep1_ref, keep2_ref, small_ref, send1_ref, send2_ref, wide,
):
    core = info_ref[1]
    rows, span = keep1_ref.shape[0], mix0_ref.shape[1]
    both = s0_ref[...] + s1_ref[...]
    up = u0_ref[...] + u1_ref[...]
    width = small_ref.shape[1]
    small_ref[...] = jnp.zeros_like(small_ref)
    small_ref[0:2, :] = both[4:6]
    small_ref[2:6, :] = both[0:4]
    small_ref[6:7, :] = up[:, :width]
    small_ref[7:8, :] = up[:, width:]
    small_ref[8:9, :] = d0_ref[...] + d1_ref[...]
    send1_ref[rows:, :] = small_ref[...]
    left = [turned(core, height, order, first_ref[of_group(g), :], wide) for g in range(2)]
    for part in range(4):
        if part < 3:
            right = [r[part] for r in (dqkv0_ref, dqkv1_ref)]
        else:
            left = [turned(core, height, order, r[...], wide) for r in (ga0_ref, ga1_ref)]
            right = [filled(r[...], p).astype(BF16) for r, p in zip((mix0_ref, mix1_ref), PADDED)]
        keep_ref, send_ref = ((keep1_ref, send1_ref), (keep2_ref, send2_ref))[part // 2]
        cols = slice(part % 2 * span, (part % 2 + 1) * span)
        send_ref[:rows, cols] = mm(left[0][1], right[0]) + mm(left[1][1], right[1])
        keep_ref[:, cols] = mm(left[0][0], right[0]) + mm(left[1][0], right[1])


def again_kernel(
    info_ref, qkv_ref, lse0_ref, lse1_ref, hidden0_ref, hidden1_ref, x_ref,
    soft0_ref, soft1_ref, normed0_ref, normed1_ref, inverse0_ref, inverse1_ref, first_ref,
    first_inverse_ref,
):
    scaling = HEAD_DIM ** (-0.5)
    first_ref[...], first_inverse_ref[...] = norm_parts(x_ref[...].astype(F32))
    for group, lse_ref, hidden_ref, soft_ref, normed_ref, inverse_ref in (
        (0, lse0_ref, hidden0_ref, soft0_ref, normed0_ref, inverse0_ref),
        (1, lse1_ref, hidden1_ref, soft1_ref, normed1_ref, inverse1_ref),
    ):
        normed_ref[...], inverse_ref[...] = norm_parts(hidden_ref[...])
        rows, mine = PADDED[group], of_group(group)
        low = low_lanes(rows)
        keep_keys = key_mask(rows, LENGTHS[group])
        for head in range(soft_ref.shape[0]):
            lanes = slice(head // 2 * PAIR, (head // 2 + 1) * PAIR)
            own = low if head % 2 == 0 else jnp.logical_not(low)
            queries = qkv_ref[0, mine, lanes]
            queries = jnp.where(own, queries, jnp.zeros_like(queries))
            scores = mm(qkv_ref[1, mine, lanes], queries, NT) * scaling
            soft_ref[head] = jnp.where(keep_keys, jnp.exp(scores - lse_ref[head : head + 1, :]), 0.0)


def backward_kernel(
    group, info_ref, gs_ref, gs2_ref, first_ref, normed_ref, inverse_ref, ct_ref, gain_ref, ow_ref, qkv_ref,
    soft_ref, w_ref,
    *refs,
):
    *earlier, dqkv_ref, gattn_ref, gh_ref, sums_ref, gf_ref, gmix = refs
    scaling = HEAD_DIM ** (-0.5)
    rows = PADDED[group]
    mine = of_group(group)
    live = live_of(info_ref, group)
    sent = sent_of(group)
    grad_second = filled(gs_ref[sent, :] + gs2_ref[sent, :], rows)
    normed, inverse = normed_ref[...], inverse_ref[...]
    grad_hidden = ct_ref[mine, :].astype(F32) + norm_back(grad_second, normed, inverse, row(gain_ref))
    gh_ref[...] = grad_hidden
    sums_ref[0:1, :] = col_sum(grad_second * normed)
    sums_ref[1:2, :] = col_sum(grad_second)
    gattn = (live * grad_hidden).astype(BF16)
    gattn_ref[...] = gattn
    sums_ref[2:3, :] = col_sum(gattn.astype(F32))
    gmix[...] = mm(gattn, ow_ref[...], NT).astype(BF16)
    low = low_lanes(rows)
    for pair in range(qkv_ref.shape[2] // PAIR):
        lanes = slice(pair * PAIR, (pair + 1) * PAIR)
        queries, keys, values = (qkv_ref[c, mine, lanes] for c in range(3))
        grads = gmix[:, lanes]
        keys_t = keys.T
        zero = jnp.zeros_like(queries)
        dq_t, dk, dv = [], [], []
        for side in range(2):
            own = low if side == 0 else jnp.logical_not(low)
            head = 2 * pair + side
            soft = soft_ref[head]
            grad_soft = mm(values, jnp.where(own, grads, zero), NT)
            inner = jnp.sum(grad_soft * soft, axis=0, keepdims=True)
            grad_scores = (soft * (grad_soft - inner)).astype(BF16)
            dv.append(mm(soft.astype(BF16), grads))
            dk.append(mm(grad_scores, queries))
            dq_t.append(mm(keys_t[side * HEAD_DIM : (side + 1) * HEAD_DIM], grad_scores))
        dqkv_ref[0, :, lanes] = (jnp.concatenate(dq_t, axis=0).T * scaling).astype(BF16)
        dqkv_ref[1, :, lanes] = (jnp.where(low, dk[0], dk[1]) * scaling).astype(BF16)
        dqkv_ref[2, :, lanes] = jnp.where(low, dv[0], dv[1]).astype(BF16)
    part = mm(dqkv_ref[0], w_ref[0], NT) + mm(dqkv_ref[1], w_ref[1], NT) + mm(dqkv_ref[2], w_ref[2], NT)
    if earlier:
        gf_ref[sent_of(1 - group), :] = earlier[0][...]
        gf_ref[sent, :] = part[: SENT[group]]
    else:
        gf_ref[...] = part[: SENT[group]]
    first_normed = first_ref[mine, :]
    sums_ref[4:5, :] = col_sum(part * first_normed)
    sums_ref[5:6, :] = col_sum(part)
    half = qkv_ref.shape[2]
    sums_ref[3:4, :half] = col_sum(dqkv_ref[0].astype(F32))
    sums_ref[3:4, half:] = col_sum(dqkv_ref[2].astype(F32))


def mlp_part_kernel(info_ref, act0_ref, act1_ref, down_ref, out_ref):
    for group, act_ref in enumerate((act0_ref, act1_ref)):
        out_ref[sent_of(group), :] = mm(act_ref[...], down_ref[...])[: SENT[group]]


def small_end_kernel(small_ref, gain2, bias2, outb, qvb, upb, downb):
    total = small_ref[...]
    width = total.shape[1]
    for n, ref in enumerate((gain2, bias2, outb)):
        ref[...] = total[2 + n].reshape(width)
    qvb[0:1, :] = total[5:6, : width // 2]
    qvb[1:2, :] = total[5:6, width // 2 :]
    upb[:width] = total[6].reshape(width)
    upb[width:] = total[7].reshape(width)
    downb[...] = total[8].reshape(width)


def norm1_end_kernel(info_ref, small_ref, other_ref, gain1, bias1):
    for n, ref in enumerate((gain1, bias1)):
        ref[...] = (small_ref[n] + other_ref[n]).reshape(small_ref.shape[1])


def input_kernel(info_ref, first_ref, inverse_ref, gh0_ref, gh1_ref, gain_ref, gf_ref, gf2_ref, grad_ref):
    start = 0
    for group, gh_ref in enumerate((gh0_ref, gh1_ref)):
        length, sent = LENGTHS[group], sent_of(group)
        grad_first = gf_ref[sent, :] + gf2_ref[sent, :]
        mine = slice(STARTS[group], STARTS[group] + SENT[group])
        normed, inverse = first_ref[mine, :], inverse_ref[mine, :]
        value = gh_ref[: SENT[group], :] + norm_back(grad_first, normed, inverse, row(gain_ref))
        grad_ref[start : start + length, :] = value[:length]
        start += length


def output_kernel(info_ref, h0_ref, h1_ref, m_ref, m2_ref, bias_ref, out_ref, wide):
    start = 0
    for group, h_ref in enumerate((h0_ref, h1_ref)):
        length, mine = LENGTHS[group], sent_of(group)
        value = h_ref[: SENT[group], :] + live_of(info_ref, group) * (
            m_ref[mine, :] + m2_ref[mine, :] + row(bias_ref)
        )
        wide[start : start + length, :] = value[:length]
        start += length
    out_ref[...] = wide[...].astype(BF16)


def stage_kernel(bit, count, info_ref, keep_ref, *refs):
    pieces, (send_ref, rest_ref) = refs[:count], refs[count:]
    mine = info_ref[4 + bit]
    half = keep_ref.shape[0] // 2
    at = 0
    for piece in pieces:
        cols = slice(at, at + piece.shape[1])
        at += piece.shape[1]
        low = keep_ref[:half, cols] + piece[:half, :]
        high = keep_ref[half:, cols] + piece[half:, :]
        send_ref[:, cols] = jnp.where(mine == 0, high, low)
        rest_ref[:, cols] = jnp.where(mine == 0, low, high)


def stage_both_kernel(bit, info_ref, keep1_ref, keep2_ref, got1_ref, got2_ref, send_ref, rest_ref):
    cols = keep1_ref.shape[1]
    for n, (keep_ref, got_ref) in enumerate(((keep1_ref, got1_ref), (keep2_ref, got2_ref))):
        at = pl.ds(n * cols, cols)
        stage_kernel(bit, 1, info_ref, keep_ref, got_ref, send_ref.at[:, at], rest_ref.at[:, at])


def both_end_kernel(info_ref, keep_ref, got_ref, down_ref, up_ref):
    cols = down_ref.shape[1]
    down_ref[...] = keep_ref[:, :cols] + got_ref[:, :cols]
    up_ref[...] = keep_ref[:, cols:] + got_ref[:, cols:]


def stage_small_kernel(bit, info_ref, keep_ref, small_ref, piece_ref, send_ref, rest_ref, total_ref):
    rows = keep_ref.shape[0]
    mine, half = info_ref[4 + bit], rows // 2
    total = small_ref[...] + piece_ref[rows:, :]
    total_ref[...] = total
    low = keep_ref[:half, :] + piece_ref[:half, :]
    high = keep_ref[half:, :] + piece_ref[half:rows, :]
    send_ref[:half, :] = jnp.where(mine == 0, high, low)
    send_ref[half:, :] = total
    rest_ref[...] = jnp.where(mine == 0, low, high)


def attn_done_kernel(info_ref, keep_ref, small_ref, piece_ref, out_ref, total_ref):
    rows = keep_ref.shape[0]
    out_ref[...] = keep_ref[...] + piece_ref[:rows, :]
    total_ref[...] = small_ref[...] + piece_ref[rows:, :]


def attn_last_kernel(info_ref, done1_ref, keep2_ref, got2_ref, small_ref, qkv_ref, out_ref, *rest):
    span = out_ref.shape[1]
    qkv_ref[0] = done1_ref[:, :span]
    qkv_ref[1] = done1_ref[:, span:]
    qkv_ref[2] = keep2_ref[:, :span] + got2_ref[:, :span]
    out_ref[...] = keep2_ref[:, span:] + got2_ref[:, span:]
    small_end_kernel(small_ref, *rest)


SMEM_SPEC = pl.BlockSpec(memory_space=pltpu.SMEM)
VMEM_SPEC = pl.BlockSpec(memory_space=pltpu.VMEM)
LATER = pl.BlockSpec(memory_space=pl.ANY)


def held(*shape, dtype=F32):
    return pltpu.VMEM(shape, dtype)


def shaped(*shape, dtype=F32):
    return pltpu.HBM(shape, dtype)


def in_vmem(value):
    return pltpu.with_memory_space_constraint(value, pltpu.VMEM)


def in_hbm(value):
    return pltpu.with_memory_space_constraint(value, pltpu.HBM)


class Order:
    def __init__(self, info):
        self.info = info
        self.last = None

    def call(self, kernel, name, outs, operands, room=3, plain=False, **kwargs):
        many = isinstance(outs, (tuple, list))
        outs = tuple(outs) if many else (outs,)
        count = len(operands) + 1
        extra = [] if self.last is None else [self.last]

        def body(*refs):
            kernel(*refs[:count], *refs[count + len(extra) :])

        results = pl.pallas_call(
            body,
            out_shape=outs,
            name=name,
            in_specs=[SMEM_SPEC] + [pl.BlockSpec() if plain else VMEM_SPEC] * (count - 1) + [LATER] * len(extra),
            out_specs=tuple(VMEM_SPEC if o.memory_space == pltpu.VMEM else pl.BlockSpec() for o in outs),
            compiler_params=pltpu.CompilerParams(vmem_limit_bytes=room * MIB),
            cost_estimate=pl.CostEstimate(flops=COST.get(name, 1), bytes_accessed=1, transcendentals=0),
            **kwargs,
        )(self.info, *map(in_hbm if plain else in_vmem, operands), *extra)
        self.last = results[0]
        return results if many else results[0]


def swap_sides(value):
    return lax.ppermute(value, "tensor", [(0, 1), (1, 0)])


def swap_bit(value, size, bit):
    return lax.ppermute(value, "dp", [(i, i ^ (1 << bit)) for i in range(size)])


class Scatter:
    def __init__(self, order, size, bits, keep, send, small=None):
        self.small = small
        self.order, self.size, self.bits, self.keep, self.level = order, size, bits, keep, 0
        self.got = [swap_bit(piece, size, 0) for piece in send]

    def stage(self, name):
        bit = self.bits[self.level]
        self.level += 1
        half = (self.keep.shape[0] // 2, self.keep.shape[1])
        if self.small is not None:
            send, self.keep, self.small = self.order.call(
                functools.partial(stage_small_kernel, bit), f"{name}_{self.level}",
                (held(half[0] + 16, half[1]), held(*half), held(16, half[1])), [self.keep, self.small, *self.got],
            )
            self.got = [swap_bit(send, self.size, bit)]
            return
        send, self.keep = self.order.call(
            functools.partial(stage_kernel, bit, len(self.got)), f"{name}_{self.level}",
            (held(*half), held(*half)), [self.keep, *self.got],
        )
        self.got = [swap_bit(send, self.size, bit)]


def per_device(
    dp_size,
    images_in,
    small_counts,
    large_counts,
    norm1_gain,
    norm1_bias,
    qkv_weight,
    qv_bias,
    out_weight,
    out_bias,
    norm2_gain,
    norm2_bias,
    up_weight,
    up_bias,
    down_weight,
    down_bias,
    out_cotangent,
):
    width = images_in.shape[1]
    span = out_weight.shape[0]
    units = down_weight.shape[0]
    index = lax.axis_index("dp")
    side = lax.axis_index("tensor")
    core = index & 1
    bits = dp_size.bit_length() - 1
    height = width // dp_size
    order = Order(
        jnp.stack(
            [side, core, small_counts[0], large_counts[0]] + [(index >> b) & 1 for b in range(bits)]
        ).astype(jnp.int32)
    )

    quarter = span // 4
    near = (index >> 1) & 1
    ow_send = lax.dynamic_slice_in_dim(out_weight, (2 * core + near) * quarter, quarter, 0).astype(F32)
    ow_one = swap_sides(ow_send)

    weights = qkv_weight.transpose(1, 0, 2)
    heads = span // HEAD_DIM
    first, qkv, x_pad, ct_pad, *rest = order.call(
        forward_kernel, "attn_forward",
        (
            held(ROWS, width, dtype=BF16), held(3, ROWS, span, dtype=BF16), held(ROWS, width, dtype=BF16),
            held(ROWS, width, dtype=BF16), *(held(heads, p) for p in PADDED), *(held(p, span) for p in SENT),
        ),
        [images_in, out_cotangent, norm1_gain, norm1_bias, weights, qv_bias], room=24, plain=True,
        scratch_shapes=[pltpu.VMEM((LENGTHS[0] + PADDED[1] + 3, width), F32)],
    )
    lse, mix = rest[:2], rest[2:]
    mix2 = [swap_sides(m) for m in mix]
    ow_one, *halves = order.call(
        relay_kernel, "out_weight_relay",
        (held(quarter, width), held(quarter, width // 2), held(quarter, width // 2)), [ow_one],
    )
    ow_two = [swap_bit(v, dp_size, 1) for v in halves]
    ow_got1 = swap_bit(ow_one, dp_size, 0)
    early = order.call(
        grad_act_kernel, "grad_act",
        tuple(
            spec
            for p in PADDED
            for spec in (held(p, width, dtype=BF16), held(p, units), held(1, width))
        ),
        [ct_pad, down_weight], room=8,
    )
    gmlp, gact, downsum = (early[i::3] for i in range(3))
    ow_two = order.call(next_kernel, "out_weight_next", (held(quarter, width // 2),) * 2, ow_two)
    ow_got2 = [swap_bit(v, dp_size, 0) for v in ow_two]
    ow_all = order.call(
        join_kernel, "out_weight_join", held(2 * span, width, dtype=BF16),
        [out_weight, ow_one, *ow_two, ow_got1, *ow_got2],
    )

    mlp, gs = [None, None], []
    for group in (1, 0):
        padded = PADDED[group]
        tall = SENT[group] + sum(g.shape[0] for g in gs)
        *mlp[group], total = order.call(
            functools.partial(mlp_kernel, group, 512), "mlp_" + "ab"[group],
            (
                held(padded, width), held(padded, width, dtype=BF16),
                held(padded, units, dtype=BF16), held(padded, units, dtype=BF16),
                held(1, units), held(tall, width),
            ),
            [
                x_pad, gact[group], mix[group], mix2[group], ow_all, out_bias, norm2_gain, norm2_bias,
                up_weight, up_bias, *gs,
            ],
            room=16, scratch_shapes=[pltpu.VMEM((padded, 2 * span), BF16)],
        )
        gs = [total]
    gs = gs[0]
    gs2 = swap_sides(gs)
    hidden, second, act, gpre, upsum = zip(*mlp)

    first_x = tuple(range(1, bits))
    first_z = (2, 1) + first_x[2:]

    def weight_grads(name, bit_order, left, right, piece):
        count = units // piece
        keep, *send = order.call(
            functools.partial(weights_kernel, height, piece, bit_order), name,
            (held(width // 2, units),) + (held(width // 2, piece),) * count, [*left, *right], room=12,
            scratch_shapes=[pltpu.VMEM((width, max(PADDED)), F32)],
        )
        return Scatter(order, dp_size, bit_order, keep, send)

    down_sum = weight_grads("down_weights", first_x, gmlp, act, units // 2)
    up_sum = weight_grads("up_weights", first_z, second, gpre, units // 2)
    down_sum.stage("down")
    up_sum.stage("up")
    mlp_part = order.call(mlp_part_kernel, "mlp_part", held(SENT_ROWS, width), [*act, down_weight], room=8)
    mlp2 = swap_sides(mlp_part)

    again = order.call(
        again_kernel, "attn_again",
        (
            *(held(heads, p, p) for p in PADDED), *(held(p, width) for p in PADDED), *(held(p, 1) for p in PADDED),
            held(ROWS, width), held(ROWS, 1),
        ),
        [qkv, *lse, *hidden, x_pad], room=8,
    )
    soft, normed, inverse, first_normed = again[:2], again[2:4], again[4:6], again[6]
    first_inverse = again[7]

    def go_back(group, *earlier):
        padded = PADDED[group]
        tall = SENT[group] + sum(e.shape[0] for e in earlier)
        return order.call(
            functools.partial(backward_kernel, group), "attn_backward_" + "ab"[group],
            (
                held(3, padded, span, dtype=BF16), held(padded, width, dtype=BF16),
                held(padded, width), held(8, width), held(tall, width),
            ),
            [
                gs, gs2, first_normed, normed[group], inverse[group], ct_pad, norm2_gain, out_weight, qkv, soft[group],
                weights, *earlier,
            ],
            scratch_shapes=[pltpu.VMEM((padded, span), BF16)], room=16,
        )

    *back1, gf = go_back(1)
    down_sum.stage("down")
    up_sum.stage("up")
    *back0, gf = go_back(0, gf)
    gf2 = swap_sides(gf)
    dqkv, gattn, gh, sums = zip(back0, back1)

    for n in range(3, bits - 1):
        down_sum.stage("down")
        up_sum.stage("up")
    rows = width // 2
    keep1, keep2, small, *send = order.call(
        functools.partial(attn_weights_kernel, height, first_x), "attn_weights",
        (
            held(rows, 2 * span), held(rows, 2 * span), held(16, width),
            held(rows + 16, 2 * span), held(rows, 2 * span),
        ),
        [first, *dqkv, *gattn, *mix, *sums, *upsum, *downsum], room=12,
        scratch_shapes=[pltpu.VMEM((width, max(PADDED)), F32)],
    )
    attn1 = Scatter(order, dp_size, first_x, keep1, send[:1], small)
    half = (down_sum.keep.shape[0] // 2, 2 * units)
    both, keep_both = order.call(
        functools.partial(stage_both_kernel, first_x[-1]), "mlp_3", (held(*half), held(*half)),
        [down_sum.keep, up_sum.keep, *down_sum.got, *up_sum.got],
    )
    got_both = swap_bit(both, dp_size, first_x[-1])
    attn1.stage("attn1")
    attn2 = Scatter(order, dp_size, first_x, keep2, send[1:])
    attn2.stage("attn2")
    block_out = order.call(
        output_kernel, "block_out", shaped(*images_in.shape, dtype=BF16),
        [*hidden, mlp_part, mlp2, down_bias], room=8, scratch_shapes=[pltpu.VMEM(images_in.shape, F32)],
    )
    for _ in range(1, bits - 1):
        attn1.stage("attn1")
        attn2.stage("attn2")
    down_block, up_block = order.call(
        both_end_kernel, "mlp_end", (shaped(height, units),) * 2, [keep_both, got_both]
    )
    input_grad = order.call(
        input_kernel, "input_back", shaped(*images_in.shape), [first_normed, first_inverse, *gh, norm1_gain, gf, gf2], room=8
    )
    done1, small = order.call(
        attn_done_kernel, "attn1_end", (held(height, width), held(16, width)),
        [attn1.keep, attn1.small, *attn1.got],
    )
    small2 = swap_sides(small)
    vector = shaped(width)
    qkv_block, out_block, *small_out = order.call(
        attn_last_kernel, "attn_end",
        (
            shaped(3, height, span), shaped(height, span),
            vector, vector, vector, shaped(2, span), shaped(units), vector,
        ),
        [done1, attn2.keep, *attn2.got, small],
    )
    norm1_out = order.call(norm1_end_kernel, "norm1_end", (vector, vector), [small, small2])

    return (
        block_out,
        input_grad,
        *norm1_out,
        qkv_block.transpose(1, 0, 2),
        small_out[3],
        out_block.T,
        small_out[2],
        small_out[0],
        small_out[1],
        up_block,
        small_out[4],
        down_block.T,
        small_out[5],
    )


def solution(mesh):
    placed = (
        P("dp", None),
        P("dp"),
        P("dp"),
        P(),
        P(),
        P(None, None, "tensor"),
        P(None, "tensor"),
        P("tensor", None),
        P(),
        P(),
        P(),
        P(None, "tensor"),
        P("tensor"),
        P("tensor", None),
        P(),
        P("dp", None),
    )
    return jax.shard_map(
        functools.partial(per_device, mesh.shape["dp"]),
        mesh=mesh,
        in_specs=placed,
        out_specs=(
            P("dp", None),
            P("dp", None),
            P(),
            P(),
            P("dp", None, "tensor"),
            P(None, "tensor"),
            P("tensor", "dp"),
            P(),
            P(),
            P(),
            P("dp", "tensor"),
            P("tensor"),
            P("tensor", "dp"),
            P(),
        ),
        check_vma=False,
    )
```
